128 devices in a mesh: tower: 2 (over y_lo), batch: 64 (over z, y_hi, x, core).
Axes of the slice: x: 4, y: 4 (y_hi: 2, y_lo: 2; y = y_hi * 2 + y_lo), z: 4, core: 2. Of those that a mesh axis runs over, the one named last changes fastest.
Arguments:
- states: bfloat16 [2, 16384, 1280], P('tower', 'batch'), may hold values from -6 to 6
- projection: bfloat16 [2, 1280, 1024], P('tower'), may hold values from -6 to 6
- prompt_ids: int32 [16384], P('batch'), may hold values from 0 to 8191
- log_temper: float32 [1], replicated, may hold values from 1.5 to 2.5
- logit_offset: float32 [1], replicated, may hold values from -6 to -2
Outputs:
- state_grad: bfloat16 [2, 16384, 1280], P('tower', 'batch')
- projection_grad: float32 [2, 1280, 1024], P('tower', 'batch')
The draws below stay inside these ranges and needn't reach their ends.
All inputs are finite; a program needn't handle non-finite values.
Results may differ from the reference program's by a relative error of at most 0.007.
Values may be sent and summed in bfloat16 or wider, within the bound.
A program may use at most 128 MiB of HBM per device.

```python
import math
import jax
import jax.numpy as jnp
from jax import lax

FEAT = 1280
EMB = 1024
PAIRS = 16384


def touch_ends(result, stream_key, least, largest):
    spot = [jax.random.randint(jax.random.fold_in(stream_key, axis), (), 0, length) for axis, length in enumerate(result.shape)]
    longest = result.shape.index(max(result.shape))
    beside = spot[:longest] + [(spot[longest] + 1) % result.shape[longest]] + spot[longest + 1:]
    return result.at[tuple(spot)].set(least).at[tuple(beside)].set(largest)


def shard_levels(stream_key, dims, split, smallest, high):
    gain = 1.0
    for dim, shards_of in split:
        steps = jax.random.uniform(jax.random.fold_in(jax.random.fold_in(stream_key, 6), dim), (shards_of,), jnp.float32, smallest / len(split), high / len(split))
        gain = gain * jnp.repeat(jnp.exp(steps), dims[dim] // shards_of).reshape((-1,) + (1,) * (len(dims) - 1 - dim))
    return gain


def normal_values(key, dims, scale, bound, shards=(), kind=jnp.bfloat16):
    result = scale * jax.random.normal(key, dims, jnp.float32)
    if shards:
        result = result * shard_levels(key, dims, shards, -0.22, 0.18)
    return jnp.clip(result, -bound, bound).astype(kind)


def setup_inputs(seed: int = 0) -> dict:
    arg_keys = jax.random.split(jax.random.key(seed), 6)
    return {
        "states": normal_values(arg_keys[0], (2, PAIRS, FEAT), 1.0, 6.0, ((0, 2), (1, 64))),
        "projection": normal_values(arg_keys[1], (2, FEAT, EMB), 1.0, 6.0, ((0, 2),)),
        "prompt_ids": touch_ends(jax.random.randint(arg_keys[2], (PAIRS,), 0, PAIRS // 2), jax.random.fold_in(arg_keys[2], 1), 0, (PAIRS // 2) - 1).astype(jnp.int32),
        "log_temper": jnp.clip(jax.random.uniform(arg_keys[3], (1,), jnp.float32, 1.5, 2.5), 1.5, 2.5),
        "logit_offset": jnp.clip(jax.random.uniform(arg_keys[4], (1,), jnp.float32, -6.0, -2.0), -6.0, -2.0),
    }


LOSS_SCALE = 16.0
EPSILON = 1e-06

def forward(inputs, matrix):
    raw_proj = jnp.dot(inputs, matrix, preferred_element_type=jnp.float32)
    length_row = jnp.sqrt(lax.optimization_barrier(jnp.sum(raw_proj * raw_proj, axis=1, keepdims=True)) + EPSILON)
    unit_rows = raw_proj / length_row
    return (length_row, unit_rows, unit_rows.astype(jnp.bfloat16))

def backward(inputs, matrix, length_row, unit_rows, emb_grad):
    along_unit = lax.optimization_barrier(jnp.sum(unit_rows * emb_grad, axis=1, keepdims=True))
    raw_grad = ((emb_grad - unit_rows * along_unit) / length_row).astype(jnp.bfloat16)
    state_grad = lax.dot_general(raw_grad, matrix, (((1,), (1,)), ((), ())), preferred_element_type=jnp.float32).astype(jnp.bfloat16)
    matrix_grad = lax.dot_general(inputs, raw_grad, (((0,), (0,)), ((), ())), preferred_element_type=jnp.float32)
    return (state_grad, matrix_grad)

def reference(states, projection, prompt_ids, log_temper, logit_offset):
    temper = jnp.exp(log_temper[0])
    offset = logit_offset[0]
    audio_len, audio_unit, audio_emb = forward(states[0], projection[0])
    text_len, text_unit, text_emb = forward(states[1], projection[1])
    pair_count = states.shape[1]
    block_len = math.gcd(pair_count, 1024)
    block_count = pair_count // block_len

    def advance(text_sum, block_index):
        first_row = block_index * block_len
        rows_audio = lax.dynamic_slice_in_dim(audio_emb, first_row, block_len, 0)
        rows_ids = lax.dynamic_slice_in_dim(prompt_ids, first_row, block_len, 0)
        logits = temper * lax.dot_general(rows_audio, text_emb, (((1,), (1,)), ((), ())), preferred_element_type=jnp.float32) + offset
        sign_vals = jnp.where(rows_ids[:, None] == prompt_ids[None, :], 1.0, -1.0).astype(jnp.float32)
        pair_grad = (-LOSS_SCALE * sign_vals * jax.nn.sigmoid(-sign_vals * logits)).astype(jnp.bfloat16)
        audio_part = jnp.dot(pair_grad, text_emb, preferred_element_type=jnp.float32)
        text_sum = text_sum + lax.dot_general(pair_grad, rows_audio, (((0,), (0,)), ((), ())), preferred_element_type=jnp.float32)
        return (text_sum, audio_part)
    text_sum, audio_parts = lax.scan(advance, jnp.zeros((pair_count, audio_emb.shape[1]), jnp.float32), jnp.arange(block_count, dtype=jnp.int32))
    audio_sum = audio_parts.reshape(pair_count, audio_emb.shape[1])
    audio_sgrad, audio_wgrad = backward(states[0], projection[0], audio_len, audio_unit, temper * audio_sum)
    text_sgrad, text_wgrad = backward(states[1], projection[1], text_len, text_unit, temper * text_sum)
    return (jnp.stack([audio_sgrad, text_sgrad]), jnp.stack([audio_wgrad, text_wgrad]))
```

```python
import jax
import jax.numpy as jnp
from jax import lax
from jax.experimental import pallas as pl
from jax.experimental.pallas import tpu as pltpu
from jax.sharding import PartitionSpec as P

EPSILON = 1e-06
MESH = pl.DeviceIdType.MESH
F32, BF16 = jnp.float32, jnp.bfloat16
NT = (((1,), (1,)), ((), ()))
TN = (((0,), (0,)), ((), ()))
NN = (((1,), (0,)), ((), ()))

ROWS = 256
EMB = 1024
FEAT = 1280
CHUNK = 64
QS = ROWS // CHUNK
HALF = EMB // 2
FEAT_Z = FEAT // 4
OWN_ROWS = 40


class Sems:
    sizes = dict(
        y=QS, y_id=1, ring=2 * 12, ring_id=2 * 3, core=4, core_id=4, core_s=1,
        part=4, far=2 * QS, to_next=2 * QS, to_prev=2 * QS, y_back=QS,
        rg=QS, st_p=4, st_q=4, mid=2, end_p=4, end_q=4, last=1,
    )

    @classmethod
    def at(cls, name, index=0):
        base = 0
        for key, size in cls.sizes.items():
            if key == name:
                return base + index
            base += size
        raise KeyError(name)

    @classmethod
    def total(cls):
        return sum(cls.sizes.values())


def dot(a, b, dims):
    return lax.dot_general(a, b, dims, preferred_element_type=F32)


def kernel(
    s_ref, w_ref, id_ref, lt_ref, of_ref, sg_ref, pg_ref,
    blocks, ids, raw, inv, pair, grad, out_buf, far_in, near_in, part_out, part_in, y_out, y_in,
    rg, rg_mine, rg_theirs, s_other, s_t, mat, p_out, q_out, p_in, q_in, p_sum, q_sum, mid_out, mid_in,
    p_two, q_two, p_end, q_end, last_out, last_in, ssem, rsem,
):
    tower = lax.axis_index("tower")
    batch = lax.axis_index("batch")
    core = lax.rem(batch, 2)
    px = lax.rem(batch // 2, 4)
    yh = lax.rem(batch // 8, 2)
    pz = batch // 16
    other = 1 - tower

    def dev(t, z, y, x, c):
        return (t, ((z * 2 + y) * 4 + x) * 2 + c)

    def ring_x(d):
        return dev(tower, pz, yh, lax.rem(px + d, 4), core)

    def ring_z(d):
        return dev(tower, lax.rem(pz + d, 4), yh, px, core)

    def ring_of(r, d):
        return dev(tower, lax.rem(pz + r * d, 4), yh, lax.rem(px + (1 - r) * d, 4), core)

    partner = dev(tower, pz, yh, px, 1 - core)
    y_up = dev(other, pz, jnp.where(tower == 1, 1 - yh, yh), px, core)
    y_down = dev(other, pz, jnp.where(tower == 0, 1 - yh, yh), px, core)
    y_two = dev(tower, pz, 1 - yh, px, core)

    def block(r, slot):
        return slot + r * (4 + slot)

    def copy(name, index, src, dst, where):
        k = Sems.at(name) + index
        return pltpu.make_async_remote_copy(
            src_ref=src, dst_ref=dst, send_sem=ssem.at[k], recv_sem=rsem.at[k],
            device_id=where, device_id_type=MESH,
        )

    def arrived(name, index, ref):
        copy(name, index, ref, ref, partner).wait_recv()

    def left(name, index, ref):
        copy(name, index, ref, ref, partner).wait_send()

    def rows(q):
        return pl.ds(CHUNK * q, CHUNK)

    barrier = pltpu.get_barrier_semaphore()
    near = [partner, y_up, y_down, y_two] + [ring_x(d) for d in (1, 2, 3)] + [ring_z(d) for d in (1, 2, 3)]
    for where in near:
        pl.semaphore_signal(barrier, inc=1, device_id=where, device_id_type=MESH)

    @pl.loop(0, 2)
    def _(n):
        cols = pl.ds(pl.multiple_of(n * HALF, HALF), HALF)
        raw[:, cols] = dot(s_ref[...], w_ref[:, cols], NN)

    pl.semaphore_wait(barrier, len(near))

    own0 = block(tower, 0)
    oth0 = block(other, 0)

    def to_next(k, r, q):
        return copy("ring", 12 * k + q, blocks.at[block(r, 0), rows(q)], blocks.at[block(r, 1), rows(q)], ring_of(r, 1))

    def to_prev(k, r, q):
        return copy("ring", 12 * k + 4 + q, blocks.at[block(r, 0), rows(q)], blocks.at[block(r, 3), rows(q)], ring_of(r, 3))

    def onward(k, r, q):
        slot, d = (1, 1) if q < 2 else (3, 3)
        return copy("ring", 12 * k + 8 + q, blocks.at[block(r, slot), rows(q)], blocks.at[block(r, 2), rows(q)], ring_of(r, d))

    def got_next(k, r, q):
        arrived("ring", 12 * k + q, blocks.at[block(r, 1), rows(q)])

    def got_prev(k, r, q):
        arrived("ring", 12 * k + 4 + q, blocks.at[block(r, 3), rows(q)])

    def got_onward(k, r, q):
        arrived("ring", 12 * k + 8 + q, blocks.at[block(r, 2), rows(q)])

    def ids_out(k, r):
        copy("ring_id", 3 * k, ids.at[block(r, 0)], ids.at[block(r, 1)], ring_of(r, 1)).start()
        copy("ring_id", 3 * k + 1, ids.at[block(r, 0)], ids.at[block(r, 3)], ring_of(r, 3)).start()

    def ids_onward(k, r):
        arrived("ring_id", 3 * k, ids.at[block(r, 1)])
        copy("ring_id", 3 * k + 2, ids.at[block(r, 1)], ids.at[block(r, 2)], ring_of(r, 1)).start()
        arrived("ring_id", 3 * k + 1, ids.at[block(r, 3)])

    def core_send(slot):
        copy("core", slot, blocks.at[4 + 2 * slot], blocks.at[5 + 2 * slot], partner).start()
        copy("core_id", slot, ids.at[4 + 2 * slot], ids.at[5 + 2 * slot], partner).start()

    def core_got(slot):
        arrived("core", slot, blocks.at[5 + 2 * slot])
        arrived("core_id", slot, ids.at[5 + 2 * slot])

    ids[own0] = jnp.broadcast_to(id_ref[...], (8, ROWS))
    copy("y_id", 0, ids.at[own0], ids.at[own0], y_up).start()
    for q in range(QS):
        part = raw[rows(q), :]
        length = jnp.sqrt(jnp.sum(part * part, axis=1, keepdims=True) + EPSILON)
        scale = 1.0 / length
        inv[rows(q), :] = jnp.broadcast_to(scale, (CHUNK, 128))
        blocks[own0, rows(q)] = (part * scale).astype(BF16)
        copy("y", q, blocks.at[own0, rows(q)], blocks.at[own0, rows(q)], y_up).start()
        to_next(0, tower, q).start()
        if q >= 2:
            to_prev(0, tower, q).start()
    for q in range(2):
        to_prev(0, tower, q).start()
    ids_out(0, tower)

    @pl.when(tower == 1)
    def _():
        core_send(0)

    copy("core_s", 0, s_ref, s_other, partner).start()
    s_t[:, :ROWS] = s_ref[...].T

    def y_got(q):
        arrived("y", q, blocks.at[oth0, rows(q)])
        to_next(1, other, q).start()
        to_prev(1, other, q).start()

    y_got(0)
    got_next(0, tower, 0)
    onward(0, tower, 0).start()
    got_prev(0, tower, 2)
    onward(0, tower, 2).start()
    y_got(1)
    got_next(0, tower, 1)
    onward(0, tower, 1).start()
    got_prev(0, tower, 3)
    onward(0, tower, 3).start()
    ids_onward(0, tower)
    arrived("y_id", 0, ids.at[oth0])
    ids_out(1, other)
    y_got(2)
    y_got(3)

    @pl.when(tower == 0)
    def _():
        core_send(0)

    for q in range(2):
        got_next(1, other, q)
        onward(1, other, q).start()
    for q in range(2):
        got_next(0, tower, 2 + q)
        got_prev(0, tower, q)
    ids_onward(1, other)

    @pl.when(tower == 1)
    def _():
        core_send(1)
        core_send(3)
        core_got(0)
        core_got(1)
        core_got(3)

    @pl.when(tower == 0)
    def _():
        core_got(0)

    temper = jnp.exp(lt_ref[...])
    slope = 0.5 * temper
    shift = 0.5 * of_ref[...]

    def unit(a, b):
        i = jnp.where(tower == 0, a, b)
        j = jnp.where(tower == 0, b, a)
        at = pl.multiple_of(4 + 2 * j, 2)
        text = blocks[pl.ds(at, 2)].reshape(2 * ROWS, EMB)
        logit = dot(blocks[i], text, NT)
        value = jnp.tanh(logit * slope + shift) * 8.0
        row = jnp.concatenate([ids[at, 0:1, :], ids[at + 1, 0:1, :]], axis=1).astype(F32)
        col = jnp.broadcast_to(ids[i, 0:1, :].astype(F32), (128, ROWS)).T
        same = jnp.concatenate([col] * 4, axis=1) == row
        value = value + jnp.where(same, -8.0, 8.0)
        here = pl.ds(pl.multiple_of(i * ROWS, ROWS), ROWS)
        pair[here, pl.ds(pl.multiple_of(j * 2 * ROWS, 2 * ROWS), 2 * ROWS)] = value.astype(BF16)

    @pl.loop(0, 3)
    def _(u):
        unit(u + u // 2, 0)

    for q in (2, 3):
        got_prev(1, other, q)
        onward(1, other, q).start()
    for q in (0, 1):
        got_prev(1, other, q)
        got_next(1, other, q + 2)

    @pl.when(tower == 0)
    def _():
        core_send(1)
        core_send(3)

    for q in range(QS):
        got_onward(0, tower, q)
    arrived("ring_id", 2, ids.at[block(tower, 2)])

    @pl.when(tower == 1)
    def _():
        core_send(2)

    @pl.when(tower == 0)
    def _():
        core_got(1)
        core_got(3)

    @pl.loop(0, 6)
    def _(u):
        a = u // 2
        unit(a + a // 2, 1 + 2 * lax.rem(u, 2))

    @pl.when(tower == 1)
    def _():
        core_got(2)

    @pl.loop(0, 3)
    def _(u):
        unit(2, u + u // 2)

    arrived("core_s", 0, s_other)
    s_t[:, ROWS:] = s_other[...].T

    for q in range(QS):
        got_onward(1, other, q)
    arrived("ring_id", 5, ids.at[block(other, 2)])

    @pl.when(tower == 0)
    def _():
        core_send(2)
        core_got(2)

    @pl.loop(0, 4)
    def _(u):
        unit(u, 2)

    def text_terms(half, slot):
        audio = blocks[pl.ds(0, 4)].reshape(4 * ROWS, EMB)
        return dot(pair[:, pl.ds((2 * slot + half) * ROWS, ROWS)], audio, TN)

    def audio_terms(slot):
        @pl.loop(0, 2)
        def _(n):
            cols = pl.ds(pl.multiple_of(n * HALF, HALF), HALF)
            text = blocks[pl.ds(4, 8), :, cols].reshape(8 * ROWS, HALF)
            grad[0, slot, :, cols] = dot(pair[pl.ds(slot * ROWS, ROWS), :], text, NN)

    def give(slot):
        part_out[slot] = text_terms(1, slot).astype(BF16)
        copy("part", slot, part_out.at[slot], part_in.at[slot], partner).start()

    def keep(slot):
        grad[1, slot] = text_terms(0, slot)
        arrived("part", slot, part_in.at[slot])
        grad[1, slot] += part_in[slot].astype(F32)

    def far_copy(r, q):
        return copy("far", QS * r + q, out_buf.at[r, 2, rows(q)], far_in.at[r, rows(q)], ring_of(r, 1 if q < 2 else 3))

    def next_copy(r, q):
        return copy("to_next", QS * r + q, out_buf.at[r, 3, rows(q)], near_in.at[r, 0, rows(q)], ring_of(r, 1))

    def prev_copy(r, q):
        return copy("to_prev", QS * r + q, out_buf.at[r, 1, rows(q)], near_in.at[r, 1, rows(q)], ring_of(r, 3))

    def send_far(r):
        out_buf[r, 2] = grad[r, 2].astype(BF16)
        for q in (0, 2, 1, 3):
            far_copy(r, q).start()

    def send_next(r):
        for q in range(QS):
            term = grad[r, 3, rows(q), :]
            if q < 2:
                arrived("far", QS * r + q, far_in.at[r, rows(q)])
                term += far_in[r, rows(q), :].astype(F32)
            out_buf[r, 3, rows(q), :] = term.astype(BF16)
            next_copy(r, q).start()

    def send_prev(r):
        for q in range(QS):
            term = grad[r, 1, rows(q), :]
            if q >= 2:
                arrived("far", QS * r + q, far_in.at[r, rows(q)])
                term += far_in[r, rows(q), :].astype(F32)
            out_buf[r, 1, rows(q), :] = term.astype(BF16)
            prev_copy(r, q).start()

    give(2)
    audio_terms(2)
    send_far(0)
    keep(2)
    send_far(1)
    give(3)
    give(1)
    audio_terms(3)
    send_next(0)
    audio_terms(1)
    send_prev(0)
    keep(3)
    send_next(1)
    keep(1)
    send_prev(1)
    give(0)
    audio_terms(0)
    keep(0)

    def reduced(r, q):
        arrived("to_next", QS * r + q, near_in.at[r, 0, rows(q)])
        arrived("to_prev", QS * r + q, near_in.at[r, 1, rows(q)])
        return (
            grad[r, 0, rows(q), :]
            + near_in[r, 0, rows(q), :].astype(F32)
            + near_in[r, 1, rows(q), :].astype(F32)
        )

    def back_copy(q):
        return copy("y_back", q, y_out.at[rows(q)], y_in.at[rows(q)], y_down)

    for q in range(QS):
        y_out[rows(q), :] = reduced(other, q).astype(BF16)
        back_copy(q).start()

    def rg_copy(q):
        return copy("rg", q, rg_theirs.at[rows(q)], rg_mine.at[pl.ds(ROWS + CHUNK * q, CHUNK)], partner)

    for q in range(QS):
        total = reduced(tower, q)
        arrived("y_back", q, y_in.at[rows(q)])
        emb_grad = temper * (total + y_in[rows(q), :].astype(F32))
        scale = inv[rows(q), 0:1]
        unit_rows = raw[rows(q), :] * scale
        along = jnp.sum(unit_rows * emb_grad, axis=1, keepdims=True)
        value = ((emb_grad - unit_rows * along) * scale).astype(BF16)
        rg[rows(q), :] = value
        low, high = value[:, :HALF], value[:, HALF:]
        rg_mine[rows(q), :] = jnp.where(core == 0, low, high)
        rg_theirs[rows(q), :] = jnp.where(core == 0, high, low)
        rg_copy(q).start()

    for q in range(QS):
        arrived("rg", q, rg_mine.at[pl.ds(ROWS + CHUNK * q, CHUNK)])

    @pl.loop(0, FEAT // 256)
    def _(n):
        here = pl.ds(pl.multiple_of(n * 256, 256), 256)
        mat[here, :] = dot(s_t[here, :], rg_mine[...], NN)

    def z_rows(d):
        at = pl.ds(pl.multiple_of(lax.rem(pz + d, 4) * FEAT_Z, FEAT_Z), FEAT_Z)
        return mat[at, :256]

    def x_rows(d):
        pieces = []
        for k in range(8):
            at = pl.multiple_of(k * 4 * OWN_ROWS + lax.rem(px + d, 4) * OWN_ROWS, 8)
            pieces.append(mat[pl.ds(at, OWN_ROWS), 256:])
        return jnp.concatenate(pieces, axis=0)

    def p_copy(d):
        return copy("st_p", d, p_out.at[d], p_in.at[d], ring_z(d))

    def q_copy(d):
        return copy("st_q", d, q_out.at[d], q_in.at[d], ring_x(d))

    for d in (2, 1, 3):
        p_out[d] = z_rows(d).astype(BF16)
        p_copy(d).start()
        q_out[d] = x_rows(d).astype(BF16)
        q_copy(d).start()

    @pl.loop(0, FEAT // 256)
    def _(n):
        here = pl.ds(pl.multiple_of(n * 256, 256), 256)
        sg_ref[:, here] = dot(rg[...], w_ref[here, :], NT).astype(BF16)

    p_one = z_rows(0)
    for d in (1, 3, 2):
        arrived("st_p", d, p_in.at[d])
        p_one += p_in[d].astype(F32)
    p_sum[...] = p_one
    at = pl.multiple_of((1 - yh) * 4 * OWN_ROWS, 8)
    mid_out[0] = p_sum[pl.ds(at, 4 * OWN_ROWS), :].astype(BF16)
    copy("mid", 0, mid_out.at[0], mid_in.at[0], y_two).start()

    def q_rows(y):
        pieces = []
        for k in range(4):
            at = pl.multiple_of(k * 2 * OWN_ROWS + y * OWN_ROWS, 8)
            pieces.append(q_sum[pl.ds(at, OWN_ROWS), :])
        return jnp.concatenate(pieces, axis=0)

    q_one = x_rows(0)
    for d in (1, 3, 2):
        arrived("st_q", d, q_in.at[d])
        q_one += q_in[d].astype(F32)
    q_sum[...] = q_one
    mid_out[1] = q_rows(1 - yh).astype(BF16)
    copy("mid", 1, mid_out.at[1], mid_in.at[1], y_two).start()

    arrived("mid", 0, mid_in.at[0])
    at = pl.multiple_of(yh * 4 * OWN_ROWS, 8)
    p_two[...] = p_sum[pl.ds(at, 4 * OWN_ROWS), :] + mid_in[0].astype(F32)

    def end_rows(p, d):
        return pl.ds(pl.multiple_of(lax.rem(p + d, 4) * OWN_ROWS, 8), OWN_ROWS)

    def p_last(d):
        return copy("end_p", d, p_two.at[end_rows(px, d)], p_end.at[d], ring_x(d))

    def q_last(d):
        return copy("end_q", d, q_two.at[end_rows(pz, d)], q_end.at[d], ring_z(d))

    for d in (2, 1, 3):
        p_last(d).start()
    arrived("mid", 1, mid_in.at[1])
    q_two[...] = q_rows(yh) + mid_in[1].astype(F32)
    for d in (2, 1, 3):
        q_last(d).start()

    p_fin = p_two[end_rows(px, 0), :]
    q_fin = q_two[end_rows(pz, 0), :]
    for d in (1, 3, 2):
        arrived("end_p", d, p_end.at[d])
        p_fin += p_end[d]
    for d in (1, 3, 2):
        arrived("end_q", d, q_end.at[d])
        q_fin += q_end[d]
    both = jnp.concatenate([p_fin, q_fin], axis=1)
    first, second = both[:20], both[20:]
    theirs = jnp.where(core == 0, second, first)
    mine = jnp.where(core == 0, first, second)
    last_out[...] = jnp.concatenate([theirs, jnp.zeros((4, HALF), F32)], axis=0)
    copy("last", 0, last_out, last_in, partner).start()
    arrived("last", 0, last_in)
    got = last_in[:20, :]
    pg_ref[:, :HALF] = jnp.where(core == 0, mine, got)
    pg_ref[:, HALF:] = jnp.where(core == 0, got, mine)

    some = blocks.at[0]
    for q in range(QS):
        left("y", q, some.at[rows(q)])
        left("y_back", q, some.at[rows(q)])
        left("rg", q, rg_theirs.at[rows(q)])
    left("y_id", 0, ids.at[0])
    for k in range(24):
        left("ring", k, some.at[rows(0)])
    for k in range(6):
        left("ring_id", k, ids.at[0])
    for k in range(4):
        left("core", k, some)
        left("core_id", k, ids.at[0])
        left("part", k, some)
    left("core_s", 0, s_other)
    for k in range(2 * QS):
        left("far", k, some.at[rows(0)])
        left("to_next", k, some.at[rows(0)])
        left("to_prev", k, some.at[rows(0)])
    for d in (1, 2, 3):
        left("st_p", d, p_out.at[d])
        left("st_q", d, q_out.at[d])
        left("end_p", d, p_end.at[d])
        left("end_q", d, q_end.at[d])
    for k in range(2):
        left("mid", k, mid_out.at[k])
    left("last", 0, last_out)


def local(states, projection, prompt_ids, log_temper, logit_offset):
    vmem = pl.BlockSpec(memory_space=pltpu.VMEM)
    scratch = [
        ((12, ROWS, EMB), BF16),
        ((12, 8, ROWS), jnp.int32),
        ((ROWS, EMB), F32),
        ((ROWS, 128), F32),
        ((4 * ROWS, 8 * ROWS), BF16),
        ((2, 4, ROWS, EMB), F32),
        ((2, 4, ROWS, EMB), BF16),
        ((2, ROWS, EMB), BF16),
        ((2, 2, ROWS, EMB), BF16),
        ((4, ROWS, EMB), BF16),
        ((4, ROWS, EMB), BF16),
        ((ROWS, EMB), BF16),
        ((ROWS, EMB), BF16),
        ((ROWS, EMB), BF16),
        ((2 * ROWS, HALF), BF16),
        ((ROWS, HALF), BF16),
        ((ROWS, FEAT), BF16),
        ((FEAT, 2 * ROWS), BF16),
        ((FEAT, HALF), F32),
        ((4, FEAT_Z, 256), BF16),
        ((4, FEAT_Z, 256), BF16),
        ((4, FEAT_Z, 256), BF16),
        ((4, FEAT_Z, 256), BF16),
        ((FEAT_Z, 256), F32),
        ((FEAT_Z, 256), F32),
        ((2, FEAT_Z // 2, 256), BF16),
        ((2, FEAT_Z // 2, 256), BF16),
        ((FEAT_Z // 2, 256), F32),
        ((FEAT_Z // 2, 256), F32),
        ((4, OWN_ROWS, 256), F32),
        ((4, OWN_ROWS, 256), F32),
        ((24, HALF), F32),
        ((24, HALF), F32),
    ]
    state_grad, owned = pl.pallas_call(
        kernel,
        out_shape=(
            jax.ShapeDtypeStruct((ROWS, FEAT), BF16),
            jax.ShapeDtypeStruct((20, EMB), F32),
        ),
        in_specs=[vmem] * 5,
        out_specs=(vmem, vmem),
        scratch_shapes=[pltpu.VMEM(shape, kind) for shape, kind in scratch]
        + [pltpu.SemaphoreType.DMA((Sems.total(),)), pltpu.SemaphoreType.DMA((Sems.total(),))],
        compiler_params=pltpu.CompilerParams(
            collective_id=0, has_side_effects=True, vmem_limit_bytes=60 * 2**20
        ),
        name="contrast",
    )(
        states[0],
        projection[0],
        prompt_ids.reshape(1, ROWS),
        log_temper.reshape(1, 1),
        logit_offset.reshape(1, 1),
    )
    return state_grad[None], owned[None]


def solution(mesh):
    return jax.shard_map(
        local,
        mesh=mesh,
        in_specs=(P("tower", "batch", None), P("tower", None, None), P("batch"), P(), P()),
        out_specs=(P("tower", "batch", None), P("tower", "batch", None)),
        check_vma=False,
    )
```

```python
import jax
import jax.numpy as jnp
from jax import lax
from jax.experimental import pallas as pl
from jax.experimental.pallas import tpu as pltpu
from jax.sharding import PartitionSpec as P

EPSILON = 1e-06
MESH = pl.DeviceIdType.MESH
F32, BF16 = jnp.float32, jnp.bfloat16
NT = (((1,), (1,)), ((), ()))
TN = (((0,), (0,)), ((), ()))
NN = (((1,), (0,)), ((), ()))

ROWS = 256
EMB = 1024
FEAT = 1280
CHUNK = 32
QS = ROWS // CHUNK
HALF = EMB // 2
FEAT_Z = FEAT // 4
OWN_ROWS = 40
OTHER0 = 8

Y_ORDER = (0, 4, 1, 5, 2, 6, 3, 7)
NEXT_ORDER = (0, 1, 2, 3, 6, 7, 4, 5)
PREV_ORDER = (4, 5, 6, 7, 0, 1, 2, 3)
BACK_NEXT = (4, 5, 0, 1, 2, 3, 6, 7)
BACK_PREV = ((2, 3, 4, 5, 6, 7, 0, 1), (4, 5, 6, 7, 2, 3))
BACK_ORDER = (4, 5, 6, 0, 7, 1, 2, 3)


class Sems:
    sizes = dict(
        y=QS, y_id=1, ring=2 * 3 * QS, ring_id=2 * 3, core=4, core_id=4, core_s=1, extra=4,
        part=4, far=2 * QS, to_next=2 * QS, to_prev=2 * QS, y_extra=4, y_back=QS,
        rg=QS, st_p=4, st_q=4, mid=2, end_p=4, end_q=4, last=1,
    )

    @classmethod
    def at(cls, name, index=0):
        base = 0
        for key, size in cls.sizes.items():
            if key == name:
                return base + index
            base += size
        raise KeyError(name)

    @classmethod
    def total(cls):
        return sum(cls.sizes.values())


def dot(a, b, dims):
    return lax.dot_general(a, b, dims, preferred_element_type=F32)


def kernel(
    s_hbm, w_hbm, id_ref, lt_ref, of_ref, sg_ref, pg_ref,
    s_ref, w_ref, blocks, ids, raw, inv, pair, grad, out_buf, far_in, near_in, extra_out, extra_in, part_out, part_in, y_out, y_in,
    rg, rg_mine, rg_theirs, s_other, s_t, mat, p_out, q_out, p_in, q_in, p_sum, q_sum, mid_out, mid_in,
    p_two, q_two, p_end, q_end, last_out, last_in, lsem, ssem, rsem,
):
    tower = lax.axis_index("tower")
    batch = lax.axis_index("batch")
    core = lax.rem(batch, 2)
    px = lax.rem(batch // 2, 4)
    yh = lax.rem(batch // 8, 2)
    pz = batch // 16
    other = 1 - tower

    def dev(t, z, y, x, c):
        return (t, ((z * 2 + y) * 4 + x) * 2 + c)

    def ring_x(d):
        return dev(tower, pz, yh, lax.rem(px + d, 4), core)

    def ring_z(d):
        return dev(tower, lax.rem(pz + d, 4), yh, px, core)

    def ring(k, d):
        r = tower if k == 0 else other
        return dev(tower, lax.rem(pz + r * d, 4), yh, lax.rem(px + (1 - r) * d, 4), core)

    partner = dev(tower, pz, yh, px, 1 - core)
    y_up = dev(other, pz, jnp.where(tower == 1, 1 - yh, yh), px, core)
    y_down = dev(other, pz, jnp.where(tower == 0, 1 - yh, yh), px, core)
    y_two = dev(tower, pz, 1 - yh, px, core)

    def block(k, slot):
        return 2 * slot if k == 0 else OTHER0 + slot

    def copy(name, index, src, dst, where):
        n = Sems.at(name) + index
        return pltpu.make_async_remote_copy(
            src_ref=src, dst_ref=dst, send_sem=ssem.at[n], recv_sem=rsem.at[n],
            device_id=where, device_id_type=MESH,
        )

    def arrived(name, index, ref):
        copy(name, index, ref, ref, partner).wait_recv()

    def left(name, index, ref):
        copy(name, index, ref, ref, partner).wait_send()

    def rows(q):
        return pl.ds(CHUNK * q, CHUNK)

    def piece(k, slot, q):
        return blocks.at[block(k, slot), rows(q)]

    barrier = pltpu.get_barrier_semaphore()
    near = [partner, y_up, y_down, y_two] + [ring_x(d) for d in (1, 2, 3)] + [ring_z(d) for d in (1, 2, 3)]
    for where in near:
        pl.semaphore_signal(barrier, inc=1, device_id=where, device_id_type=MESH)

    def halves(n):
        return pl.ds(n * HALF, HALF)

    loads = [pltpu.make_async_copy(s_hbm, s_ref, lsem.at[0])]
    loads += [pltpu.make_async_copy(w_hbm.at[:, halves(n)], w_ref.at[:, halves(n)], lsem.at[1 + n]) for n in range(2)]
    for load in loads:
        load.start()
    ids[0] = jnp.broadcast_to(id_ref[...], (8, ROWS))
    loads[0].wait()
    for n in range(2):
        loads[1 + n].wait()
        raw[:, halves(n)] = dot(s_ref[...], w_ref[:, halves(n)], NN)

    pl.semaphore_wait(barrier, len(near))

    def to_next(k, q):
        return copy("ring", 3 * QS * k + q, piece(k, 0, q), piece(k, 1, q), ring(k, 1))

    def to_prev(k, q):
        return copy("ring", 3 * QS * k + QS + q, piece(k, 0, q), piece(k, 3, q), ring(k, 3))

    def onward(k, q):
        slot = 1 if q < QS // 2 else 3
        return copy("ring", 3 * QS * k + 2 * QS + q, piece(k, slot, q), piece(k, 2, q), ring(k, slot))

    def got_next(k, q):
        arrived("ring", 3 * QS * k + q, piece(k, 1, q))

    def got_prev(k, q):
        arrived("ring", 3 * QS * k + QS + q, piece(k, 3, q))

    def got_onward(k, q):
        arrived("ring", 3 * QS * k + 2 * QS + q, piece(k, 2, q))

    def extra(n):
        slot, q = ((1, 6), (1, 7), (3, 0), (3, 1))[n]
        return copy("extra", n, piece(0, slot, q), piece(1, slot, q), y_up)

    def got_extra(n):
        slot, q = ((1, 6), (1, 7), (3, 0), (3, 1))[n]
        arrived("extra", n, piece(1, slot, q))

    def ids_out(k):
        copy("ring_id", 3 * k, ids.at[block(k, 0)], ids.at[block(k, 1)], ring(k, 1)).start()
        copy("ring_id", 3 * k + 1, ids.at[block(k, 0)], ids.at[block(k, 3)], ring(k, 3)).start()

    def ids_onward(k):
        arrived("ring_id", 3 * k, ids.at[block(k, 1)])
        copy("ring_id", 3 * k + 2, ids.at[block(k, 1)], ids.at[block(k, 2)], ring(k, 1)).start()
        arrived("ring_id", 3 * k + 1, ids.at[block(k, 3)])

    def core_send(slot):
        copy("core", slot, blocks.at[2 * slot], blocks.at[2 * slot + 1], partner).start()
        copy("core_id", slot, ids.at[2 * slot], ids.at[2 * slot + 1], partner).start()

    def core_got(slot):
        arrived("core", slot, blocks.at[2 * slot + 1])
        arrived("core_id", slot, ids.at[2 * slot + 1])

    copy("y_id", 0, ids.at[0], ids.at[OTHER0], y_up).start()
    ids_out(0)
    for m, q in enumerate(Y_ORDER):
        part = raw[rows(q), :]
        length = jnp.sqrt(jnp.sum(part * part, axis=1, keepdims=True) + EPSILON)
        scale = 1.0 / length
        inv[rows(q), :] = jnp.broadcast_to(scale, (CHUNK, 128))
        blocks[0, rows(q)] = (part * scale).astype(BF16)
        copy("y", q, piece(0, 0, q), piece(1, 0, q), y_up).start()
        if m < 6:
            (to_next(0, q) if q < 4 else to_prev(0, q)).start()
    for q in (3, 6, 7, 4, 5):
        to_next(0, q).start()
    for q in (7, 0, 1, 2, 3):
        to_prev(0, q).start()
    core_send(0)
    copy("core_s", 0, s_ref, s_other, partner).start()
    s_t[:, :ROWS] = s_ref[...].T

    def step(m):
        q = Y_ORDER[m]
        arrived("y", q, piece(1, 0, q))
        if q < 6:
            to_next(1, q).start()
        if q >= 2:
            to_prev(1, q).start()
        q = NEXT_ORDER[m]
        got_next(0, q)
        if q < 4:
            onward(0, q).start()
        elif q >= 6:
            extra(q - 6).start()
        q = PREV_ORDER[m]
        got_prev(0, q)
        if q >= 4:
            onward(0, q).start()
        elif q < 2:
            extra(2 + q).start()

    def pass_next(q):
        got_next(1, q)
        onward(1, q).start()

    def pass_prev(q):
        got_prev(1, q)
        onward(1, q).start()

    step(0)
    step(1)
    ids_onward(0)
    arrived("y_id", 0, ids.at[OTHER0])
    ids_out(1)
    arrived("core_s", 0, s_other)
    s_t[:, ROWS:] = s_other[...].T
    step(2)
    step(3)
    pass_next(0)
    step(4)
    pass_prev(4)
    step(5)
    pass_next(1)
    step(6)
    pass_prev(5)
    step(7)
    core_send(1)
    core_send(3)
    ids_onward(1)
    pass_next(2)
    core_got(0)
    core_got(1)
    core_got(3)

    temper = jnp.exp(jnp.full((1, 1), lt_ref[0], F32))
    slope = 0.5 * temper
    shift = jnp.full((1, 1), 0.5 * of_ref[0], F32)

    def unit(a, b):
        at = pl.multiple_of(2 * b, 2)
        own = blocks[pl.ds(at, 2)].reshape(2 * ROWS, EMB)
        logit = dot(blocks[OTHER0 + a], own, NT)
        value = jnp.tanh(logit * slope + shift) * 8.0
        row = jnp.concatenate([ids[at, 0:1, :], ids[at + 1, 0:1, :]], axis=1).astype(F32)
        col = jnp.broadcast_to(ids[OTHER0 + a, 0:1, :].astype(F32), (128, ROWS)).T
        same = jnp.concatenate([col] * 4, axis=1) == row
        value = value + jnp.where(same, -8.0, 8.0)
        here = pl.ds(pl.multiple_of(a * ROWS, ROWS), ROWS)
        pair[here, pl.ds(pl.multiple_of(b * 2 * ROWS, 2 * ROWS), 2 * ROWS)] = value.astype(BF16)

    @pl.loop(0, 3)
    def _(u):
        unit(0, u + u // 2)

        @pl.when(u == 0)
        def _():
            pass_prev(6)

        @pl.when(u == 1)
        def _():
            pass_next(3)

        @pl.when(u == 2)
        def _():
            pass_prev(7)

    for q in (4, 5):
        got_next(1, q)
    for q in (2, 3):
        got_prev(1, q)
    for n in range(4):
        got_extra(n)
    for q in range(QS):
        got_onward(0, q)
    arrived("ring_id", 2, ids.at[block(0, 2)])
    core_send(2)

    @pl.loop(0, 6)
    def _(u):
        a = u // 3
        b = u - 3 * a
        unit(1 + 2 * a, b + b // 2)

    core_got(2)
    for q in range(QS):
        got_onward(1, q)
    arrived("ring_id", 5, ids.at[block(1, 2)])

    @pl.loop(0, 4)
    def _(u):
        unit(2, u)

    def own_terms(half, slot):
        rest = blocks[pl.ds(OTHER0, 4)].reshape(4 * ROWS, EMB)
        return dot(pair[:, pl.ds((2 * slot + half) * ROWS, ROWS)], rest, TN)

    def other_terms(slot):
        @pl.loop(0, 2)
        def _(n):
            cols = pl.ds(pl.multiple_of(n * HALF, HALF), HALF)
            own = blocks[pl.ds(0, 8), :, cols].reshape(8 * ROWS, HALF)
            grad[1, slot, :, cols] = dot(pair[pl.ds(slot * ROWS, ROWS), :], own, NN)

    def give(slot):
        part_out[slot] = own_terms(1, slot).astype(BF16)
        copy("part", slot, part_out.at[slot], part_in.at[slot], partner).start()

    def keep(slot):
        grad[0, slot] = own_terms(0, slot)
        arrived("part", slot, part_in.at[slot])
        grad[0, slot] += part_in[slot].astype(F32)

    def far_copy(k, q):
        return copy("far", QS * k + q, out_buf.at[k, 2, rows(q)], far_in.at[k, rows(q)], ring(k, 1 if q < 4 else 3))

    def next_copy(k, q):
        return copy("to_next", QS * k + q, out_buf.at[k, 3, rows(q)], near_in.at[k, 0, rows(q)], ring(k, 1))

    def prev_copy(k, q):
        return copy("to_prev", QS * k + q, out_buf.at[k, 1, rows(q)], near_in.at[k, 1, rows(q)], ring(k, 3))

    def extra_of(slot, q):
        if (slot, q) in ((3, 6), (3, 7), (1, 0), (1, 1)):
            return {(3, 6): 0, (3, 7): 1, (1, 0): 2, (1, 1): 3}[slot, q]
        return None

    def extra_back(n):
        return copy("y_extra", n, extra_out.at[rows(n)], extra_in.at[rows(n)], y_down)

    def send_far(k):
        for q in (0, 4, 1, 5, 2, 6, 3, 7):
            out_buf[k, 2, rows(q), :] = grad[k, 2, rows(q), :].astype(BF16)
            far_copy(k, q).start()

    def send_extra(slot):
        for q in range(QS):
            n = extra_of(slot, q)
            if n is not None:
                extra_out[rows(n), :] = grad[1, slot, rows(q), :].astype(BF16)
                extra_back(n).start()

    def send_near(k, slot, order, make):
        for q in order:
            n = extra_of(slot, q)
            if n is not None and k == 1:
                continue
            term = grad[k, slot, rows(q), :]
            if (q < 4) == (slot == 3):
                arrived("far", QS * k + q, far_in.at[k, rows(q)])
                term += far_in[k, rows(q), :].astype(F32)
            if n is not None:
                arrived("y_extra", n, extra_in.at[rows(n)])
                term += extra_in[rows(n), :].astype(F32)
            out_buf[k, slot, rows(q), :] = term.astype(BF16)
            make(k, q).start()

    other_terms(2)
    send_far(1)

    @pl.loop(0, 3)
    def _(u):
        unit(u + u // 2, 2)

    give(2)
    other_terms(3)
    send_extra(3)
    send_near(1, 3, BACK_NEXT, next_copy)
    keep(2)
    send_far(0)
    other_terms(1)
    send_extra(1)
    send_near(1, 1, BACK_PREV[1], prev_copy)
    give(3)
    give(1)
    keep(3)
    send_near(0, 3, BACK_NEXT, next_copy)
    keep(1)
    send_near(0, 1, BACK_PREV[0], prev_copy)
    other_terms(0)
    give(0)
    keep(0)

    def reduced(k, q):
        total = grad[k, 0, rows(q), :]
        if k == 0 or extra_of(3, q) is None:
            arrived("to_next", QS * k + q, near_in.at[k, 0, rows(q)])
            total += near_in[k, 0, rows(q), :].astype(F32)
        if k == 0 or extra_of(1, q) is None:
            arrived("to_prev", QS * k + q, near_in.at[k, 1, rows(q)])
            total += near_in[k, 1, rows(q), :].astype(F32)
        return total

    def back_copy(q):
        return copy("y_back", q, y_out.at[rows(q)], y_in.at[rows(q)], y_down)

    for q in BACK_ORDER:
        y_out[rows(q), :] = reduced(1, q).astype(BF16)
        back_copy(q).start()

    def rg_copy(q):
        return copy("rg", q, rg_theirs.at[rows(q)], rg_mine.at[pl.ds(ROWS + CHUNK * q, CHUNK)], partner)

    for q in BACK_ORDER:
        total = reduced(0, q)
        arrived("y_back", q, y_in.at[rows(q)])
        emb_grad = temper * (total + y_in[rows(q), :].astype(F32))
        scale = inv[rows(q), 0:1]
        unit_rows = raw[rows(q), :] * scale
        along = jnp.sum(unit_rows * emb_grad, axis=1, keepdims=True)
        value = ((emb_grad - unit_rows * along) * scale).astype(BF16)
        rg[rows(q), :] = value
        low, high = value[:, :HALF], value[:, HALF:]
        rg_mine[rows(q), :] = jnp.where(core == 0, low, high)
        rg_theirs[rows(q), :] = jnp.where(core == 0, high, low)
        rg_copy(q).start()

    for q in range(QS):
        arrived("rg", q, rg_mine.at[pl.ds(ROWS + CHUNK * q, CHUNK)])

    @pl.loop(0, FEAT // 256)
    def _(n):
        here = pl.ds(pl.multiple_of(n * 256, 256), 256)
        mat[here, :] = dot(s_t[here, :], rg_mine[...], NN)

    def z_rows(d):
        at = pl.ds(pl.multiple_of(lax.rem(pz + d, 4) * FEAT_Z, FEAT_Z), FEAT_Z)
        return mat[at, :256]

    def x_rows(d):
        pieces = []
        for k in range(8):
            at = pl.multiple_of(k * 4 * OWN_ROWS + lax.rem(px + d, 4) * OWN_ROWS, 8)
            pieces.append(mat[pl.ds(at, OWN_ROWS), 256:])
        return jnp.concatenate(pieces, axis=0)

    def p_copy(d):
        return copy("st_p", d, p_out.at[d], p_in.at[d], ring_z(d))

    def q_copy(d):
        return copy("st_q", d, q_out.at[d], q_in.at[d], ring_x(d))

    for d in (2, 1, 3):
        p_out[d] = z_rows(d).astype(BF16)
        p_copy(d).start()
        q_out[d] = x_rows(d).astype(BF16)
        q_copy(d).start()

    @pl.loop(0, FEAT // 256)
    def _(n):
        here = pl.ds(pl.multiple_of(n * 256, 256), 256)
        sg_ref[:, here] = dot(rg[...], w_ref[here, :], NT).astype(BF16)

    p_one = z_rows(0)
    for d in (1, 3, 2):
        arrived("st_p", d, p_in.at[d])
        p_one += p_in[d].astype(F32)
    p_sum[...] = p_one
    at = pl.multiple_of((1 - yh) * 4 * OWN_ROWS, 8)
    mid_out[0] = p_sum[pl.ds(at, 4 * OWN_ROWS), :].astype(BF16)
    copy("mid", 0, mid_out.at[0], mid_in.at[0], y_two).start()

    def q_rows(y):
        pieces = []
        for k in range(4):
            at = pl.multiple_of(k * 2 * OWN_ROWS + y * OWN_ROWS, 8)
            pieces.append(q_sum[pl.ds(at, OWN_ROWS), :])
        return jnp.concatenate(pieces, axis=0)

    q_one = x_rows(0)
    for d in (1, 3, 2):
        arrived("st_q", d, q_in.at[d])
        q_one += q_in[d].astype(F32)
    q_sum[...] = q_one
    mid_out[1] = q_rows(1 - yh).astype(BF16)
    copy("mid", 1, mid_out.at[1], mid_in.at[1], y_two).start()

    arrived("mid", 0, mid_in.at[0])
    at = pl.multiple_of(yh * 4 * OWN_ROWS, 8)
    p_two[...] = p_sum[pl.ds(at, 4 * OWN_ROWS), :] + mid_in[0].astype(F32)

    def end_rows(p, d):
        return pl.ds(pl.multiple_of(lax.rem(p + d, 4) * OWN_ROWS, 8), OWN_ROWS)

    def p_last(d):
        return copy("end_p", d, p_two.at[end_rows(px, d)], p_end.at[d], ring_x(d))

    def q_last(d):
        return copy("end_q", d, q_two.at[end_rows(pz, d)], q_end.at[d], ring_z(d))

    for d in (2, 1, 3):
        p_last(d).start()
    arrived("mid", 1, mid_in.at[1])
    q_two[...] = q_rows(yh) + mid_in[1].astype(F32)
    for d in (2, 1, 3):
        q_last(d).start()

    p_fin = p_two[end_rows(px, 0), :]
    q_fin = q_two[end_rows(pz, 0), :]
    for d in (1, 3, 2):
        arrived("end_p", d, p_end.at[d])
        p_fin += p_end[d]
    for d in (1, 3, 2):
        arrived("end_q", d, q_end.at[d])
        q_fin += q_end[d]
    both = jnp.concatenate([p_fin, q_fin], axis=1)
    first, second = both[:20], both[20:]
    theirs = jnp.where(core == 0, second, first)
    mine = jnp.where(core == 0, first, second)
    last_out[...] = jnp.concatenate([theirs, jnp.zeros((4, HALF), F32)], axis=0)
    copy("last", 0, last_out, last_in, partner).start()
    arrived("last", 0, last_in)
    got = last_in[:20, :]
    pg_ref[:, 0, :HALF] = jnp.where(core == 0, mine, got)
    pg_ref[:, 0, HALF:] = jnp.where(core == 0, got, mine)

    some = blocks.at[0]
    for q in range(QS):
        left("y", q, some.at[rows(q)])
        left("y_back", q, some.at[rows(q)])
        left("rg", q, rg_theirs.at[rows(q)])
    left("y_id", 0, ids.at[0])
    for k in range(2):
        for q in range(QS):
            if k == 0 or q < 6:
                left("ring", 3 * QS * k + q, some.at[rows(0)])
            if k == 0 or q >= 2:
                left("ring", 3 * QS * k + QS + q, some.at[rows(0)])
            left("ring", 3 * QS * k + 2 * QS + q, some.at[rows(0)])
            left("far", QS * k + q, some.at[rows(0)])
            if k == 0 or extra_of(3, q) is None:
                left("to_next", QS * k + q, some.at[rows(0)])
            if k == 0 or extra_of(1, q) is None:
                left("to_prev", QS * k + q, some.at[rows(0)])
    for n in range(6):
        left("ring_id", n, ids.at[0])
    for n in range(4):
        left("core", n, some)
        left("core_id", n, ids.at[0])
        left("part", n, some)
        left("extra", n, some.at[rows(0)])
        left("y_extra", n, some.at[rows(0)])
    left("core_s", 0, s_other)
    for d in (1, 2, 3):
        left("st_p", d, p_out.at[d])
        left("st_q", d, q_out.at[d])
        left("end_p", d, p_end.at[d])
        left("end_q", d, q_end.at[d])
    for n in range(2):
        left("mid", n, mid_out.at[n])
    left("last", 0, last_out)


def local(states, projection, prompt_ids, log_temper, logit_offset):
    vmem = pl.BlockSpec(memory_space=pltpu.VMEM)
    smem = pl.BlockSpec(memory_space=pltpu.SMEM)
    hbm = pl.BlockSpec(memory_space=pl.ANY)
    scratch = [
        ((ROWS, FEAT), BF16),
        ((FEAT, EMB), BF16),
        ((12, ROWS, EMB), BF16),
        ((12, 8, ROWS), jnp.int32),
        ((ROWS, EMB), F32),
        ((ROWS, 128), F32),
        ((4 * ROWS, 8 * ROWS), BF16),
        ((2, 4, ROWS, EMB), F32),
        ((2, 4, ROWS, EMB), BF16),
        ((2, ROWS, EMB), BF16),
        ((2, 2, ROWS, EMB), BF16),
        ((4 * CHUNK, EMB), BF16),
        ((4 * CHUNK, EMB), BF16),
        ((4, ROWS, EMB), BF16),
        ((4, ROWS, EMB), BF16),
        ((ROWS, EMB), BF16),
        ((ROWS, EMB), BF16),
        ((ROWS, EMB), BF16),
        ((2 * ROWS, HALF), BF16),
        ((ROWS, HALF), BF16),
        ((ROWS, FEAT), BF16),
        ((FEAT, 2 * ROWS), BF16),
        ((FEAT, HALF), F32),
        ((4, FEAT_Z, 256), BF16),
        ((4, FEAT_Z, 256), BF16),
        ((4, FEAT_Z, 256), BF16),
        ((4, FEAT_Z, 256), BF16),
        ((FEAT_Z, 256), F32),
        ((FEAT_Z, 256), F32),
        ((2, FEAT_Z // 2, 256), BF16),
        ((2, FEAT_Z // 2, 256), BF16),
        ((FEAT_Z // 2, 256), F32),
        ((FEAT_Z // 2, 256), F32),
        ((4, OWN_ROWS, 256), F32),
        ((4, OWN_ROWS, 256), F32),
        ((24, HALF), F32),
        ((24, HALF), F32),
    ]
    state_grad, owned = pl.pallas_call(
        kernel,
        out_shape=(
            jax.ShapeDtypeStruct((ROWS, FEAT), BF16),
            jax.ShapeDtypeStruct((20, 1, EMB), F32),
        ),
        in_specs=[hbm, hbm, vmem, smem, smem],
        out_specs=(vmem, vmem),
        scratch_shapes=[pltpu.VMEM(shape, kind) for shape, kind in scratch]
        + [pltpu.SemaphoreType.DMA((3,))]
        + [pltpu.SemaphoreType.DMA((Sems.total(),)), pltpu.SemaphoreType.DMA((Sems.total(),))],
        compiler_params=pltpu.CompilerParams(
            collective_id=0, has_side_effects=True, vmem_limit_bytes=60 * 2**20
        ),
        name="contrast",
    )(states[0], projection[0], prompt_ids.reshape(1, ROWS), log_temper, logit_offset)
    return state_grad[None], owned.reshape(1, 20, EMB)


def solution(mesh):
    return jax.shard_map(
        local,
        mesh=mesh,
        in_specs=(P("tower", "batch", None), P("tower", None, None), P("batch"), P(), P()),
        out_specs=(P("tower", "batch", None), P("tower", "batch", None)),
        check_vma=False,
    )
```

```python
import jax
import jax.numpy as jnp
from jax import lax
from jax.experimental import pallas as pl
from jax.experimental.pallas import tpu as pltpu
from jax.sharding import PartitionSpec as P

EPSILON = 1e-06
MESH = pl.DeviceIdType.MESH
F32, BF16 = jnp.float32, jnp.bfloat16
NT = (((1,), (1,)), ((), ()))
TN = (((0,), (0,)), ((), ()))
NN = (((1,), (0,)), ((), ()))

ROWS = 256
EMB = 1024
FEAT = 1280
CHUNK = 32
QS = ROWS // CHUNK
HALF = EMB // 2
FEAT_Z = FEAT // 4
OWN_ROWS = 40
OTHER0 = 8

Y_ORDER = (0, 4, 1, 5, 2, 6, 3, 7)
NEXT_ORDER = (0, 1, 2, 3, 6, 7, 4, 5)
PREV_ORDER = (4, 5, 6, 7, 0, 1, 2, 3)
BACK_ORDER = (4, 5, 6, 0, 7, 1, 2, 3)


class Sems:
    sizes = dict(
        y=QS, y_id=1, ring=2 * 3 * QS, ring_id=2 * 3, core=4, core_id=4, core_s=1, extra=4,
        part=4, far=2 * QS, to_next=2 * QS, to_prev=2 * QS, y_extra=4, y_back=QS,
        rg=QS, st_p=4, st_q=4, mid=2, end_p=4, end_q=4, last=1,
    )

    @classmethod
    def at(cls, name, index=0):
        base = 0
        for key, size in cls.sizes.items():
            if key == name:
                return base + index
            base += size
        raise KeyError(name)

    @classmethod
    def total(cls):
        return sum(cls.sizes.values())


def dot(a, b, dims):
    return lax.dot_general(a, b, dims, preferred_element_type=F32)


def kernel(
    s_hbm, w_hbm, id_ref, lt_ref, of_ref, sg_ref, pg_ref,
    s_ref, w_ref, blocks, ids, raw, inv, pair, grad, out_buf, far_in, near_in, extra_out, extra_in, part_out, part_in, y_out, y_in,
    rg, rg_mine, rg_theirs, s_other, s_t, mat, p_out, q_out, p_in, q_in, p_sum, q_sum, mid_out, mid_in,
    p_two, q_two, p_end, q_end, last_out, last_in, lsem, ssem, rsem,
):
    tower = lax.axis_index("tower")
    batch = lax.axis_index("batch")
    core = lax.rem(batch, 2)
    px = lax.rem(batch // 2, 4)
    yh = lax.rem(batch // 8, 2)
    pz = batch // 16
    other = 1 - tower

    def dev(t, z, y, x, c):
        return (t, ((z * 2 + y) * 4 + x) * 2 + c)

    def ring_x(d):
        return dev(tower, pz, yh, lax.rem(px + d, 4), core)

    def ring_z(d):
        return dev(tower, lax.rem(pz + d, 4), yh, px, core)

    def ring(k, d):
        r = tower if k == 0 else other
        return dev(tower, lax.rem(pz + r * d, 4), yh, lax.rem(px + (1 - r) * d, 4), core)

    partner = dev(tower, pz, yh, px, 1 - core)
    y_up = dev(other, pz, jnp.where(tower == 1, 1 - yh, yh), px, core)
    y_down = dev(other, pz, jnp.where(tower == 0, 1 - yh, yh), px, core)
    y_two = dev(tower, pz, 1 - yh, px, core)

    def block(k, slot):
        return 2 * slot if k == 0 else OTHER0 + slot

    def copy(name, index, src, dst, where):
        n = Sems.at(name) + index
        return pltpu.make_async_remote_copy(
            src_ref=src, dst_ref=dst, send_sem=ssem.at[n], recv_sem=rsem.at[n],
            device_id=where, device_id_type=MESH,
        )

    def arrived(name, index, ref):
        copy(name, index, ref, ref, partner).wait_recv()

    def left(name, index, ref):
        copy(name, index, ref, ref, partner).wait_send()

    def rows(q):
        return pl.ds(CHUNK * q, CHUNK)

    def piece(k, slot, q):
        return blocks.at[block(k, slot), rows(q)]

    barrier = pltpu.get_barrier_semaphore()
    near = [partner, y_up, y_down, y_two] + [ring_x(d) for d in (1, 2, 3)] + [ring_z(d) for d in (1, 2, 3)]
    for where in near:
        pl.semaphore_signal(barrier, inc=1, device_id=where, device_id_type=MESH)

    def halves(n):
        return pl.ds(n * HALF, HALF)

    loads = [pltpu.make_async_copy(s_hbm, s_ref, lsem.at[0])]
    loads += [pltpu.make_async_copy(w_hbm.at[:, halves(n)], w_ref.at[:, halves(n)], lsem.at[1 + n]) for n in range(2)]
    for load in loads:
        load.start()
    ids[0] = jnp.broadcast_to(id_ref[...], (8, ROWS))
    loads[0].wait()
    for n in range(2):
        loads[1 + n].wait()
        raw[:, halves(n)] = dot(s_ref[...], w_ref[:, halves(n)], NN)

    pl.semaphore_wait(barrier, len(near))

    def to_next(k, q):
        return copy("ring", 3 * QS * k + q, piece(k, 0, q), piece(k, 1, q), ring(k, 1))

    def to_prev(k, q):
        return copy("ring", 3 * QS * k + QS + q, piece(k, 0, q), piece(k, 3, q), ring(k, 3))

    def onward(k, q):
        slot = 1 if q < QS // 2 else 3
        return copy("ring", 3 * QS * k + 2 * QS + q, piece(k, slot, q), piece(k, 2, q), ring(k, slot))

    def got_next(k, q):
        arrived("ring", 3 * QS * k + q, piece(k, 1, q))

    def got_prev(k, q):
        arrived("ring", 3 * QS * k + QS + q, piece(k, 3, q))

    def got_onward(k, q):
        arrived("ring", 3 * QS * k + 2 * QS + q, piece(k, 2, q))

    def extra(n):
        slot, q = ((1, 6), (1, 7), (3, 0), (3, 1))[n]
        return copy("extra", n, piece(0, slot, q), piece(1, slot, q), y_up)

    def got_extra(n):
        slot, q = ((1, 6), (1, 7), (3, 0), (3, 1))[n]
        arrived("extra", n, piece(1, slot, q))

    def ids_out(k):
        copy("ring_id", 3 * k, ids.at[block(k, 0)], ids.at[block(k, 1)], ring(k, 1)).start()
        copy("ring_id", 3 * k + 1, ids.at[block(k, 0)], ids.at[block(k, 3)], ring(k, 3)).start()

    def ids_onward(k):
        arrived("ring_id", 3 * k, ids.at[block(k, 1)])
        copy("ring_id", 3 * k + 2, ids.at[block(k, 1)], ids.at[block(k, 2)], ring(k, 1)).start()
        arrived("ring_id", 3 * k + 1, ids.at[block(k, 3)])

    def core_send(slot):
        copy("core", slot, blocks.at[2 * slot], blocks.at[2 * slot + 1], partner).start()
        copy("core_id", slot, ids.at[2 * slot], ids.at[2 * slot + 1], partner).start()

    def core_got(slot):
        arrived("core", slot, blocks.at[2 * slot + 1])
        arrived("core_id", slot, ids.at[2 * slot + 1])

    copy("y_id", 0, ids.at[0], ids.at[OTHER0], y_up).start()
    ids_out(0)
    for m, q in enumerate(Y_ORDER):
        part = raw[rows(q), :]
        length = jnp.sqrt(jnp.sum(part * part, axis=1, keepdims=True) + EPSILON)
        scale = 1.0 / length
        inv[rows(q), :] = jnp.broadcast_to(scale, (CHUNK, 128))
        blocks[0, rows(q)] = (part * scale).astype(BF16)
        copy("y", q, piece(0, 0, q), piece(1, 0, q), y_up).start()
        if m < 6:
            (to_next(0, q) if q < 4 else to_prev(0, q)).start()
    for q in (3, 6, 7, 4, 5):
        to_next(0, q).start()
    for q in (7, 0, 1, 2, 3):
        to_prev(0, q).start()
    core_send(0)
    copy("core_s", 0, s_ref, s_other, partner).start()
    s_t[:, :ROWS] = s_ref[...].T

    def step(m):
        q = Y_ORDER[m]
        arrived("y", q, piece(1, 0, q))
        if q < 6:
            to_next(1, q).start()
        if q >= 2:
            to_prev(1, q).start()
        q = NEXT_ORDER[m]
        got_next(0, q)
        if q < 4:
            onward(0, q).start()
        elif q >= 6:
            extra(q - 6).start()
        q = PREV_ORDER[m]
        got_prev(0, q)
        if q >= 4:
            onward(0, q).start()
        elif q < 2:
            extra(2 + q).start()

    def pass_next(q):
        got_next(1, q)
        onward(1, q).start()

    def pass_prev(q):
        got_prev(1, q)
        onward(1, q).start()

    step(0)
    step(1)
    ids_onward(0)
    arrived("y_id", 0, ids.at[OTHER0])
    ids_out(1)
    arrived("core_s", 0, s_other)
    s_t[:, ROWS:] = s_other[...].T
    step(2)
    step(3)
    pass_next(0)
    step(4)
    pass_prev(4)
    step(5)
    pass_next(1)
    step(6)
    pass_prev(5)
    step(7)
    core_send(1)
    core_send(3)
    ids_onward(1)
    pass_next(2)
    core_got(0)
    core_got(1)
    core_got(3)

    temper = jnp.exp(jnp.full((1, 1), lt_ref[0], F32))
    slope = 0.5 * temper
    shift = jnp.full((1, 1), 0.5 * of_ref[0], F32)

    def unit(a, b):
        at = pl.multiple_of(2 * b, 2)
        own = blocks[pl.ds(at, 2)].reshape(2 * ROWS, EMB)
        logit = dot(blocks[OTHER0 + a], own, NT)
        value = jnp.tanh(logit * slope + shift) * 8.0
        row = jnp.concatenate([ids[at, 0:1, :], ids[at + 1, 0:1, :]], axis=1).astype(F32)
        col = jnp.broadcast_to(ids[OTHER0 + a, 0:1, :].astype(F32), (128, ROWS)).T
        same = jnp.concatenate([col] * 4, axis=1) == row
        value = value + jnp.where(same, -8.0, 8.0)
        here = pl.ds(pl.multiple_of(a * ROWS, ROWS), ROWS)
        pair[here, pl.ds(pl.multiple_of(b * 2 * ROWS, 2 * ROWS), 2 * ROWS)] = value.astype(BF16)

    @pl.loop(0, 3)
    def _(u):
        unit(0, u + u // 2)

        @pl.when(u == 0)
        def _():
            pass_prev(6)

        @pl.when(u == 1)
        def _():
            pass_next(3)

        @pl.when(u == 2)
        def _():
            pass_prev(7)

    for q in (4, 5):
        got_next(1, q)
    for q in (2, 3):
        got_prev(1, q)
    for n in range(4):
        got_extra(n)
    for q in range(QS):
        got_onward(0, q)
    arrived("ring_id", 2, ids.at[block(0, 2)])
    core_send(2)

    @pl.loop(0, 6)
    def _(u):
        a = u // 3
        b = u - 3 * a
        unit(1 + 2 * a, b + b // 2)

    core_got(2)
    for q in range(QS):
        got_onward(1, q)
    arrived("ring_id", 5, ids.at[block(1, 2)])

    @pl.loop(0, 4)
    def _(u):
        unit(2, u)

    def own_terms(half, slot):
        rest = blocks[pl.ds(OTHER0, 4)].reshape(4 * ROWS, EMB)
        return dot(pair[:, pl.ds((2 * slot + half) * ROWS, ROWS)], rest, TN)

    def other_terms(slot):
        @pl.loop(0, 2)
        def _(n):
            cols = pl.ds(pl.multiple_of(n * HALF, HALF), HALF)
            own = blocks[pl.ds(0, 8), :, cols].reshape(8 * ROWS, HALF)
            grad[1, slot, :, cols] = dot(pair[pl.ds(slot * ROWS, ROWS), :], own, NN)

    def give(slot):
        part_out[slot] = own_terms(1, slot).astype(BF16)
        copy("part", slot, part_out.at[slot], part_in.at[slot], partner).start()

    def keep(slot):
        grad[0, slot] = own_terms(0, slot)
        arrived("part", slot, part_in.at[slot])
        grad[0, slot] += part_in[slot].astype(F32)

    def far_copy(k, q):
        return copy("far", QS * k + q, out_buf.at[k, 2, rows(q)], far_in.at[k, rows(q)], ring(k, 1 if q < 4 else 3))

    def next_copy(k, q):
        return copy("to_next", QS * k + q, out_buf.at[k, 3, rows(q)], near_in.at[k, 0, rows(q)], ring(k, 1))

    def prev_copy(k, q):
        return copy("to_prev", QS * k + q, out_buf.at[k, 1, rows(q)], near_in.at[k, 1, rows(q)], ring(k, 3))

    def extra_of(slot, q):
        if (slot, q) in ((3, 6), (3, 7), (1, 0), (1, 1)):
            return {(3, 6): 0, (3, 7): 1, (1, 0): 2, (1, 1): 3}[slot, q]
        return None

    def extra_back(n):
        return copy("y_extra", n, extra_out.at[rows(n)], extra_in.at[rows(n)], y_down)

    def send_far(k):
        for q in (0, 4, 1, 5, 2, 6, 3, 7):
            out_buf[k, 2, rows(q), :] = grad[k, 2, rows(q), :].astype(BF16)
            far_copy(k, q).start()

    def send_extra(slot):
        for q in range(QS):
            n = extra_of(slot, q)
            if n is not None:
                extra_out[rows(n), :] = grad[1, slot, rows(q), :].astype(BF16)
                extra_back(n).start()

    def send_near(k, slot, order, make):
        for q in order:
            n = extra_of(slot, q)
            if n is not None and k == 1:
                continue
            term = grad[k, slot, rows(q), :]
            if (q < 4) == (slot == 3):
                arrived("far", QS * k + q, far_in.at[k, rows(q)])
                term += far_in[k, rows(q), :].astype(F32)
            if n is not None:
                arrived("y_extra", n, extra_in.at[rows(n)])
                term += extra_in[rows(n), :].astype(F32)
            out_buf[k, slot, rows(q), :] = term.astype(BF16)
            make(k, q).start()

    def reduced(k, q):
        total = grad[k, 0, rows(q), :]
        if k == 0 or extra_of(3, q) is None:
            arrived("to_next", QS * k + q, near_in.at[k, 0, rows(q)])
            total += near_in[k, 0, rows(q), :].astype(F32)
        if k == 0 or extra_of(1, q) is None:
            arrived("to_prev", QS * k + q, near_in.at[k, 1, rows(q)])
            total += near_in[k, 1, rows(q), :].astype(F32)
        return total

    def back_copy(q):
        return copy("y_back", q, y_out.at[rows(q)], y_in.at[rows(q)], y_down)

    def send_back(order):
        for q in order:
            y_out[rows(q), :] = reduced(1, q).astype(BF16)
            back_copy(q).start()

    other_terms(2)
    send_far(1)

    @pl.loop(0, 3)
    def _(u):
        unit(u + u // 2, 2)

    give(2)
    other_terms(3)
    send_extra(3)
    send_near(1, 3, (4, 5), next_copy)
    keep(2)
    send_far(0)
    other_terms(1)
    send_extra(1)
    send_near(1, 1, (2, 3), prev_copy)
    send_near(1, 3, (0, 1, 2, 3), next_copy)
    send_near(1, 1, (4, 5, 6, 7), prev_copy)
    give(3)
    give(1)
    other_terms(0)
    keep(3)
    send_near(0, 3, (4, 5), next_copy)
    keep(1)
    send_near(0, 1, (2, 3), prev_copy)
    send_back(BACK_ORDER[:2])
    for n in range(4):
        send_near(0, 3, (n,), next_copy)
        send_near(0, 1, (n + 4,), prev_copy)
    send_near(0, 3, (6, 7), next_copy)
    send_near(0, 1, (0, 1), prev_copy)
    give(0)
    send_back(BACK_ORDER[2:4])
    keep(0)
    send_back(BACK_ORDER[4:])

    def rg_copy(q):
        return copy("rg", q, rg_theirs.at[rows(q)], rg_mine.at[pl.ds(ROWS + CHUNK * q, CHUNK)], partner)

    for q in BACK_ORDER:
        total = reduced(0, q)
        arrived("y_back", q, y_in.at[rows(q)])
        emb_grad = temper * (total + y_in[rows(q), :].astype(F32))
        scale = inv[rows(q), 0:1]
        unit_rows = raw[rows(q), :] * scale
        along = jnp.sum(unit_rows * emb_grad, axis=1, keepdims=True)
        value = ((emb_grad - unit_rows * along) * scale).astype(BF16)
        rg[rows(q), :] = value
        low, high = value[:, :HALF], value[:, HALF:]
        rg_mine[rows(q), :] = jnp.where(core == 0, low, high)
        rg_theirs[rows(q), :] = jnp.where(core == 0, high, low)
        rg_copy(q).start()

    for q in range(QS):
        arrived("rg", q, rg_mine.at[pl.ds(ROWS + CHUNK * q, CHUNK)])

    @pl.loop(0, FEAT // 256)
    def _(n):
        here = pl.ds(pl.multiple_of(n * 256, 256), 256)
        mat[here, :] = dot(s_t[here, :], rg_mine[...], NN)

    def z_rows(d):
        at = pl.ds(pl.multiple_of(lax.rem(pz + d, 4) * FEAT_Z, FEAT_Z), FEAT_Z)
        return mat[at, :256]

    def x_rows(d):
        pieces = []
        for k in range(8):
            at = pl.multiple_of(k * 4 * OWN_ROWS + lax.rem(px + d, 4) * OWN_ROWS, 8)
            pieces.append(mat[pl.ds(at, OWN_ROWS), 256:])
        return jnp.concatenate(pieces, axis=0)

    def p_copy(d):
        return copy("st_p", d, p_out.at[d], p_in.at[d], ring_z(d))

    def q_copy(d):
        return copy("st_q", d, q_out.at[d], q_in.at[d], ring_x(d))

    for d in (2, 1, 3):
        p_out[d] = z_rows(d).astype(BF16)
        p_copy(d).start()
        q_out[d] = x_rows(d).astype(BF16)
        q_copy(d).start()

    @pl.loop(0, FEAT // 256)
    def _(n):
        here = pl.ds(pl.multiple_of(n * 256, 256), 256)
        sg_ref[:, here] = dot(rg[...], w_ref[here, :], NT).astype(BF16)

    p_one = z_rows(0)
    for d in (1, 3, 2):
        arrived("st_p", d, p_in.at[d])
        p_one += p_in[d].astype(F32)
    p_sum[...] = p_one
    at = pl.multiple_of((1 - yh) * 4 * OWN_ROWS, 8)
    mid_out[0] = p_sum[pl.ds(at, 4 * OWN_ROWS), :].astype(BF16)
    copy("mid", 0, mid_out.at[0], mid_in.at[0], y_two).start()

    def q_rows(y):
        pieces = []
        for k in range(4):
            at = pl.multiple_of(k * 2 * OWN_ROWS + y * OWN_ROWS, 8)
            pieces.append(q_sum[pl.ds(at, OWN_ROWS), :])
        return jnp.concatenate(pieces, axis=0)

    q_one = x_rows(0)
    for d in (1, 3, 2):
        arrived("st_q", d, q_in.at[d])
        q_one += q_in[d].astype(F32)
    q_sum[...] = q_one
    mid_out[1] = q_rows(1 - yh).astype(BF16)
    copy("mid", 1, mid_out.at[1], mid_in.at[1], y_two).start()

    arrived("mid", 0, mid_in.at[0])
    at = pl.multiple_of(yh * 4 * OWN_ROWS, 8)
    p_two[...] = p_sum[pl.ds(at, 4 * OWN_ROWS), :] + mid_in[0].astype(F32)

    def end_rows(p, d):
        return pl.ds(pl.multiple_of(lax.rem(p + d, 4) * OWN_ROWS, 8), OWN_ROWS)

    def p_last(d):
        return copy("end_p", d, p_two.at[end_rows(px, d)], p_end.at[d], ring_x(d))

    def q_last(d):
        return copy("end_q", d, q_two.at[end_rows(pz, d)], q_end.at[d], ring_z(d))

    for d in (2, 1, 3):
        p_last(d).start()
    arrived("mid", 1, mid_in.at[1])
    q_two[...] = q_rows(yh) + mid_in[1].astype(F32)
    for d in (2, 1, 3):
        q_last(d).start()

    p_fin = p_two[end_rows(px, 0), :]
    q_fin = q_two[end_rows(pz, 0), :]
    for d in (1, 3, 2):
        arrived("end_p", d, p_end.at[d])
        p_fin += p_end[d]
    for d in (1, 3, 2):
        arrived("end_q", d, q_end.at[d])
        q_fin += q_end[d]
    both = jnp.concatenate([p_fin, q_fin], axis=1)
    first, second = both[:20], both[20:]
    theirs = jnp.where(core == 0, second, first)
    mine = jnp.where(core == 0, first, second)
    last_out[...] = jnp.concatenate([theirs, jnp.zeros((4, HALF), F32)], axis=0)
    copy("last", 0, last_out, last_in, partner).start()
    arrived("last", 0, last_in)
    got = last_in[:20, :]
    pg_ref[:, 0, :HALF] = jnp.where(core == 0, mine, got)
    pg_ref[:, 0, HALF:] = jnp.where(core == 0, got, mine)

    some = blocks.at[0]
    for q in range(QS):
        left("y", q, some.at[rows(q)])
        left("y_back", q, some.at[rows(q)])
        left("rg", q, rg_theirs.at[rows(q)])
    left("y_id", 0, ids.at[0])
    for k in range(2):
        for q in range(QS):
            if k == 0 or q < 6:
                left("ring", 3 * QS * k + q, some.at[rows(0)])
            if k == 0 or q >= 2:
                left("ring", 3 * QS * k + QS + q, some.at[rows(0)])
            left("ring", 3 * QS * k + 2 * QS + q, some.at[rows(0)])
            left("far", QS * k + q, some.at[rows(0)])
            if k == 0 or extra_of(3, q) is None:
                left("to_next", QS * k + q, some.at[rows(0)])
            if k == 0 or extra_of(1, q) is None:
                left("to_prev", QS * k + q, some.at[rows(0)])
    for n in range(6):
        left("ring_id", n, ids.at[0])
    for n in range(4):
        left("core", n, some)
        left("core_id", n, ids.at[0])
        left("part", n, some)
        left("extra", n, some.at[rows(0)])
        left("y_extra", n, some.at[rows(0)])
    left("core_s", 0, s_other)
    for d in (1, 2, 3):
        left("st_p", d, p_out.at[d])
        left("st_q", d, q_out.at[d])
        left("end_p", d, p_end.at[d])
        left("end_q", d, q_end.at[d])
    for n in range(2):
        left("mid", n, mid_out.at[n])
    left("last", 0, last_out)


def local(states, projection, prompt_ids, log_temper, logit_offset):
    vmem = pl.BlockSpec(memory_space=pltpu.VMEM)
    smem = pl.BlockSpec(memory_space=pltpu.SMEM)
    hbm = pl.BlockSpec(memory_space=pl.ANY)
    scratch = [
        ((ROWS, FEAT), BF16),
        ((FEAT, EMB), BF16),
        ((12, ROWS, EMB), BF16),
        ((12, 8, ROWS), jnp.int32),
        ((ROWS, EMB), F32),
        ((ROWS, 128), F32),
        ((4 * ROWS, 8 * ROWS), BF16),
        ((2, 4, ROWS, EMB), F32),
        ((2, 4, ROWS, EMB), BF16),
        ((2, ROWS, EMB), BF16),
        ((2, 2, ROWS, EMB), BF16),
        ((4 * CHUNK, EMB), BF16),
        ((4 * CHUNK, EMB), BF16),
        ((4, ROWS, EMB), BF16),
        ((4, ROWS, EMB), BF16),
        ((ROWS, EMB), BF16),
        ((ROWS, EMB), BF16),
        ((ROWS, EMB), BF16),
        ((2 * ROWS, HALF), BF16),
        ((ROWS, HALF), BF16),
        ((ROWS, FEAT), BF16),
        ((FEAT, 2 * ROWS), BF16),
        ((FEAT, HALF), F32),
        ((4, FEAT_Z, 256), BF16),
        ((4, FEAT_Z, 256), BF16),
        ((4, FEAT_Z, 256), BF16),
        ((4, FEAT_Z, 256), BF16),
        ((FEAT_Z, 256), F32),
        ((FEAT_Z, 256), F32),
        ((2, FEAT_Z // 2, 256), BF16),
        ((2, FEAT_Z // 2, 256), BF16),
        ((FEAT_Z // 2, 256), F32),
        ((FEAT_Z // 2, 256), F32),
        ((4, OWN_ROWS, 256), F32),
        ((4, OWN_ROWS, 256), F32),
        ((24, HALF), F32),
        ((24, HALF), F32),
    ]
    state_grad, owned = pl.pallas_call(
        kernel,
        out_shape=(
            jax.ShapeDtypeStruct((ROWS, FEAT), BF16),
            jax.ShapeDtypeStruct((20, 1, EMB), F32),
        ),
        in_specs=[hbm, hbm, vmem, smem, smem],
        out_specs=(vmem, vmem),
        scratch_shapes=[pltpu.VMEM(shape, kind) for shape, kind in scratch]
        + [pltpu.SemaphoreType.DMA((3,))]
        + [pltpu.SemaphoreType.DMA((Sems.total(),)), pltpu.SemaphoreType.DMA((Sems.total(),))],
        compiler_params=pltpu.CompilerParams(
            collective_id=0, has_side_effects=True, vmem_limit_bytes=60 * 2**20
        ),
        name="contrast",
    )(states[0], projection[0], prompt_ids.reshape(1, ROWS), log_temper, logit_offset)
    return state_grad[None], owned.reshape(1, 20, EMB)


def solution(mesh):
    return jax.shard_map(
        local,
        mesh=mesh,
        in_specs=(P("tower", "batch", None), P("tower", None, None), P("batch"), P(), P()),
        out_specs=(P("tower", "batch", None), P("tower", "batch", None)),
        check_vma=False,
    )
```

```python
import jax
import jax.numpy as jnp
from jax import lax
from jax.experimental import pallas as pl
from jax.experimental.pallas import tpu as pltpu
from jax.sharding import PartitionSpec as P

EPSILON = 1e-06
MESH = pl.DeviceIdType.MESH
F32, BF16 = jnp.float32, jnp.bfloat16
NT = (((1,), (1,)), ((), ()))
TN = (((0,), (0,)), ((), ()))
NN = (((1,), (0,)), ((), ()))

ROWS = 256
EMB = 1024
FEAT = 1280
CHUNK = 32
QS = ROWS // CHUNK
HALF = EMB // 2
FEAT_Z = FEAT // 4
OWN_ROWS = 40
OTHER0 = 8

Y_ORDER = (0, 4, 1, 5, 2, 6, 3, 7)
NEXT_ORDER = (0, 1, 2, 3, 6, 7, 4, 5)
PREV_ORDER = (4, 5, 6, 7, 0, 1, 2, 3)
BACK_ORDER = (4, 5, 6, 0, 7, 1, 2, 3)


class Sems:
    sizes = dict(
        y=QS, y_id=1, ring=2 * 3 * QS, ring_id=2 * 3, core=4, core_id=4, core_s=1, extra=4,
        part=4, far=2 * QS, to_next=2 * QS, to_prev=2 * QS, y_extra=4, y_back=QS,
        rg=QS, st=8, end=16, last=1,
    )

    @classmethod
    def at(cls, name, index=0):
        base = 0
        for key, size in cls.sizes.items():
            if key == name:
                return base + index
            base += size
        raise KeyError(name)

    @classmethod
    def total(cls):
        return sum(cls.sizes.values())


def dot(a, b, dims):
    return lax.dot_general(a, b, dims, preferred_element_type=F32)


def kernel(
    s_hbm, w_hbm, id_hbm, lt_hbm, of_hbm, sg_ref, pg_ref,
    s_ref, w_ref, id_ref, lt_ref, of_ref, blocks, ids, raw, inv, pair, grad, out_buf, far_in, near_in, extra_out, extra_in, part_out, part_in, y_out, y_in,
    rg, rg_mine, rg_theirs, s_other, s_t, s_x, tall, st_out, st_in, st_sum, end_out, end_in, last_out, last_in,
    lsem, ssem, rsem,
):
    tower = lax.axis_index("tower")
    batch = lax.axis_index("batch")
    core = lax.rem(batch, 2)
    px = lax.rem(batch // 2, 4)
    yh = lax.rem(batch // 8, 2)
    pz = batch // 16
    other = 1 - tower

    def dev(t, z, y, x, c):
        return (t, ((z * 2 + y) * 4 + x) * 2 + c)

    def ring_x(d):
        return dev(tower, pz, yh, lax.rem(px + d, 4), core)

    def ring_z(d):
        return dev(tower, lax.rem(pz + d, 4), yh, px, core)

    def ring(k, d):
        r = tower if k == 0 else other
        return dev(tower, lax.rem(pz + r * d, 4), yh, lax.rem(px + (1 - r) * d, 4), core)

    partner = dev(tower, pz, yh, px, 1 - core)
    y_up = dev(other, pz, jnp.where(tower == 1, 1 - yh, yh), px, core)
    y_down = dev(other, pz, jnp.where(tower == 0, 1 - yh, yh), px, core)

    def plane(n, dy, d):
        x = lax.rem(px + d, 4) if n == 0 else px
        z = pz if n == 0 else lax.rem(pz + d, 4)
        return dev(tower, z, 1 - yh if dy else yh, x, core)

    def block(k, slot):
        return 2 * slot if k == 0 else OTHER0 + slot

    def copy(name, index, src, dst, where):
        n = Sems.at(name) + index
        return pltpu.make_async_remote_copy(
            src_ref=src, dst_ref=dst, send_sem=ssem.at[n], recv_sem=rsem.at[n],
            device_id=where, device_id_type=MESH,
        )

    def arrived(name, index, ref):
        copy(name, index, ref, ref, partner).wait_recv()

    def left(name, index, ref):
        copy(name, index, ref, ref, partner).wait_send()

    def rows(q):
        return pl.ds(CHUNK * q, CHUNK)

    def piece(k, slot, q):
        return blocks.at[block(k, slot), rows(q)]

    barrier = pltpu.get_barrier_semaphore()
    near = [partner, y_up, y_down, plane(0, 1, 0)]
    near += [plane(n, dy, d) for n in range(2) for dy in range(2) for d in (1, 2, 3)]
    for where in near:
        pl.semaphore_signal(barrier, inc=1, device_id=where, device_id_type=MESH)

    def halves(n):
        return pl.ds(n * HALF, HALF)

    loads = [pltpu.make_async_copy(s_hbm, s_ref, lsem.at[0])]
    loads += [pltpu.make_async_copy(w_hbm.at[:, halves(n)], w_ref.at[:, halves(n)], lsem.at[1 + n]) for n in range(2)]
    small = [(id_hbm, id_ref), (lt_hbm, lt_ref), (of_hbm, of_ref)]
    small = [pltpu.make_async_copy(src, dst, lsem.at[3 + n]) for n, (src, dst) in enumerate(small)]
    for load in loads + small:
        load.start()
    small[0].wait()
    ids[0] = jnp.broadcast_to(id_ref[...], (8, ROWS))
    small[1].wait()
    small[2].wait()
    loads[0].wait()
    for n in range(2):
        loads[1 + n].wait()
        raw[:, halves(n)] = dot(s_ref[...], w_ref[:, halves(n)], NN)

    pl.semaphore_wait(barrier, len(near))

    def to_next(k, q):
        return copy("ring", 3 * QS * k + q, piece(k, 0, q), piece(k, 1, q), ring(k, 1))

    def to_prev(k, q):
        return copy("ring", 3 * QS * k + QS + q, piece(k, 0, q), piece(k, 3, q), ring(k, 3))

    def onward(k, q):
        slot = 1 if q < QS // 2 else 3
        return copy("ring", 3 * QS * k + 2 * QS + q, piece(k, slot, q), piece(k, 2, q), ring(k, slot))

    def got_next(k, q):
        arrived("ring", 3 * QS * k + q, piece(k, 1, q))

    def got_prev(k, q):
        arrived("ring", 3 * QS * k + QS + q, piece(k, 3, q))

    def got_onward(k, q):
        arrived("ring", 3 * QS * k + 2 * QS + q, piece(k, 2, q))

    def extra(n):
        slot, q = ((1, 6), (1, 7), (3, 0), (3, 1))[n]
        return copy("extra", n, piece(0, slot, q), piece(1, slot, q), y_up)

    def got_extra(n):
        slot, q = ((1, 6), (1, 7), (3, 0), (3, 1))[n]
        arrived("extra", n, piece(1, slot, q))

    def ids_out(k):
        copy("ring_id", 3 * k, ids.at[block(k, 0)], ids.at[block(k, 1)], ring(k, 1)).start()
        copy("ring_id", 3 * k + 1, ids.at[block(k, 0)], ids.at[block(k, 3)], ring(k, 3)).start()

    def ids_onward(k):
        arrived("ring_id", 3 * k, ids.at[block(k, 1)])
        copy("ring_id", 3 * k + 2, ids.at[block(k, 1)], ids.at[block(k, 2)], ring(k, 1)).start()
        arrived("ring_id", 3 * k + 1, ids.at[block(k, 3)])

    def core_send(slot):
        copy("core", slot, blocks.at[2 * slot], blocks.at[2 * slot + 1], partner).start()
        copy("core_id", slot, ids.at[2 * slot], ids.at[2 * slot + 1], partner).start()

    def core_got(slot):
        arrived("core", slot, blocks.at[2 * slot + 1])
        arrived("core_id", slot, ids.at[2 * slot + 1])

    copy("y_id", 0, ids.at[0], ids.at[OTHER0], y_up).start()
    ids_out(0)
    for m, q in enumerate(Y_ORDER):
        part = raw[rows(q), :]
        length = jnp.sqrt(jnp.sum(part * part, axis=1, keepdims=True) + EPSILON)
        scale = 1.0 / length
        inv[rows(q), :] = jnp.broadcast_to(scale, (CHUNK, 128))
        blocks[0, rows(q)] = (part * scale).astype(BF16)
        copy("y", q, piece(0, 0, q), piece(1, 0, q), y_up).start()
        if m < 6:
            (to_next(0, q) if q < 4 else to_prev(0, q)).start()
    for q in (3, 6, 7, 4, 5):
        to_next(0, q).start()
    for q in (7, 0, 1, 2, 3):
        to_prev(0, q).start()
    core_send(0)
    def turn(states, first):
        tall[...] = states[...].astype(F32).T
        here = pl.ds(first, ROWS)
        s_t[:, here] = tall[...].astype(BF16)
        for x in range(4):
            pieces = [tall[pl.ds((4 * k + x) * OWN_ROWS, OWN_ROWS), :] for k in range(8)]
            s_x[pl.ds(x * FEAT_Z, FEAT_Z), here] = jnp.concatenate(pieces, axis=0).astype(BF16)

    copy("core_s", 0, s_ref, s_other, partner).start()
    turn(s_ref, 0)

    def step(m):
        q = Y_ORDER[m]
        arrived("y", q, piece(1, 0, q))
        if q < 6:
            to_next(1, q).start()
        if q >= 2:
            to_prev(1, q).start()
        q = NEXT_ORDER[m]
        got_next(0, q)
        if q < 4:
            onward(0, q).start()
        elif q >= 6:
            extra(q - 6).start()
        q = PREV_ORDER[m]
        got_prev(0, q)
        if q >= 4:
            onward(0, q).start()
        elif q < 2:
            extra(2 + q).start()

    def pass_next(q):
        got_next(1, q)
        onward(1, q).start()

    def pass_prev(q):
        got_prev(1, q)
        onward(1, q).start()

    step(0)
    step(1)
    ids_onward(0)
    arrived("y_id", 0, ids.at[OTHER0])
    ids_out(1)
    arrived("core_s", 0, s_other)
    turn(s_other, ROWS)
    step(2)
    step(3)
    pass_next(0)
    step(4)
    pass_prev(4)
    step(5)
    pass_next(1)
    step(6)
    pass_prev(5)
    step(7)
    core_send(1)
    core_send(3)
    ids_onward(1)
    pass_next(2)
    core_got(0)
    core_got(1)
    core_got(3)

    temper = jnp.exp(jnp.full((1, 1), lt_ref[0], F32))
    slope = 0.5 * temper
    shift = jnp.full((1, 1), 0.5 * of_ref[0], F32)

    def unit(a, b):
        at = pl.multiple_of(2 * b, 2)
        own = blocks[pl.ds(at, 2)].reshape(2 * ROWS, EMB)
        logit = dot(blocks[OTHER0 + a], own, NT)
        value = jnp.tanh(logit * slope + shift) * 8.0
        row = jnp.concatenate([ids[at, 0:1, :], ids[at + 1, 0:1, :]], axis=1).astype(F32)
        col = jnp.broadcast_to(ids[OTHER0 + a, 0:1, :].astype(F32), (128, ROWS)).T
        same = jnp.concatenate([col] * 4, axis=1) == row
        value = value + jnp.where(same, -8.0, 8.0)
        here = pl.ds(pl.multiple_of(a * ROWS, ROWS), ROWS)
        pair[here, pl.ds(pl.multiple_of(b * 2 * ROWS, 2 * ROWS), 2 * ROWS)] = value.astype(BF16)

    @pl.loop(0, 3)
    def _(u):
        unit(0, u + u // 2)

        @pl.when(u == 0)
        def _():
            pass_prev(6)

        @pl.when(u == 1)
        def _():
            pass_next(3)

        @pl.when(u == 2)
        def _():
            pass_prev(7)

    for q in (4, 5):
        got_next(1, q)
    for q in (2, 3):
        got_prev(1, q)
    for n in range(4):
        got_extra(n)
    for q in range(QS):
        got_onward(0, q)
    arrived("ring_id", 2, ids.at[block(0, 2)])
    core_send(2)

    @pl.loop(0, 6)
    def _(u):
        a = u // 3
        b = u - 3 * a
        unit(1 + 2 * a, b + b // 2)

    core_got(2)
    for q in range(QS):
        got_onward(1, q)
    arrived("ring_id", 5, ids.at[block(1, 2)])

    @pl.loop(0, 4)
    def _(u):
        unit(2, u)

    def own_terms(half, slot):
        rest = blocks[pl.ds(OTHER0, 4)].reshape(4 * ROWS, EMB)
        return dot(pair[:, pl.ds((2 * slot + half) * ROWS, ROWS)], rest, TN)

    def other_terms(slot):
        @pl.loop(0, 2)
        def _(n):
            cols = pl.ds(pl.multiple_of(n * HALF, HALF), HALF)
            own = blocks[pl.ds(0, 8), :, cols].reshape(8 * ROWS, HALF)
            grad[1, slot, :, cols] = dot(pair[pl.ds(slot * ROWS, ROWS), :], own, NN)

    def give(slot):
        part_out[slot] = own_terms(1, slot).astype(BF16)
        copy("part", slot, part_out.at[slot], part_in.at[slot], partner).start()

    def keep(slot):
        grad[0, slot] = own_terms(0, slot)
        arrived("part", slot, part_in.at[slot])
        grad[0, slot] += part_in[slot].astype(F32)

    def far_copy(k, q):
        return copy("far", QS * k + q, out_buf.at[k, 2, rows(q)], far_in.at[k, rows(q)], ring(k, 1 if q < 4 else 3))

    def next_copy(k, q):
        return copy("to_next", QS * k + q, out_buf.at[k, 3, rows(q)], near_in.at[k, 0, rows(q)], ring(k, 1))

    def prev_copy(k, q):
        return copy("to_prev", QS * k + q, out_buf.at[k, 1, rows(q)], near_in.at[k, 1, rows(q)], ring(k, 3))

    def extra_of(slot, q):
        if (slot, q) in ((3, 6), (3, 7), (1, 0), (1, 1)):
            return {(3, 6): 0, (3, 7): 1, (1, 0): 2, (1, 1): 3}[slot, q]
        return None

    def extra_back(n):
        return copy("y_extra", n, extra_out.at[rows(n)], extra_in.at[rows(n)], y_down)

    def send_far(k):
        for q in (0, 4, 1, 5, 2, 6, 3, 7):
            out_buf[k, 2, rows(q), :] = grad[k, 2, rows(q), :].astype(BF16)
            far_copy(k, q).start()

    def send_extra(slot):
        for q in range(QS):
            n = extra_of(slot, q)
            if n is not None:
                extra_out[rows(n), :] = grad[1, slot, rows(q), :].astype(BF16)
                extra_back(n).start()

    def send_near(k, slot, order, make):
        for q in order:
            n = extra_of(slot, q)
            if n is not None and k == 1:
                continue
            term = grad[k, slot, rows(q), :]
            if (q < 4) == (slot == 3):
                arrived("far", QS * k + q, far_in.at[k, rows(q)])
                term += far_in[k, rows(q), :].astype(F32)
            if n is not None:
                arrived("y_extra", n, extra_in.at[rows(n)])
                term += extra_in[rows(n), :].astype(F32)
            out_buf[k, slot, rows(q), :] = term.astype(BF16)
            make(k, q).start()

    def reduced(k, q):
        total = grad[k, 0, rows(q), :]
        if k == 0 or extra_of(3, q) is None:
            arrived("to_next", QS * k + q, near_in.at[k, 0, rows(q)])
            total += near_in[k, 0, rows(q), :].astype(F32)
        if k == 0 or extra_of(1, q) is None:
            arrived("to_prev", QS * k + q, near_in.at[k, 1, rows(q)])
            total += near_in[k, 1, rows(q), :].astype(F32)
        return total

    def back_copy(q):
        return copy("y_back", q, y_out.at[rows(q)], y_in.at[rows(q)], y_down)

    def send_back(order):
        for q in order:
            y_out[rows(q), :] = reduced(1, q).astype(BF16)
            back_copy(q).start()

    other_terms(2)
    send_far(1)

    @pl.loop(0, 3)
    def _(u):
        unit(u + u // 2, 2)

    give(2)
    other_terms(3)
    send_extra(3)
    send_near(1, 3, (4, 5), next_copy)
    keep(2)
    send_far(0)
    other_terms(1)
    send_extra(1)
    send_near(1, 1, (2, 3), prev_copy)
    send_near(1, 3, (0, 1, 2, 3), next_copy)
    send_near(1, 1, (4, 5, 6, 7), prev_copy)
    give(3)
    give(1)
    other_terms(0)
    keep(3)
    send_near(0, 3, (4, 5), next_copy)
    keep(1)
    send_near(0, 1, (2, 3), prev_copy)
    send_back(BACK_ORDER[:2])
    for n in range(4):
        send_near(0, 3, (n,), next_copy)
        send_near(0, 1, (n + 4,), prev_copy)
    send_near(0, 3, (6, 7), next_copy)
    send_near(0, 1, (0, 1), prev_copy)
    give(0)
    send_back(BACK_ORDER[2:4])
    keep(0)
    send_back(BACK_ORDER[4:])

    def rg_copy(q):
        return copy("rg", q, rg_theirs.at[rows(q)], rg_mine.at[pl.ds(ROWS + CHUNK * q, CHUNK)], partner)

    for q in BACK_ORDER:
        total = reduced(0, q)
        arrived("y_back", q, y_in.at[rows(q)])
        emb_grad = temper * (total + y_in[rows(q), :].astype(F32))
        scale = inv[rows(q), 0:1]
        unit_rows = raw[rows(q), :] * scale
        along = jnp.sum(unit_rows * emb_grad, axis=1, keepdims=True)
        value = ((emb_grad - unit_rows * along) * scale).astype(BF16)
        rg[rows(q), :] = value
        low, high = value[:, :HALF], value[:, HALF:]
        rg_mine[rows(q), :] = jnp.where(core == 0, low, high)
        rg_theirs[rows(q), :] = jnp.where(core == 0, high, low)
        rg_copy(q).start()

    for q in range(QS):
        arrived("rg", q, rg_mine.at[pl.ds(ROWS + CHUNK * q, CHUNK)])

    def part_of(n, d):
        at = pl.multiple_of(lax.rem((px if n else pz) + d, 4) * FEAT_Z, FEAT_Z)
        return dot((s_x if n else s_t)[pl.ds(at, FEAT_Z), :], rg_mine[:, pl.ds(256 * n, 256)], NN)

    def st_copy(n, d):
        return copy("st", 4 * n + d, st_out.at[n, d], st_in.at[n, d], ring_x(d) if n else ring_z(d))

    for d in (2, 1, 3):
        for n in range(2):
            st_out[n, d] = part_of(n, d).astype(BF16)
            st_copy(n, d).start()
    for n in range(2):
        st_sum[n] = part_of(n, 0)

    @pl.loop(0, FEAT // 256)
    def _(n):
        here = pl.ds(pl.multiple_of(n * 256, 256), 256)
        sg_ref[:, here] = dot(rg[...], w_ref[here, :], NT).astype(BF16)

    def group(n, dy, d):
        y = jnp.where(dy == 0, yh, 1 - yh)
        g = y * 4 + lax.rem(px + d, 4) if n == 0 else lax.rem(pz + d, 4) * 2 + y
        return st_sum[n, pl.ds(pl.multiple_of(g * OWN_ROWS, 8), OWN_ROWS), :]

    def stacked(value):
        return jnp.concatenate([value[:, :128], value[:, 128:]], axis=0)

    def end_copy(n, k):
        return copy("end", 8 * n + k, end_out.at[n, k], end_in.at[n, k], plane(n, k // 4, k % 4))

    for n in range(2):
        for d in (1, 3, 2):
            arrived("st", 4 * n + d, st_in.at[n, d])
        st_sum[n] += st_in[n, 1].astype(F32) + st_in[n, 2].astype(F32) + st_in[n, 3].astype(F32)
        for k in (6, 5, 7, 4, 2, 1, 3):
            end_out[n, k] = stacked(group(n, k // 4, k % 4)).astype(BF16)
            end_copy(n, k).start()

    def finished(n):
        total = stacked(group(n, 0, 0))
        for k in (1, 3, 2, 4, 5, 7, 6):
            arrived("end", 8 * n + k, end_in.at[n, k])
            total += end_in[n, k].astype(F32)
        return jnp.concatenate([total[:OWN_ROWS], total[OWN_ROWS:]], axis=1)

    p_fin = finished(0)
    q_fin = finished(1)
    both = jnp.concatenate([p_fin, q_fin], axis=1)
    first, second = both[:20], both[20:]
    theirs = jnp.where(core == 0, second, first)
    mine = jnp.where(core == 0, first, second)
    last_out[...] = jnp.concatenate([theirs, jnp.zeros((4, HALF), F32)], axis=0)
    copy("last", 0, last_out, last_in, partner).start()
    arrived("last", 0, last_in)
    got = last_in[:20, :]
    pg_ref[:, 0, :HALF] = jnp.where(core == 0, mine, got)
    pg_ref[:, 0, HALF:] = jnp.where(core == 0, got, mine)

    some = blocks.at[0]
    for q in range(QS):
        left("y", q, some.at[rows(q)])
        left("y_back", q, some.at[rows(q)])
        left("rg", q, rg_theirs.at[rows(q)])
    left("y_id", 0, ids.at[0])
    for k in range(2):
        for q in range(QS):
            if k == 0 or q < 6:
                left("ring", 3 * QS * k + q, some.at[rows(0)])
            if k == 0 or q >= 2:
                left("ring", 3 * QS * k + QS + q, some.at[rows(0)])
            left("ring", 3 * QS * k + 2 * QS + q, some.at[rows(0)])
            left("far", QS * k + q, some.at[rows(0)])
            if k == 0 or extra_of(3, q) is None:
                left("to_next", QS * k + q, some.at[rows(0)])
            if k == 0 or extra_of(1, q) is None:
                left("to_prev", QS * k + q, some.at[rows(0)])
    for n in range(6):
        left("ring_id", n, ids.at[0])
    for n in range(4):
        left("core", n, some)
        left("core_id", n, ids.at[0])
        left("part", n, some)
        left("extra", n, some.at[rows(0)])
        left("y_extra", n, some.at[rows(0)])
    left("core_s", 0, s_other)
    for n in range(2):
        for d in (1, 2, 3):
            left("st", 4 * n + d, st_out.at[n, d])
        for k in range(1, 8):
            left("end", 8 * n + k, end_out.at[n, k])
    left("last", 0, last_out)


def local(states, projection, prompt_ids, log_temper, logit_offset):
    vmem = pl.BlockSpec(memory_space=pltpu.VMEM)
    hbm = pl.BlockSpec(memory_space=pl.ANY)
    scratch = [
        ((ROWS, FEAT), BF16),
        ((FEAT, EMB), BF16),
        ((1, ROWS), jnp.int32),
        None,
        None,
        ((12, ROWS, EMB), BF16),
        ((12, 8, ROWS), jnp.int32),
        ((ROWS, EMB), F32),
        ((ROWS, 128), F32),
        ((4 * ROWS, 8 * ROWS), BF16),
        ((2, 4, ROWS, EMB), F32),
        ((2, 4, ROWS, EMB), BF16),
        ((2, ROWS, EMB), BF16),
        ((2, 2, ROWS, EMB), BF16),
        ((4 * CHUNK, EMB), BF16),
        ((4 * CHUNK, EMB), BF16),
        ((4, ROWS, EMB), BF16),
        ((4, ROWS, EMB), BF16),
        ((ROWS, EMB), BF16),
        ((ROWS, EMB), BF16),
        ((ROWS, EMB), BF16),
        ((2 * ROWS, HALF), BF16),
        ((ROWS, HALF), BF16),
        ((ROWS, FEAT), BF16),
        ((FEAT, 2 * ROWS), BF16),
        ((FEAT, 2 * ROWS), BF16),
        ((FEAT, ROWS), F32),
        ((2, 4, FEAT_Z, 256), BF16),
        ((2, 4, FEAT_Z, 256), BF16),
        ((2, FEAT_Z, 256), F32),
        ((2, 8, 2 * OWN_ROWS, 128), BF16),
        ((2, 8, 2 * OWN_ROWS, 128), BF16),
        ((24, HALF), F32),
        ((24, HALF), F32),
    ]
    state_grad, owned = pl.pallas_call(
        kernel,
        out_shape=(
            jax.ShapeDtypeStruct((ROWS, FEAT), BF16),
            jax.ShapeDtypeStruct((20, 1, EMB), F32),
        ),
        in_specs=[hbm] * 5,
        out_specs=(vmem, vmem),
        scratch_shapes=[pltpu.VMEM(*what) if what else pltpu.SMEM((1,), F32) for what in scratch]
        + [pltpu.SemaphoreType.DMA((6,))]
        + [pltpu.SemaphoreType.DMA((Sems.total(),)), pltpu.SemaphoreType.DMA((Sems.total(),))],
        compiler_params=pltpu.CompilerParams(
            collective_id=0, has_side_effects=True, vmem_limit_bytes=60 * 2**20
        ),
        name="contrast",
    )(states[0], projection[0], prompt_ids.reshape(1, ROWS), log_temper, logit_offset)
    return state_grad[None], owned.reshape(1, 20, EMB)


def solution(mesh):
    return jax.shard_map(
        local,
        mesh=mesh,
        in_specs=(P("tower", "batch", None), P("tower", None, None), P("batch"), P(), P()),
        out_specs=(P("tower", "batch", None), P("tower", "batch", None)),
        check_vma=False,
    )
```

```python
import jax
import jax.numpy as jnp
from jax import lax
from jax.experimental import pallas as pl
from jax.experimental.pallas import tpu as pltpu
from jax.sharding import PartitionSpec as P

EPSILON = 1e-06
MESH = pl.DeviceIdType.MESH
F32, BF16 = jnp.float32, jnp.bfloat16
NT = (((1,), (1,)), ((), ()))
TN = (((0,), (0,)), ((), ()))
NN = (((1,), (0,)), ((), ()))

ROWS = 256
EMB = 1024
FEAT = 1280
CHUNK = 32
QS = ROWS // CHUNK
HALF = EMB // 2
FEAT_Z = FEAT // 4
OWN_ROWS = 40
OTHER0 = 8

Y_ORDER = (0, 4, 1, 5, 2, 6, 3, 7)
NEXT_ORDER = (2, 3, 0, 1, 6, 7, 4, 5)
PREV_ORDER = (6, 7, 4, 5, 2, 3, 0, 1)
EXTRA = (2, 6, 3, 7)
BACK_ORDER = (4, 5, 6, 0, 7, 1, 2, 3)


class Sems:
    sizes = dict(
        y=QS, y_id=1, ring=2 * 3 * QS, ring_id=2 * 3, core=16, core_id=4, core_s=1, extra=4,
        part=4, far=2 * QS, to_next=2 * QS, to_prev=2 * QS, y_extra=4, y_back=QS,
        rg=QS, st=8, end=16, last=1,
    )

    @classmethod
    def at(cls, name, index=0):
        base = 0
        for key, size in cls.sizes.items():
            if key == name:
                return base + index
            base += size
        raise KeyError(name)

    @classmethod
    def total(cls):
        return sum(cls.sizes.values())


def dot(a, b, dims):
    return lax.dot_general(a, b, dims, preferred_element_type=F32)


def kernel(
    s_hbm, w_hbm, id_hbm, lt_hbm, of_hbm, sg_ref, pg_ref,
    s_ref, w_ref, id_ref, lt_ref, of_ref, blocks, ids, raw, inv, pair, grad, out_buf, far_in, near_in, extra_out, extra_in, part_out, part_in, y_out, y_in,
    rg, rg_mine, rg_theirs, s_other, s_t, s_x, tall, st_out, st_in, st_sum, end_out, end_in, last_out, last_in,
    lsem, ssem, rsem,
):
    tower = lax.axis_index("tower")
    batch = lax.axis_index("batch")
    core = lax.rem(batch, 2)
    px = lax.rem(batch // 2, 4)
    yh = lax.rem(batch // 8, 2)
    pz = batch // 16
    other = 1 - tower

    def dev(t, z, y, x, c):
        return (t, ((z * 2 + y) * 4 + x) * 2 + c)

    def ring_x(d):
        return dev(tower, pz, yh, lax.rem(px + d, 4), core)

    def ring_z(d):
        return dev(tower, lax.rem(pz + d, 4), yh, px, core)

    def ring(k, d):
        r = tower if k == 0 else other
        return dev(tower, lax.rem(pz + r * d, 4), yh, lax.rem(px + (1 - r) * d, 4), core)

    partner = dev(tower, pz, yh, px, 1 - core)
    y_up = dev(other, pz, jnp.where(tower == 1, 1 - yh, yh), px, core)
    y_down = dev(other, pz, jnp.where(tower == 0, 1 - yh, yh), px, core)

    def plane(n, dy, d):
        x = lax.rem(px + d, 4) if n == 0 else px
        z = pz if n == 0 else lax.rem(pz + d, 4)
        return dev(tower, z, 1 - yh if dy else yh, x, core)

    def block(k, slot):
        return 2 * slot if k == 0 else OTHER0 + slot

    def copy(name, index, src, dst, where):
        n = Sems.at(name) + index
        return pltpu.make_async_remote_copy(
            src_ref=src, dst_ref=dst, send_sem=ssem.at[n], recv_sem=rsem.at[n],
            device_id=where, device_id_type=MESH,
        )

    def arrived(name, index, ref):
        copy(name, index, ref, ref, partner).wait_recv()

    def left(name, index, ref):
        copy(name, index, ref, ref, partner).wait_send()

    def rows(q):
        return pl.ds(CHUNK * q, CHUNK)

    def piece(k, slot, q):
        return blocks.at[block(k, slot), rows(q)]

    barrier = pltpu.get_barrier_semaphore()
    near = [partner, y_up, y_down, plane(0, 1, 0)]
    near += [plane(n, dy, d) for n in range(2) for dy in range(2) for d in (1, 2, 3)]
    for where in near:
        pl.semaphore_signal(barrier, inc=1, device_id=where, device_id_type=MESH)

    def halves(n):
        return pl.ds(n * HALF, HALF)

    loads = [pltpu.make_async_copy(s_hbm, s_ref, lsem.at[0])]
    loads += [pltpu.make_async_copy(w_hbm.at[:, halves(n)], w_ref.at[:, halves(n)], lsem.at[1 + n]) for n in range(2)]
    small = [(id_hbm, id_ref), (lt_hbm, lt_ref), (of_hbm, of_ref)]
    small = [pltpu.make_async_copy(src, dst, lsem.at[3 + n]) for n, (src, dst) in enumerate(small)]
    for load in loads + small:
        load.start()
    small[0].wait()
    ids[0] = jnp.broadcast_to(id_ref[...], (8, ROWS))
    small[1].wait()
    small[2].wait()
    loads[0].wait()
    for n in range(2):
        loads[1 + n].wait()
        raw[:, halves(n)] = dot(s_ref[...], w_ref[:, halves(n)], NN)

    pl.semaphore_wait(barrier, len(near))

    def to_next(k, q):
        return copy("ring", 3 * QS * k + q, piece(k, 0, q), piece(k, 1, q), ring(k, 1))

    def to_prev(k, q):
        return copy("ring", 3 * QS * k + QS + q, piece(k, 0, q), piece(k, 3, q), ring(k, 3))

    def onward(k, q):
        slot = 1 if q < QS // 2 else 3
        return copy("ring", 3 * QS * k + 2 * QS + q, piece(k, slot, q), piece(k, 2, q), ring(k, slot))

    def got_next(k, q):
        arrived("ring", 3 * QS * k + q, piece(k, 1, q))

    def got_prev(k, q):
        arrived("ring", 3 * QS * k + QS + q, piece(k, 3, q))

    def got_onward(k, q):
        arrived("ring", 3 * QS * k + 2 * QS + q, piece(k, 2, q))

    def extra(n):
        return copy("extra", n, piece(0, 2, EXTRA[n]), piece(1, 2, EXTRA[n]), y_up)

    def ids_out(k):
        copy("ring_id", 3 * k, ids.at[block(k, 0)], ids.at[block(k, 1)], ring(k, 1)).start()
        copy("ring_id", 3 * k + 1, ids.at[block(k, 0)], ids.at[block(k, 3)], ring(k, 3)).start()

    def ids_onward(k):
        arrived("ring_id", 3 * k, ids.at[block(k, 1)])
        copy("ring_id", 3 * k + 2, ids.at[block(k, 1)], ids.at[block(k, 2)], ring(k, 1)).start()
        arrived("ring_id", 3 * k + 1, ids.at[block(k, 3)])

    def core_copy(slot, n):
        there = pl.ds(2 * CHUNK * n, 2 * CHUNK)
        return copy("core", 4 * slot + n, blocks.at[2 * slot, there], blocks.at[2 * slot + 1, there], partner)

    def core_send(slot, *pieces):
        for n in pieces:
            core_copy(slot, n).start()

    def core_got(slot):
        for n in range(4):
            arrived("core", 4 * slot + n, blocks.at[2 * slot + 1, pl.ds(2 * CHUNK * n, 2 * CHUNK)])
        arrived("core_id", slot, ids.at[2 * slot + 1])

    def core_ids(slot):
        copy("core_id", slot, ids.at[2 * slot], ids.at[2 * slot + 1], partner).start()

    copy("y_id", 0, ids.at[0], ids.at[OTHER0], y_up).start()
    ids_out(0)
    def own_rows(q):
        part = raw[rows(q), :]
        length = jnp.sqrt(jnp.sum(part * part, axis=1, keepdims=True) + EPSILON)
        scale = 1.0 / length
        inv[rows(q), :] = jnp.broadcast_to(scale, (CHUNK, 128))
        blocks[0, rows(q)] = (part * scale).astype(BF16)

    def y_send(q):
        copy("y", q, piece(0, 0, q), piece(1, 0, q), y_up).start()

    for q in (0, 1):
        own_rows(q)
        y_send(q)
        own_rows(q + 2)
        to_next(0, q + 2).start()
        own_rows(q + 4)
        y_send(q + 4)
        own_rows(q + 6)
        to_prev(0, q + 6).start()
    for q in EXTRA:
        y_send(q)
    for q in (0, 1, 6):
        to_next(0, q).start()
    for q in (4, 5, 2):
        to_prev(0, q).start()
    core_send(0, 0, 1, 2, 3)
    core_ids(0)

    def turn(states, first):
        tall[...] = states[...].astype(F32).T
        here = pl.ds(first, ROWS)
        s_t[:, here] = tall[...].astype(BF16)
        for x in range(4):
            pieces = [tall[pl.ds((4 * k + x) * OWN_ROWS, OWN_ROWS), :] for k in range(8)]
            s_x[pl.ds(x * FEAT_Z, FEAT_Z), here] = jnp.concatenate(pieces, axis=0).astype(BF16)

    copy("core_s", 0, s_ref, s_other, partner).start()
    turn(s_ref, 0)

    temper = jnp.exp(jnp.full((1, 1), lt_ref[0], F32))
    slope = 0.5 * temper
    shift = jnp.full((1, 1), 0.5 * of_ref[0], F32)

    def unit(a, b):
        at = 2 * b
        own = blocks[pl.ds(at, 2)].reshape(2 * ROWS, EMB)
        logit = dot(blocks[OTHER0 + a], own, NT)
        value = jnp.tanh(logit * slope + shift) * 8.0
        row = jnp.concatenate([ids[at, 0:1, :], ids[at + 1, 0:1, :]], axis=1).astype(F32)
        col = jnp.broadcast_to(ids[OTHER0 + a, 0:1, :].astype(F32), (128, ROWS)).T
        same = jnp.concatenate([col] * 4, axis=1) == row
        value = value + jnp.where(same, -8.0, 8.0)
        pair[pl.ds(a * ROWS, ROWS), pl.ds(b * 2 * ROWS, 2 * ROWS)] = value.astype(BF16)

    def y_got(m):
        q = Y_ORDER[m]
        arrived("y", q, piece(1, 0, q))
        to_next(1, q).start()
        to_prev(1, q).start()

    def own_on(m):
        for q, got in ((NEXT_ORDER[m], got_next), (PREV_ORDER[m], got_prev)):
            got(0, q)
            onward(0, q).start()

    def other_on(q):
        (got_next if q < 4 else got_prev)(1, q)
        onward(1, q).start()

    def far_on(n):
        got_onward(0, EXTRA[n])
        extra(n).start()

    y_got(0)
    own_on(0)
    y_got(1)
    own_on(1)
    ids_onward(0)
    core_ids(1)
    core_ids(3)
    arrived("y_id", 0, ids.at[OTHER0])
    ids_out(1)
    arrived("core_s", 0, s_other)
    turn(s_other, ROWS)
    y_got(2)
    own_on(2)
    y_got(3)
    own_on(3)
    for q in (7, 4, 5):
        to_next(0, q).start()
    for q in (3, 0, 1):
        to_prev(0, q).start()
    core_send(1, 0, 1)
    core_send(3, 2, 3)
    other_on(0)
    y_got(4)
    other_on(4)
    y_got(5)
    far_on(0)
    far_on(1)
    ids_onward(1)
    other_on(1)
    y_got(6)
    far_on(2)
    far_on(3)
    core_send(2, 1, 3)
    other_on(5)
    y_got(7)
    arrived("ring_id", 2, ids.at[block(0, 2)])
    core_ids(2)
    core_got(0)
    unit(0, 0)
    for q in (0, 4):
        got_onward(0, q)
    for q in (1, 5):
        got_onward(0, q)
    core_send(2, 0, 2)
    got_next(0, 6)
    got_next(0, 7)
    core_send(1, 3)
    got_prev(0, 2)
    got_prev(0, 3)
    core_send(3, 1)
    core_got(2)
    unit(0, 2)
    for q in (4, 5):
        got_next(0, q)
    core_send(1, 2)
    for q in (0, 1):
        got_prev(0, q)
    core_send(3, 0)
    for q in (0, 4, 1, 5):
        got_onward(1, q)
    for n in range(4):
        arrived("extra", n, piece(1, 2, EXTRA[n]))
    arrived("ring_id", 5, ids.at[block(1, 2)])
    unit(2, 0)
    unit(2, 2)
    core_got(1)
    unit(2, 1)
    core_got(3)
    unit(2, 3)

    def own_terms(half, slot):
        rest = blocks[pl.ds(OTHER0, 4)].reshape(4 * ROWS, EMB)
        return dot(pair[:, pl.ds((2 * slot + half) * ROWS, ROWS)], rest, TN)

    def other_terms(slot):
        for n in range(2):
            cols = halves(n)
            own = blocks[pl.ds(0, 8), :, cols].reshape(8 * ROWS, HALF)
            value = dot(pair[pl.ds(slot * ROWS, ROWS), :], own, NN)
            if slot == 2:
                out_buf[1, 2, :, cols] = value.astype(BF16)
            else:
                grad[1, slot, :, cols] = value

    def give(slot):
        part_out[slot] = own_terms(1, slot).astype(BF16)
        copy("part", slot, part_out.at[slot], part_in.at[slot], partner).start()

    def keep(slot):
        arrived("part", slot, part_in.at[slot])
        value = own_terms(0, slot) + part_in[slot].astype(F32)
        if slot == 2:
            out_buf[0, 2] = value.astype(BF16)
        else:
            grad[0, slot] = value

    def far_copy(k, q):
        return copy("far", QS * k + q, out_buf.at[k, 2, rows(q)], far_in.at[k, rows(q)], ring(k, 1 if q < 4 else 3))

    def next_copy(k, q):
        return copy("to_next", QS * k + q, out_buf.at[k, 3, rows(q)], near_in.at[k, 0, rows(q)], ring(k, 1))

    def prev_copy(k, q):
        return copy("to_prev", QS * k + q, out_buf.at[k, 1, rows(q)], near_in.at[k, 1, rows(q)], ring(k, 3))

    def extra_of(slot, q):
        if (slot, q) in ((3, 6), (3, 7), (1, 0), (1, 1)):
            return {(3, 6): 0, (3, 7): 1, (1, 0): 2, (1, 1): 3}[slot, q]
        return None

    def extra_back(n):
        return copy("y_extra", n, extra_out.at[rows(n)], extra_in.at[rows(n)], y_down)

    def send_far(k):
        for q in (0, 4, 1, 5, 2, 6, 3, 7):
            far_copy(k, q).start()

    def send_extra(slot):
        for q in range(QS):
            n = extra_of(slot, q)
            if n is not None:
                extra_out[rows(n), :] = grad[1, slot, rows(q), :].astype(BF16)
                extra_back(n).start()

    def send_near(k, slot, order, make):
        for q in order:
            n = extra_of(slot, q)
            if n is not None and k == 1:
                continue
            term = grad[k, slot, rows(q), :]
            if (q < 4) == (slot == 3):
                arrived("far", QS * k + q, far_in.at[k, rows(q)])
                term += far_in[k, rows(q), :].astype(F32)
            if n is not None:
                arrived("y_extra", n, extra_in.at[rows(n)])
                term += extra_in[rows(n), :].astype(F32)
            out_buf[k, slot, rows(q), :] = term.astype(BF16)
            make(k, q).start()

    def reduced(k, q):
        total = grad[k, 0, rows(q), :]
        if k == 0 or extra_of(3, q) is None:
            arrived("to_next", QS * k + q, near_in.at[k, 0, rows(q)])
            total += near_in[k, 0, rows(q), :].astype(F32)
        if k == 0 or extra_of(1, q) is None:
            arrived("to_prev", QS * k + q, near_in.at[k, 1, rows(q)])
            total += near_in[k, 1, rows(q), :].astype(F32)
        return total

    def back_copy(q):
        return copy("y_back", q, y_out.at[rows(q)], y_in.at[rows(q)], y_down)

    def send_back(order):
        for q in order:
            y_out[rows(q), :] = reduced(1, q).astype(BF16)
            back_copy(q).start()

    other_terms(2)
    send_far(1)
    for q in (2, 6, 3, 7):
        got_next(1, q)
    for q in (5, 4):
        got_next(1, q)
    for q in (0, 1, 2, 3, 6, 7):
        got_prev(1, q)
    unit(3, 2)
    unit(1, 2)
    give(2)
    unit(3, 0)
    unit(3, 1)
    unit(3, 3)
    other_terms(3)
    send_extra(3)
    send_near(1, 3, (4, 5), next_copy)
    keep(2)
    send_far(0)
    unit(1, 0)
    unit(1, 1)
    unit(1, 3)
    other_terms(1)
    send_extra(1)
    send_near(1, 1, (2, 3), prev_copy)
    send_near(1, 3, (0, 1, 2, 3), next_copy)
    send_near(1, 1, (4, 5, 6, 7), prev_copy)
    unit(0, 1)
    unit(0, 3)
    give(3)
    give(1)
    other_terms(0)
    keep(3)
    send_near(0, 3, (4, 5), next_copy)
    keep(1)
    send_near(0, 1, (2, 3), prev_copy)
    send_back(BACK_ORDER[:2])
    for n in range(4):
        send_near(0, 3, (n,), next_copy)
        send_near(0, 1, (n + 4,), prev_copy)
    send_near(0, 3, (6, 7), next_copy)
    send_near(0, 1, (0, 1), prev_copy)
    give(0)
    send_back(BACK_ORDER[2:6])
    keep(0)
    send_back(BACK_ORDER[6:])

    def rg_copy(q):
        return copy("rg", q, rg_theirs.at[rows(q)], rg_mine.at[pl.ds(ROWS + CHUNK * q, CHUNK)], partner)

    for q in BACK_ORDER:
        total = reduced(0, q)
        arrived("y_back", q, y_in.at[rows(q)])
        emb_grad = temper * (total + y_in[rows(q), :].astype(F32))
        scale = inv[rows(q), 0:1]
        unit_rows = raw[rows(q), :] * scale
        along = jnp.sum(unit_rows * emb_grad, axis=1, keepdims=True)
        value = ((emb_grad - unit_rows * along) * scale).astype(BF16)
        rg[rows(q), :] = value
        low, high = value[:, :HALF], value[:, HALF:]
        rg_mine[rows(q), :] = jnp.where(core == 0, low, high)
        rg_theirs[rows(q), :] = jnp.where(core == 0, high, low)
        rg_copy(q).start()

    for q in range(QS):
        arrived("rg", q, rg_mine.at[pl.ds(ROWS + CHUNK * q, CHUNK)])

    def part_of(n, d):
        at = pl.multiple_of(lax.rem((px if n else pz) + d, 4) * FEAT_Z, FEAT_Z)
        return dot((s_x if n else s_t)[pl.ds(at, FEAT_Z), :], rg_mine[:, pl.ds(256 * n, 256)], NN)

    def st_copy(n, d):
        return copy("st", 4 * n + d, st_out.at[n, d], st_in.at[n, d], ring_x(d) if n else ring_z(d))

    for d in (2, 1, 3):
        for n in range(2):
            st_out[n, d] = part_of(n, d).astype(BF16)
            st_copy(n, d).start()
    for n in range(2):
        st_sum[n] = part_of(n, 0)

    @pl.loop(0, FEAT // 256)
    def _(n):
        here = pl.ds(pl.multiple_of(n * 256, 256), 256)
        sg_ref[:, here] = dot(rg[...], w_ref[here, :], NT).astype(BF16)

    def group(n, dy, d):
        y = jnp.where(dy == 0, yh, 1 - yh)
        g = y * 4 + lax.rem(px + d, 4) if n == 0 else lax.rem(pz + d, 4) * 2 + y
        return st_sum[n, pl.ds(pl.multiple_of(g * OWN_ROWS, 8), OWN_ROWS), :]

    def stacked(value):
        return jnp.concatenate([value[:, :128], value[:, 128:]], axis=0)

    def end_copy(n, k):
        return copy("end", 8 * n + k, end_out.at[n, k], end_in.at[n, k], plane(n, k // 4, k % 4))

    for n in range(2):
        for d in (1, 3, 2):
            arrived("st", 4 * n + d, st_in.at[n, d])
        st_sum[n] += st_in[n, 1].astype(F32) + st_in[n, 2].astype(F32) + st_in[n, 3].astype(F32)
        for k in (6, 5, 7, 4, 2, 1, 3):
            end_out[n, k] = stacked(group(n, k // 4, k % 4)).astype(BF16)
            end_copy(n, k).start()

    def finished(n):
        total = stacked(group(n, 0, 0))
        for k in (1, 3, 2, 4, 5, 7, 6):
            arrived("end", 8 * n + k, end_in.at[n, k])
            total += end_in[n, k].astype(F32)
        return jnp.concatenate([total[:OWN_ROWS], total[OWN_ROWS:]], axis=1)

    p_fin = finished(0)
    q_fin = finished(1)
    both = jnp.concatenate([p_fin, q_fin], axis=1)
    first, second = both[:20], both[20:]
    theirs = jnp.where(core == 0, second, first)
    mine = jnp.where(core == 0, first, second)
    last_out[...] = jnp.concatenate([theirs, jnp.zeros((4, HALF), F32)], axis=0)
    copy("last", 0, last_out, last_in, partner).start()
    arrived("last", 0, last_in)
    got = last_in[:20, :]
    pg_ref[:, 0, :HALF] = jnp.where(core == 0, mine, got)
    pg_ref[:, 0, HALF:] = jnp.where(core == 0, got, mine)

    some = blocks.at[0]
    for q in range(QS):
        left("y", q, some.at[rows(q)])
        left("y_back", q, some.at[rows(q)])
        left("rg", q, rg_theirs.at[rows(q)])
    left("y_id", 0, ids.at[0])
    for k in range(2):
        for q in range(QS):
            left("ring", 3 * QS * k + q, some.at[rows(0)])
            left("ring", 3 * QS * k + QS + q, some.at[rows(0)])
            if k == 0 or q not in EXTRA:
                left("ring", 3 * QS * k + 2 * QS + q, some.at[rows(0)])
            left("far", QS * k + q, some.at[rows(0)])
            if k == 0 or extra_of(3, q) is None:
                left("to_next", QS * k + q, some.at[rows(0)])
            if k == 0 or extra_of(1, q) is None:
                left("to_prev", QS * k + q, some.at[rows(0)])
    for n in range(6):
        left("ring_id", n, ids.at[0])
    for n in range(4):
        for m in range(4):
            left("core", 4 * n + m, some.at[pl.ds(0, 2 * CHUNK)])
        left("core_id", n, ids.at[0])
        left("part", n, some)
        left("extra", n, some.at[rows(0)])
        left("y_extra", n, some.at[rows(0)])
    left("core_s", 0, s_other)
    for n in range(2):
        for d in (1, 2, 3):
            left("st", 4 * n + d, st_out.at[n, d])
        for k in range(1, 8):
            left("end", 8 * n + k, end_out.at[n, k])
    left("last", 0, last_out)


def local(states, projection, prompt_ids, log_temper, logit_offset):
    vmem = pl.BlockSpec(memory_space=pltpu.VMEM)
    hbm = pl.BlockSpec(memory_space=pl.ANY)
    scratch = [
        ((ROWS, FEAT), BF16),
        ((FEAT, EMB), BF16),
        ((1, ROWS), jnp.int32),
        None,
        None,
        ((12, ROWS, EMB), BF16),
        ((12, 8, ROWS), jnp.int32),
        ((ROWS, EMB), F32),
        ((ROWS, 128), F32),
        ((4 * ROWS, 8 * ROWS), BF16),
        ((2, 4, ROWS, EMB), F32),
        ((2, 4, ROWS, EMB), BF16),
        ((2, ROWS, EMB), BF16),
        ((2, 2, ROWS, EMB), BF16),
        ((4 * CHUNK, EMB), BF16),
        ((4 * CHUNK, EMB), BF16),
        ((4, ROWS, EMB), BF16),
        ((4, ROWS, EMB), BF16),
        ((ROWS, EMB), BF16),
        ((ROWS, EMB), BF16),
        ((ROWS, EMB), BF16),
        ((2 * ROWS, HALF), BF16),
        ((ROWS, HALF), BF16),
        ((ROWS, FEAT), BF16),
        ((FEAT, 2 * ROWS), BF16),
        ((FEAT, 2 * ROWS), BF16),
        ((FEAT, ROWS), F32),
        ((2, 4, FEAT_Z, 256), BF16),
        ((2, 4, FEAT_Z, 256), BF16),
        ((2, FEAT_Z, 256), F32),
        ((2, 8, 2 * OWN_ROWS, 128), BF16),
        ((2, 8, 2 * OWN_ROWS, 128), BF16),
        ((24, HALF), F32),
        ((24, HALF), F32),
    ]
    state_grad, owned = pl.pallas_call(
        kernel,
        out_shape=(
            jax.ShapeDtypeStruct((ROWS, FEAT), BF16),
            jax.ShapeDtypeStruct((20, 1, EMB), F32),
        ),
        in_specs=[hbm] * 5,
        out_specs=(vmem, vmem),
        scratch_shapes=[pltpu.VMEM(*what) if what else pltpu.SMEM((1,), F32) for what in scratch]
        + [pltpu.SemaphoreType.DMA((6,))]
        + [pltpu.SemaphoreType.DMA((Sems.total(),)), pltpu.SemaphoreType.DMA((Sems.total(),))],
        compiler_params=pltpu.CompilerParams(
            collective_id=0, has_side_effects=True, vmem_limit_bytes=60 * 2**20
        ),
        name="contrast",
    )(states[0], projection[0], prompt_ids.reshape(1, ROWS), log_temper, logit_offset)
    return state_grad[None], owned.reshape(1, 20, EMB)


def solution(mesh):
    return jax.shard_map(
        local,
        mesh=mesh,
        in_specs=(P("tower", "batch", None), P("tower", None, None), P("batch"), P(), P()),
        out_specs=(P("tower", "batch", None), P("tower", "batch", None)),
        check_vma=False,
    )
```

```python
import jax
import jax.numpy as jnp
from jax import lax
from jax.experimental import pallas as pl
from jax.experimental.pallas import tpu as pltpu
from jax.sharding import PartitionSpec as P

EPSILON = 1e-06
MESH = pl.DeviceIdType.MESH
F32, BF16 = jnp.float32, jnp.bfloat16
NT = (((1,), (1,)), ((), ()))
TN = (((0,), (0,)), ((), ()))
NN = (((1,), (0,)), ((), ()))

ROWS = 256
EMB = 1024
FEAT = 1280
CHUNK = 32
QS = ROWS // CHUNK
HALF = EMB // 2
QUARTERS = 4
FEAT_Z = FEAT // 4
OWN_ROWS = 40
OTHER0 = 8

Y_ORDER = (0, 4, 1, 5, 2, 6, 3, 7)
NEXT_ORDER = (2, 3, 0, 1, 6, 7, 4, 5)
PREV_ORDER = (6, 7, 4, 5, 2, 3, 0, 1)
EXTRA = (2, 6, 3, 7)
BACK_ORDER = (4, 5, 6, 0, 7, 1, 2, 3)


class Sems:
    sizes = dict(
        y=QS, y_id=1, ring=2 * 3 * QS, ring_id=2 * 3, core=16, core_id=4, core_s=1, extra=4,
        part=4, far=2 * QS, to_next=2 * QS, to_prev=2 * QS, y_extra=4, y_back=QS,
        rg=QS, st=8, end=16, last=1,
    )

    @classmethod
    def at(cls, name, index=0):
        base = 0
        for key, size in cls.sizes.items():
            if key == name:
                return base + index
            base += size
        raise KeyError(name)

    @classmethod
    def total(cls):
        return sum(cls.sizes.values())


def dot(a, b, dims):
    return lax.dot_general(a, b, dims, preferred_element_type=F32)


def kernel(
    s_hbm, w_hbm, id_hbm, lt_hbm, of_hbm, sg_hbm, pg_ref,
    s_ref, w_ref, cols, sg_ref, id_ref, lt_ref, of_ref, blocks, ids, raw, inv, pair, grad, out_buf, far_in, near_in, extra_out, extra_in, part_out, part_in, y_out, y_in,
    rg, rg_mine, rg_theirs, s_other, s_t, s_x, tall, st_out, st_in, st_sum, end_out, end_in, last_out, last_in,
    lsem, ssem, rsem,
):
    tower = lax.axis_index("tower")
    batch = lax.axis_index("batch")
    core = lax.rem(batch, 2)
    px = lax.rem(batch // 2, 4)
    yh = lax.rem(batch // 8, 2)
    pz = batch // 16
    other = 1 - tower

    def dev(t, z, y, x, c):
        return (t, ((z * 2 + y) * 4 + x) * 2 + c)

    def ring_x(d):
        return dev(tower, pz, yh, lax.rem(px + d, 4), core)

    def ring_z(d):
        return dev(tower, lax.rem(pz + d, 4), yh, px, core)

    def ring(k, d):
        r = tower if k == 0 else other
        return dev(tower, lax.rem(pz + r * d, 4), yh, lax.rem(px + (1 - r) * d, 4), core)

    partner = dev(tower, pz, yh, px, 1 - core)
    y_up = dev(other, pz, jnp.where(tower == 1, 1 - yh, yh), px, core)
    y_down = dev(other, pz, jnp.where(tower == 0, 1 - yh, yh), px, core)

    def plane(n, dy, d):
        x = lax.rem(px + d, 4) if n == 0 else px
        z = pz if n == 0 else lax.rem(pz + d, 4)
        return dev(tower, z, 1 - yh if dy else yh, x, core)

    def block(k, slot):
        return 2 * slot if k == 0 else OTHER0 + slot

    def copy(name, index, src, dst, where):
        n = Sems.at(name) + index
        return pltpu.make_async_remote_copy(
            src_ref=src, dst_ref=dst, send_sem=ssem.at[n], recv_sem=rsem.at[n],
            device_id=where, device_id_type=MESH,
        )

    def arrived(name, index, ref):
        copy(name, index, ref, ref, partner).wait_recv()

    def left(name, index, ref):
        copy(name, index, ref, ref, partner).wait_send()

    def rows(q):
        return pl.ds(CHUNK * q, CHUNK)

    def piece(k, slot, q):
        return blocks.at[block(k, slot), rows(q)]

    barrier = pltpu.get_barrier_semaphore()
    near = [partner, y_up, y_down, plane(0, 1, 0)]
    near += [plane(n, dy, d) for n in range(2) for dy in range(2) for d in (1, 2, 3)]
    for where in near:
        pl.semaphore_signal(barrier, inc=1, device_id=where, device_id_type=MESH)

    def halves(n):
        return pl.ds(n * HALF, HALF)

    def quarter(n):
        return pl.ds(n * (EMB // QUARTERS), EMB // QUARTERS)

    loads = [pltpu.make_async_copy(s_hbm, s_ref, lsem.at[0])]
    loads += [pltpu.make_async_copy(w_hbm.at[:, quarter(n)], w_ref.at[:, quarter(n)], lsem.at[1 + n]) for n in range(QUARTERS)]
    small = [(id_hbm, id_ref), (lt_hbm, lt_ref), (of_hbm, of_ref)]
    small = [pltpu.make_async_copy(src, dst, lsem.at[1 + QUARTERS + n]) for n, (src, dst) in enumerate(small)]
    for load in loads + small:
        load.start()
    small[0].wait()
    ids[0] = jnp.broadcast_to(id_ref[...], (8, ROWS))
    small[1].wait()
    small[2].wait()
    loads[0].wait()
    for n in range(QUARTERS):
        loads[1 + n].wait()
        raw[:, quarter(n)] = dot(s_ref[...], w_ref[:, quarter(n)], NN)

    pl.semaphore_wait(barrier, len(near))

    def to_next(k, q):
        return copy("ring", 3 * QS * k + q, piece(k, 0, q), piece(k, 1, q), ring(k, 1))

    def to_prev(k, q):
        return copy("ring", 3 * QS * k + QS + q, piece(k, 0, q), piece(k, 3, q), ring(k, 3))

    def onward(k, q):
        slot = 1 if q < QS // 2 else 3
        return copy("ring", 3 * QS * k + 2 * QS + q, piece(k, slot, q), piece(k, 2, q), ring(k, slot))

    def got_next(k, q):
        arrived("ring", 3 * QS * k + q, piece(k, 1, q))

    def got_prev(k, q):
        arrived("ring", 3 * QS * k + QS + q, piece(k, 3, q))

    def got_onward(k, q):
        arrived("ring", 3 * QS * k + 2 * QS + q, piece(k, 2, q))

    def extra(n):
        return copy("extra", n, piece(0, 2, EXTRA[n]), piece(1, 2, EXTRA[n]), y_up)

    def ids_out(k):
        copy("ring_id", 3 * k, ids.at[block(k, 0)], ids.at[block(k, 1)], ring(k, 1)).start()
        copy("ring_id", 3 * k + 1, ids.at[block(k, 0)], ids.at[block(k, 3)], ring(k, 3)).start()

    def ids_onward(k):
        arrived("ring_id", 3 * k, ids.at[block(k, 1)])
        copy("ring_id", 3 * k + 2, ids.at[block(k, 1)], ids.at[block(k, 2)], ring(k, 1)).start()
        arrived("ring_id", 3 * k + 1, ids.at[block(k, 3)])

    def core_copy(slot, n):
        there = pl.ds(2 * CHUNK * n, 2 * CHUNK)
        return copy("core", 4 * slot + n, blocks.at[2 * slot, there], blocks.at[2 * slot + 1, there], partner)

    def core_send(slot, *pieces):
        for n in pieces:
            core_copy(slot, n).start()

    def core_got(slot, *pieces):
        for n in pieces:
            arrived("core", 4 * slot + n, blocks.at[2 * slot + 1, pl.ds(2 * CHUNK * n, 2 * CHUNK)])

    def core_ids_got(slot):
        arrived("core_id", slot, ids.at[2 * slot + 1])

    def core_ids(slot):
        copy("core_id", slot, ids.at[2 * slot], ids.at[2 * slot + 1], partner).start()

    copy("y_id", 0, ids.at[0], ids.at[OTHER0], y_up).start()
    ids_out(0)
    def own_rows(q):
        part = raw[rows(q), :]
        length = jnp.sqrt(jnp.sum(part * part, axis=1, keepdims=True) + EPSILON)
        scale = 1.0 / length
        inv[rows(q), :] = jnp.broadcast_to(scale, (CHUNK, 128))
        blocks[0, rows(q)] = (part * scale).astype(BF16)

    def y_send(q):
        copy("y", q, piece(0, 0, q), piece(1, 0, q), y_up).start()

    for q in (0, 1):
        own_rows(q)
        y_send(q)
        own_rows(q + 2)
        to_next(0, q + 2).start()
        own_rows(q + 4)
        y_send(q + 4)
        own_rows(q + 6)
        to_prev(0, q + 6).start()
    for q in EXTRA:
        y_send(q)
    for q in (0, 1, 6):
        to_next(0, q).start()
    for q in (4, 5, 2):
        to_prev(0, q).start()
    core_send(0, 0, 1, 2, 3)
    core_ids(0)

    def turn(states, first):
        tall[...] = states[...].astype(F32).T
        here = pl.ds(first, ROWS)
        s_t[:, here] = tall[...].astype(BF16)
        for x in range(4):
            pieces = [tall[pl.ds((4 * k + x) * OWN_ROWS, OWN_ROWS), :] for k in range(8)]
            s_x[pl.ds(x * FEAT_Z, FEAT_Z), here] = jnp.concatenate(pieces, axis=0).astype(BF16)

    copy("core_s", 0, s_ref, s_other, partner).start()
    turn(s_ref, 0)

    temper = jnp.exp(jnp.full((1, 1), lt_ref[0], F32))
    slope = 0.5 * temper
    shift = jnp.full((1, 1), 0.5 * of_ref[0], F32)

    def id_columns(slot):
        cols[slot] = jnp.broadcast_to(ids[OTHER0 + slot, 0:1, :].astype(F32), (128, ROWS)).T

    other_rows = {
        "0": [(0, 0, 256)],
        "2": [(2, 0, 256)],
        "early": [(1, 0, 64), (1, 128, 64), (3, 0, 64), (3, 128, 64)],
        "late": [(1, 64, 64), (1, 192, 64), (3, 64, 64), (3, 192, 64)],
    }
    own_rows_of = {
        "0": [(0, 0, 0, 256), (0, 1, 0, 256)],
        "2": [(2, 0, 0, 256), (2, 1, 0, 256)],
        "early": [(1, 0, 0, 128), (1, 1, 0, 128), (3, 0, 128, 128), (3, 1, 128, 128)],
        "late": [(1, 0, 128, 128), (1, 1, 128, 128), (3, 0, 0, 128), (3, 1, 0, 128)],
    }

    def joined(parts, axis):
        return parts[0] if len(parts) == 1 else jnp.concatenate(parts, axis=axis)

    def unit(a, b):
        left_side, right_side = other_rows[a], own_rows_of[b]
        rest = joined([blocks[OTHER0 + n, pl.ds(at, size)] for n, at, size in left_side], 0)
        own = joined([blocks[2 * n + c, pl.ds(at, size)] for n, c, at, size in right_side], 0)
        logit = dot(rest, own, NT)
        value = jnp.tanh(logit * slope + shift) * 8.0
        row = joined([ids[2 * n + c, 0:1, pl.ds(at, size)] for n, c, at, size in right_side], 1).astype(F32)
        col = joined([cols[n, pl.ds(at, size)] for n, at, size in left_side], 0)
        same = jnp.concatenate([col] * 4, axis=1) == row
        value = (value + jnp.where(same, -8.0, 8.0)).astype(BF16)
        first = 0
        for n, at, size in left_side:
            begin = 0
            for m, c, start, width in right_side:
                pair[pl.ds(n * ROWS + at, size), pl.ds((2 * m + c) * ROWS + start, width)] = value[
                    first : first + size, begin : begin + width
                ]
                begin += width
            first += size

    def y_got(m):
        q = Y_ORDER[m]
        arrived("y", q, piece(1, 0, q))
        to_next(1, q).start()
        to_prev(1, q).start()

    def own_on(m):
        for q, got in ((NEXT_ORDER[m], got_next), (PREV_ORDER[m], got_prev)):
            got(0, q)
            onward(0, q).start()

    def other_on(q):
        (got_next if q < 4 else got_prev)(1, q)
        onward(1, q).start()

    def far_on(n):
        got_onward(0, EXTRA[n])
        extra(n).start()

    y_got(0)
    own_on(0)
    y_got(1)
    own_on(1)
    ids_onward(0)
    core_ids(1)
    core_ids(3)
    arrived("y_id", 0, ids.at[OTHER0])
    ids_out(1)
    arrived("core_s", 0, s_other)
    turn(s_other, ROWS)
    y_got(2)
    own_on(2)
    y_got(3)
    own_on(3)
    for q in (7, 4, 5):
        to_next(0, q).start()
    for q in (3, 0, 1):
        to_prev(0, q).start()
    core_send(1, 0, 1)
    core_send(3, 2, 3)
    other_on(0)
    y_got(4)
    other_on(4)
    y_got(5)
    far_on(0)
    far_on(1)
    ids_onward(1)
    other_on(1)
    y_got(6)
    far_on(2)
    far_on(3)
    core_send(2, 1, 3)
    other_on(5)
    y_got(7)
    arrived("ring_id", 2, ids.at[block(0, 2)])
    core_ids(2)
    for n in (0, 1, 3):
        id_columns(n)
        core_ids_got(n)
    core_got(0, 0, 1, 2, 3)
    unit("0", "0")
    core_got(1, 0, 1)
    core_got(3, 2, 3)
    unit("0", "early")
    for q in (0, 4, 1, 5):
        got_onward(0, q)
    core_send(2, 0, 2)
    for q in (4, 5):
        got_next(1, q)
    for q in (0, 1):
        got_prev(1, q)
    unit("early", "0")
    for q in (6, 7):
        got_next(0, q)
    core_send(1, 3)
    for q in (2, 3):
        got_prev(0, q)
    core_send(3, 1)
    unit("early", "early")
    core_ids_got(2)
    core_got(2, 0, 1, 2, 3)
    unit("0", "2")
    for q in (4, 5):
        got_next(0, q)
    core_send(1, 2)
    for q in (0, 1):
        got_prev(0, q)
    core_send(3, 0)
    unit("early", "2")
    arrived("ring_id", 5, ids.at[block(1, 2)])
    id_columns(2)
    for q in (0, 4, 1, 5):
        got_onward(1, q)
    for n in range(4):
        arrived("extra", n, piece(1, 2, EXTRA[n]))
    unit("2", "0")
    unit("2", "2")
    unit("2", "early")
    core_got(1, 2, 3)
    core_got(3, 0, 1)
    unit("2", "late")

    def own_terms(half, slot):
        rest = blocks[pl.ds(OTHER0, 4)].reshape(4 * ROWS, EMB)
        return dot(pair[:, pl.ds((2 * slot + half) * ROWS, ROWS)], rest, TN)

    def other_terms(slot):
        for n in range(2):
            cols = halves(n)
            own = blocks[pl.ds(0, 8), :, cols].reshape(8 * ROWS, HALF)
            value = dot(pair[pl.ds(slot * ROWS, ROWS), :], own, NN)
            if slot == 2:
                out_buf[1, 2, :, cols] = value.astype(BF16)
            else:
                grad[1, slot, :, cols] = value

    def give(slot):
        part_out[slot] = own_terms(1, slot).astype(BF16)
        copy("part", slot, part_out.at[slot], part_in.at[slot], partner).start()

    def keep(slot):
        arrived("part", slot, part_in.at[slot])
        value = own_terms(0, slot) + part_in[slot].astype(F32)
        if slot == 2:
            out_buf[0, 2] = value.astype(BF16)
        else:
            grad[0, slot] = value

    def far_copy(k, q):
        return copy("far", QS * k + q, out_buf.at[k, 2, rows(q)], far_in.at[k, rows(q)], ring(k, 1 if q < 4 else 3))

    def next_copy(k, q):
        return copy("to_next", QS * k + q, out_buf.at[k, 3, rows(q)], near_in.at[k, 0, rows(q)], ring(k, 1))

    def prev_copy(k, q):
        return copy("to_prev", QS * k + q, out_buf.at[k, 1, rows(q)], near_in.at[k, 1, rows(q)], ring(k, 3))

    def extra_of(slot, q):
        if (slot, q) in ((3, 6), (3, 7), (1, 0), (1, 1)):
            return {(3, 6): 0, (3, 7): 1, (1, 0): 2, (1, 1): 3}[slot, q]
        return None

    def extra_back(n):
        return copy("y_extra", n, extra_out.at[rows(n)], extra_in.at[rows(n)], y_down)

    def send_far(k):
        for q in (0, 4, 1, 5, 2, 6, 3, 7):
            far_copy(k, q).start()

    def send_extra(slot):
        for q in range(QS):
            n = extra_of(slot, q)
            if n is not None:
                extra_out[rows(n), :] = grad[1, slot, rows(q), :].astype(BF16)
                extra_back(n).start()

    def send_near(k, slot, order, make):
        for q in order:
            n = extra_of(slot, q)
            if n is not None and k == 1:
                continue
            term = grad[k, slot, rows(q), :]
            if (q < 4) == (slot == 3):
                arrived("far", QS * k + q, far_in.at[k, rows(q)])
                term += far_in[k, rows(q), :].astype(F32)
            if n is not None:
                arrived("y_extra", n, extra_in.at[rows(n)])
                term += extra_in[rows(n), :].astype(F32)
            out_buf[k, slot, rows(q), :] = term.astype(BF16)
            make(k, q).start()

    def reduced(k, q):
        total = grad[k, 0, rows(q), :]
        if k == 0 or extra_of(3, q) is None:
            arrived("to_next", QS * k + q, near_in.at[k, 0, rows(q)])
            total += near_in[k, 0, rows(q), :].astype(F32)
        if k == 0 or extra_of(1, q) is None:
            arrived("to_prev", QS * k + q, near_in.at[k, 1, rows(q)])
            total += near_in[k, 1, rows(q), :].astype(F32)
        return total

    def back_copy(q):
        return copy("y_back", q, y_out.at[rows(q)], y_in.at[rows(q)], y_down)

    def send_back(order):
        for q in order:
            y_out[rows(q), :] = reduced(1, q).astype(BF16)
            back_copy(q).start()

    other_terms(2)
    send_far(1)
    for q in (2, 6, 3, 7):
        got_next(1, q)
    for q in (2, 6, 3, 7):
        got_prev(1, q)
    unit("late", "2")
    give(2)
    unit("late", "0")
    unit("late", "early")
    unit("late", "late")
    unit("early", "late")
    keep(2)
    send_far(0)
    other_terms(3)
    send_extra(3)
    send_near(1, 3, (4, 5), next_copy)
    other_terms(1)
    send_extra(1)
    send_near(1, 1, (2, 3), prev_copy)
    send_near(1, 3, (0, 1, 2, 3), next_copy)
    send_near(1, 1, (4, 5, 6, 7), prev_copy)
    unit("0", "late")
    give(3)
    give(1)
    other_terms(0)
    keep(3)
    send_near(0, 3, (4, 5), next_copy)
    keep(1)
    send_near(0, 1, (2, 3), prev_copy)
    send_back(BACK_ORDER[:2])
    for n in range(4):
        send_near(0, 3, (n,), next_copy)
        send_near(0, 1, (n + 4,), prev_copy)
    send_near(0, 3, (6, 7), next_copy)
    send_near(0, 1, (0, 1), prev_copy)
    send_back(BACK_ORDER[2:4])
    give(0)
    send_back(BACK_ORDER[4:6])
    keep(0)
    send_back(BACK_ORDER[6:])

    def rg_copy(q):
        return copy("rg", q, rg_theirs.at[rows(q)], rg_mine.at[pl.ds(ROWS + CHUNK * q, CHUNK)], partner)

    for q in BACK_ORDER:
        total = reduced(0, q)
        arrived("y_back", q, y_in.at[rows(q)])
        emb_grad = temper * (total + y_in[rows(q), :].astype(F32))
        scale = inv[rows(q), 0:1]
        unit_rows = raw[rows(q), :] * scale
        along = jnp.sum(unit_rows * emb_grad, axis=1, keepdims=True)
        value = ((emb_grad - unit_rows * along) * scale).astype(BF16)
        rg[rows(q), :] = value
        low, high = value[:, :HALF], value[:, HALF:]
        rg_mine[rows(q), :] = jnp.where(core == 0, low, high)
        rg_theirs[rows(q), :] = jnp.where(core == 0, high, low)
        rg_copy(q).start()

    for q in range(QS):
        arrived("rg", q, rg_mine.at[pl.ds(ROWS + CHUNK * q, CHUNK)])

    def part_of(n, d):
        at = pl.multiple_of(lax.rem((px if n else pz) + d, 4) * FEAT_Z, FEAT_Z)
        return dot((s_x if n else s_t)[pl.ds(at, FEAT_Z), :], rg_mine[:, pl.ds(256 * n, 256)], NN)

    def st_copy(n, d):
        return copy("st", 4 * n + d, st_out.at[n, d], st_in.at[n, d], ring_x(d) if n else ring_z(d))

    for d in (2, 1, 3):
        for n in range(2):
            st_out[n, d] = part_of(n, d).astype(BF16)
            st_copy(n, d).start()
    for n in range(2):
        st_sum[n] = part_of(n, 0)

    @pl.loop(0, FEAT // 256)
    def _(n):
        here = pl.ds(pl.multiple_of(n * 256, 256), 256)
        sg_ref[:, here] = dot(rg[...], w_ref[here, :], NT).astype(BF16)

    sg_copy = pltpu.make_async_copy(sg_ref, sg_hbm, lsem.at[4 + QUARTERS])
    sg_copy.start()

    def group(n, dy, d):
        y = jnp.where(dy == 0, yh, 1 - yh)
        g = y * 4 + lax.rem(px + d, 4) if n == 0 else lax.rem(pz + d, 4) * 2 + y
        return st_sum[n, pl.ds(pl.multiple_of(g * OWN_ROWS, 8), OWN_ROWS), :]

    def stacked(value):
        return jnp.concatenate([value[:, :128], value[:, 128:]], axis=0)

    def end_copy(n, k):
        return copy("end", 8 * n + k, end_out.at[n, k], end_in.at[n, k], plane(n, k // 4, k % 4))

    for n in range(2):
        for d in (1, 3, 2):
            arrived("st", 4 * n + d, st_in.at[n, d])
        st_sum[n] += st_in[n, 1].astype(F32) + st_in[n, 2].astype(F32) + st_in[n, 3].astype(F32)
        for k in (6, 5, 7, 4, 2, 1, 3):
            end_out[n, k] = stacked(group(n, k // 4, k % 4)).astype(BF16)
            end_copy(n, k).start()

    def finished(n):
        total = stacked(group(n, 0, 0))
        for k in (1, 3, 2, 4, 5, 7, 6):
            arrived("end", 8 * n + k, end_in.at[n, k])
            total += end_in[n, k].astype(F32)
        return jnp.concatenate([total[:OWN_ROWS], total[OWN_ROWS:]], axis=1)

    p_fin = finished(0)
    q_fin = finished(1)
    both = jnp.concatenate([p_fin, q_fin], axis=1)
    first, second = both[:20], both[20:]
    theirs = jnp.where(core == 0, second, first)
    mine = jnp.where(core == 0, first, second)
    last_out[...] = jnp.concatenate([theirs, jnp.zeros((4, HALF), F32)], axis=0)
    copy("last", 0, last_out, last_in, partner).start()
    arrived("last", 0, last_in)
    got = last_in[:20, :]
    pg_ref[:, 0, :HALF] = jnp.where(core == 0, mine, got)
    pg_ref[:, 0, HALF:] = jnp.where(core == 0, got, mine)

    sg_copy.wait()
    some = blocks.at[0]
    for q in range(QS):
        left("y", q, some.at[rows(q)])
        left("y_back", q, some.at[rows(q)])
        left("rg", q, rg_theirs.at[rows(q)])
    left("y_id", 0, ids.at[0])
    for k in range(2):
        for q in range(QS):
            left("ring", 3 * QS * k + q, some.at[rows(0)])
            left("ring", 3 * QS * k + QS + q, some.at[rows(0)])
            if k == 0 or q not in EXTRA:
                left("ring", 3 * QS * k + 2 * QS + q, some.at[rows(0)])
            left("far", QS * k + q, some.at[rows(0)])
            if k == 0 or extra_of(3, q) is None:
                left("to_next", QS * k + q, some.at[rows(0)])
            if k == 0 or extra_of(1, q) is None:
                left("to_prev", QS * k + q, some.at[rows(0)])
    for n in range(6):
        left("ring_id", n, ids.at[0])
    for n in range(4):
        for m in range(4):
            left("core", 4 * n + m, some.at[pl.ds(0, 2 * CHUNK)])
        left("core_id", n, ids.at[0])
        left("part", n, some)
        left("extra", n, some.at[rows(0)])
        left("y_extra", n, some.at[rows(0)])
    left("core_s", 0, s_other)
    for n in range(2):
        for d in (1, 2, 3):
            left("st", 4 * n + d, st_out.at[n, d])
        for k in range(1, 8):
            left("end", 8 * n + k, end_out.at[n, k])
    left("last", 0, last_out)


def local(states, projection, prompt_ids, log_temper, logit_offset):
    vmem = pl.BlockSpec(memory_space=pltpu.VMEM)
    hbm = pl.BlockSpec(memory_space=pl.ANY)
    scratch = [
        ((ROWS, FEAT), BF16),
        ((FEAT, EMB), BF16),
        ((4, ROWS, 128), F32),
        ((ROWS, FEAT), BF16),
        ((1, ROWS), jnp.int32),
        None,
        None,
        ((12, ROWS, EMB), BF16),
        ((12, 8, ROWS), jnp.int32),
        ((ROWS, EMB), F32),
        ((ROWS, 128), F32),
        ((4 * ROWS, 8 * ROWS), BF16),
        ((2, 4, ROWS, EMB), F32),
        ((2, 4, ROWS, EMB), BF16),
        ((2, ROWS, EMB), BF16),
        ((2, 2, ROWS, EMB), BF16),
        ((4 * CHUNK, EMB), BF16),
        ((4 * CHUNK, EMB), BF16),
        ((4, ROWS, EMB), BF16),
        ((4, ROWS, EMB), BF16),
        ((ROWS, EMB), BF16),
        ((ROWS, EMB), BF16),
        ((ROWS, EMB), BF16),
        ((2 * ROWS, HALF), BF16),
        ((ROWS, HALF), BF16),
        ((ROWS, FEAT), BF16),
        ((FEAT, 2 * ROWS), BF16),
        ((FEAT, 2 * ROWS), BF16),
        ((FEAT, ROWS), F32),
        ((2, 4, FEAT_Z, 256), BF16),
        ((2, 4, FEAT_Z, 256), BF16),
        ((2, FEAT_Z, 256), F32),
        ((2, 8, 2 * OWN_ROWS, 128), BF16),
        ((2, 8, 2 * OWN_ROWS, 128), BF16),
        ((24, HALF), F32),
        ((24, HALF), F32),
    ]
    state_grad, owned = pl.pallas_call(
        kernel,
        out_shape=(
            jax.ShapeDtypeStruct((ROWS, FEAT), BF16),
            jax.ShapeDtypeStruct((20, 1, EMB), F32),
        ),
        in_specs=[hbm] * 5,
        out_specs=(hbm, vmem),
        scratch_shapes=[pltpu.VMEM(*what) if what else pltpu.SMEM((1,), F32) for what in scratch]
        + [pltpu.SemaphoreType.DMA((5 + QUARTERS,))]
        + [pltpu.SemaphoreType.DMA((Sems.total(),)), pltpu.SemaphoreType.DMA((Sems.total(),))],
        compiler_params=pltpu.CompilerParams(
            collective_id=0, has_side_effects=True, vmem_limit_bytes=60 * 2**20
        ),
        name="contrast",
    )(states[0], projection[0], prompt_ids.reshape(1, ROWS), log_temper, logit_offset)
    return state_grad[None], owned.reshape(1, 20, EMB)


def solution(mesh):
    return jax.shard_map(
        local,
        mesh=mesh,
        in_specs=(P("tower", "batch", None), P("tower", None, None), P("batch"), P(), P()),
        out_specs=(P("tower", "batch", None), P("tower", "batch", None)),
        check_vma=False,
    )
```

```python
import jax
import jax.numpy as jnp
from jax import lax
from jax.experimental import pallas as pl
from jax.experimental.pallas import tpu as pltpu
from jax.sharding import PartitionSpec as P

EPSILON = 1e-06
MESH = pl.DeviceIdType.MESH
F32, BF16 = jnp.float32, jnp.bfloat16
NT = (((1,), (1,)), ((), ()))
TN = (((0,), (0,)), ((), ()))
NN = (((1,), (0,)), ((), ()))

ROWS = 256
EMB = 1024
FEAT = 1280
CHUNK = 32
QS = ROWS // CHUNK
HALF = EMB // 2
QUARTERS = 4
FEAT_Z = FEAT // 4
OWN_ROWS = 40
OTHER0 = 8

Y_ORDER = (0, 4, 1, 5, 2, 6, 3, 7)
NEXT_ORDER = (2, 3, 0, 1, 6, 7, 4, 5)
PREV_ORDER = (6, 7, 4, 5, 2, 3, 0, 1)
EXTRA = (2, 6, 3, 7)
BACK_ORDER = (4, 5, 6, 0, 7, 1, 2, 3)


class Sems:
    sizes = dict(
        y=QS, y_id=1, ring=2 * 3 * QS, ring_id=2 * 3, core=16, core_id=4, core_s=1, extra=4,
        part=4, far=2 * QS, to_next=2 * QS, to_prev=2 * QS, y_extra=4, y_back=QS,
        rg=QS, st=8, end=16, last=1,
    )

    @classmethod
    def at(cls, name, index=0):
        base = 0
        for key, size in cls.sizes.items():
            if key == name:
                return base + index
            base += size
        raise KeyError(name)

    @classmethod
    def total(cls):
        return sum(cls.sizes.values())


def dot(a, b, dims):
    return lax.dot_general(a, b, dims, preferred_element_type=F32)


def kernel(
    s_hbm, w_hbm, id_hbm, lt_hbm, of_hbm, sg_ref, pg_ref,
    s_ref, w_ref, cols, id_ref, lt_ref, of_ref, blocks, ids, raw, inv, pair, grad, out_buf, far_in, near_in, extra_out, extra_in, part_out, part_in, y_out, y_in,
    rg, rg_mine, rg_theirs, s_other, s_t, s_x, tall, st_out, st_in, st_sum, end_out, end_in, last_out, last_in,
    lsem, ssem, rsem,
):
    tower = lax.axis_index("tower")
    batch = lax.axis_index("batch")
    core = lax.rem(batch, 2)
    px = lax.rem(batch // 2, 4)
    yh = lax.rem(batch // 8, 2)
    pz = batch // 16
    other = 1 - tower

    def dev(t, z, y, x, c):
        return (t, ((z * 2 + y) * 4 + x) * 2 + c)

    def ring_x(d):
        return dev(tower, pz, yh, lax.rem(px + d, 4), core)

    def ring_z(d):
        return dev(tower, lax.rem(pz + d, 4), yh, px, core)

    def ring(k, d):
        r = tower if k == 0 else other
        return dev(tower, lax.rem(pz + r * d, 4), yh, lax.rem(px + (1 - r) * d, 4), core)

    partner = dev(tower, pz, yh, px, 1 - core)
    y_up = dev(other, pz, jnp.where(tower == 1, 1 - yh, yh), px, core)
    y_down = dev(other, pz, jnp.where(tower == 0, 1 - yh, yh), px, core)

    def plane(n, dy, d):
        x = lax.rem(px + d, 4) if n == 0 else px
        z = pz if n == 0 else lax.rem(pz + d, 4)
        return dev(tower, z, 1 - yh if dy else yh, x, core)

    def block(k, slot):
        return 2 * slot if k == 0 else OTHER0 + slot

    def copy(name, index, src, dst, where):
        n = Sems.at(name) + index
        return pltpu.make_async_remote_copy(
            src_ref=src, dst_ref=dst, send_sem=ssem.at[n], recv_sem=rsem.at[n],
            device_id=where, device_id_type=MESH,
        )

    def arrived(name, index, ref):
        copy(name, index, ref, ref, partner).wait_recv()

    def left(name, index, ref):
        copy(name, index, ref, ref, partner).wait_send()

    def rows(q):
        return pl.ds(CHUNK * q, CHUNK)

    def piece(k, slot, q):
        return blocks.at[block(k, slot), rows(q)]

    barrier = pltpu.get_barrier_semaphore()
    near = [partner, y_up, y_down, plane(0, 1, 0)]
    near += [plane(n, dy, d) for n in range(2) for dy in range(2) for d in (1, 2, 3)]
    for where in near:
        pl.semaphore_signal(barrier, inc=1, device_id=where, device_id_type=MESH)

    def halves(n):
        return pl.ds(n * HALF, HALF)

    def quarter(n):
        return pl.ds(n * (EMB // QUARTERS), EMB // QUARTERS)

    loads = [pltpu.make_async_copy(s_hbm, s_ref, lsem.at[0])]
    loads += [pltpu.make_async_copy(w_hbm.at[:, quarter(n)], w_ref.at[:, quarter(n)], lsem.at[1 + n]) for n in range(QUARTERS)]
    small = [(id_hbm, id_ref), (lt_hbm, lt_ref), (of_hbm, of_ref)]
    small = [pltpu.make_async_copy(src, dst, lsem.at[1 + QUARTERS + n]) for n, (src, dst) in enumerate(small)]
    for load in loads + small:
        load.start()
    small[0].wait()
    ids[0] = jnp.broadcast_to(id_ref[...], (8, ROWS))
    small[1].wait()
    small[2].wait()
    loads[0].wait()
    for n in range(QUARTERS):
        loads[1 + n].wait()
        raw[:, quarter(n)] = dot(s_ref[...], w_ref[:, quarter(n)], NN)

    pl.semaphore_wait(barrier, len(near))

    def to_next(k, q):
        return copy("ring", 3 * QS * k + q, piece(k, 0, q), piece(k, 1, q), ring(k, 1))

    def to_prev(k, q):
        return copy("ring", 3 * QS * k + QS + q, piece(k, 0, q), piece(k, 3, q), ring(k, 3))

    def onward(k, q):
        slot = 1 if q < QS // 2 else 3
        return copy("ring", 3 * QS * k + 2 * QS + q, piece(k, slot, q), piece(k, 2, q), ring(k, slot))

    def got_next(k, q):
        arrived("ring", 3 * QS * k + q, piece(k, 1, q))

    def got_prev(k, q):
        arrived("ring", 3 * QS * k + QS + q, piece(k, 3, q))

    def got_onward(k, q):
        arrived("ring", 3 * QS * k + 2 * QS + q, piece(k, 2, q))

    def extra(n):
        return copy("extra", n, piece(0, 2, EXTRA[n]), piece(1, 2, EXTRA[n]), y_up)

    def ids_out(k):
        copy("ring_id", 3 * k, ids.at[block(k, 0)], ids.at[block(k, 1)], ring(k, 1)).start()
        copy("ring_id", 3 * k + 1, ids.at[block(k, 0)], ids.at[block(k, 3)], ring(k, 3)).start()

    def ids_onward(k):
        arrived("ring_id", 3 * k, ids.at[block(k, 1)])
        copy("ring_id", 3 * k + 2, ids.at[block(k, 1)], ids.at[block(k, 2)], ring(k, 1)).start()
        arrived("ring_id", 3 * k + 1, ids.at[block(k, 3)])

    def core_copy(slot, n):
        there = pl.ds(2 * CHUNK * n, 2 * CHUNK)
        return copy("core", 4 * slot + n, blocks.at[2 * slot, there], blocks.at[2 * slot + 1, there], partner)

    def core_send(slot, *pieces):
        for n in pieces:
            core_copy(slot, n).start()

    def core_got(slot, *pieces):
        for n in pieces:
            arrived("core", 4 * slot + n, blocks.at[2 * slot + 1, pl.ds(2 * CHUNK * n, 2 * CHUNK)])

    def core_ids_got(slot):
        arrived("core_id", slot, ids.at[2 * slot + 1])

    def core_ids(slot):
        copy("core_id", slot, ids.at[2 * slot], ids.at[2 * slot + 1], partner).start()

    copy("y_id", 0, ids.at[0], ids.at[OTHER0], y_up).start()
    ids_out(0)
    def own_rows(q):
        part = raw[rows(q), :]
        length = jnp.sqrt(jnp.sum(part * part, axis=1, keepdims=True) + EPSILON)
        scale = 1.0 / length
        inv[rows(q), :] = jnp.broadcast_to(scale, (CHUNK, 128))
        blocks[0, rows(q)] = (part * scale).astype(BF16)

    def y_send(q):
        copy("y", q, piece(0, 0, q), piece(1, 0, q), y_up).start()

    for q in (0, 1):
        own_rows(q)
        y_send(q)
        own_rows(q + 2)
        to_next(0, q + 2).start()
        own_rows(q + 4)
        y_send(q + 4)
        own_rows(q + 6)
        to_prev(0, q + 6).start()
    for q in EXTRA:
        y_send(q)
    for q in (0, 1, 6):
        to_next(0, q).start()
    for q in (4, 5, 2):
        to_prev(0, q).start()
    core_send(0, 0, 1, 2, 3)
    core_ids(0)

    def turn(states, first):
        tall[...] = states[...].astype(F32).T
        here = pl.ds(first, ROWS)
        s_t[:, here] = tall[...].astype(BF16)
        for x in range(4):
            pieces = [tall[pl.ds((4 * k + x) * OWN_ROWS, OWN_ROWS), :] for k in range(8)]
            s_x[pl.ds(x * FEAT_Z, FEAT_Z), here] = jnp.concatenate(pieces, axis=0).astype(BF16)

    copy("core_s", 0, s_ref, s_other, partner).start()
    turn(s_ref, 0)

    temper = jnp.exp(jnp.full((1, 1), lt_ref[0], F32))
    slope = 0.5 * temper
    shift = jnp.full((1, 1), 0.5 * of_ref[0], F32)

    def id_columns(slot):
        cols[slot] = jnp.broadcast_to(ids[OTHER0 + slot, 0:1, :].astype(F32), (128, ROWS)).T

    other_rows = {
        "0": [(0, 0, 256)],
        "2": [(2, 0, 256)],
        "early": [(1, 0, 64), (1, 128, 64), (3, 0, 64), (3, 128, 64)],
        "late": [(1, 64, 64), (1, 192, 64), (3, 64, 64), (3, 192, 64)],
    }
    own_rows_of = {
        "0": [(0, 0, 0, 256), (0, 1, 0, 256)],
        "2": [(2, 0, 0, 256), (2, 1, 0, 256)],
        "early": [(1, 0, 0, 128), (1, 1, 0, 128), (3, 0, 128, 128), (3, 1, 128, 128)],
        "late": [(1, 0, 128, 128), (1, 1, 128, 128), (3, 0, 0, 128), (3, 1, 0, 128)],
    }

    def joined(parts, axis):
        return parts[0] if len(parts) == 1 else jnp.concatenate(parts, axis=axis)

    def unit(a, b):
        left_side, right_side = other_rows[a], own_rows_of[b]
        rest = joined([blocks[OTHER0 + n, pl.ds(at, size)] for n, at, size in left_side], 0)
        own = joined([blocks[2 * n + c, pl.ds(at, size)] for n, c, at, size in right_side], 0)
        logit = dot(rest, own, NT)
        value = jnp.tanh(logit * slope + shift) * 8.0
        row = joined([ids[2 * n + c, 0:1, pl.ds(at, size)] for n, c, at, size in right_side], 1).astype(F32)
        col = joined([cols[n, pl.ds(at, size)] for n, at, size in left_side], 0)
        same = jnp.concatenate([col] * 4, axis=1) == row
        value = (value + jnp.where(same, -8.0, 8.0)).astype(BF16)
        first = 0
        for n, at, size in left_side:
            begin = 0
            for m, c, start, width in right_side:
                pair[pl.ds(n * ROWS + at, size), pl.ds((2 * m + c) * ROWS + start, width)] = value[
                    first : first + size, begin : begin + width
                ]
                begin += width
            first += size

    def y_got(m):
        q = Y_ORDER[m]
        arrived("y", q, piece(1, 0, q))
        to_next(1, q).start()
        to_prev(1, q).start()

    def own_on(m):
        for q, got in ((NEXT_ORDER[m], got_next), (PREV_ORDER[m], got_prev)):
            got(0, q)
            onward(0, q).start()

    def other_on(q):
        (got_next if q < 4 else got_prev)(1, q)
        onward(1, q).start()

    def far_on(n):
        got_onward(0, EXTRA[n])
        extra(n).start()

    y_got(0)
    own_on(0)
    y_got(1)
    own_on(1)
    ids_onward(0)
    core_ids(1)
    core_ids(3)
    arrived("y_id", 0, ids.at[OTHER0])
    ids_out(1)
    arrived("core_s", 0, s_other)
    turn(s_other, ROWS)
    y_got(2)
    own_on(2)
    y_got(3)
    own_on(3)
    for q in (7, 4, 5):
        to_next(0, q).start()
    for q in (3, 0, 1):
        to_prev(0, q).start()
    core_send(1, 0, 1)
    core_send(3, 2, 3)
    other_on(0)
    y_got(4)
    other_on(4)
    y_got(5)
    far_on(0)
    far_on(1)
    ids_onward(1)
    other_on(1)
    y_got(6)
    far_on(2)
    far_on(3)
    core_send(2, 1, 3)
    other_on(5)
    y_got(7)
    arrived("ring_id", 2, ids.at[block(0, 2)])
    core_ids(2)
    for n in (0, 1, 3):
        id_columns(n)
        core_ids_got(n)
    core_got(0, 0, 1, 2, 3)
    unit("0", "0")
    core_got(1, 0, 1)
    core_got(3, 2, 3)
    unit("0", "early")
    for q in (0, 4, 1, 5):
        got_onward(0, q)
    core_send(2, 0, 2)
    for q in (4, 5):
        got_next(1, q)
    for q in (0, 1):
        got_prev(1, q)
    unit("early", "0")
    for q in (6, 7):
        got_next(0, q)
    core_send(1, 3)
    for q in (2, 3):
        got_prev(0, q)
    core_send(3, 1)
    unit("early", "early")
    core_ids_got(2)
    core_got(2, 0, 1, 2, 3)
    unit("0", "2")
    for q in (4, 5):
        got_next(0, q)
    core_send(1, 2)
    for q in (0, 1):
        got_prev(0, q)
    core_send(3, 0)
    unit("early", "2")
    arrived("ring_id", 5, ids.at[block(1, 2)])
    id_columns(2)
    for q in (0, 4, 1, 5):
        got_onward(1, q)
    for n in range(4):
        arrived("extra", n, piece(1, 2, EXTRA[n]))
    unit("2", "0")
    unit("2", "2")
    unit("2", "early")
    core_got(1, 2, 3)
    core_got(3, 0, 1)
    unit("2", "late")

    def own_terms(half, slot):
        rest = blocks[pl.ds(OTHER0, 4)].reshape(4 * ROWS, EMB)
        return dot(pair[:, pl.ds((2 * slot + half) * ROWS, ROWS)], rest, TN)

    def other_terms(slot):
        for n in range(2):
            cols = halves(n)
            own = blocks[pl.ds(0, 8), :, cols].reshape(8 * ROWS, HALF)
            value = dot(pair[pl.ds(slot * ROWS, ROWS), :], own, NN)
            if slot == 2:
                out_buf[1, 2, :, cols] = value.astype(BF16)
            else:
                grad[1, slot, :, cols] = value

    def give(slot):
        part_out[slot] = own_terms(1, slot).astype(BF16)
        copy("part", slot, part_out.at[slot], part_in.at[slot], partner).start()

    def keep(slot):
        arrived("part", slot, part_in.at[slot])
        value = own_terms(0, slot) + part_in[slot].astype(F32)
        if slot == 2:
            out_buf[0, 2] = value.astype(BF16)
        else:
            grad[0, slot] = value

    def far_copy(k, q):
        return copy("far", QS * k + q, out_buf.at[k, 2, rows(q)], far_in.at[k, rows(q)], ring(k, 1 if q < 4 else 3))

    def next_copy(k, q):
        return copy("to_next", QS * k + q, out_buf.at[k, 3, rows(q)], near_in.at[k, 0, rows(q)], ring(k, 1))

    def prev_copy(k, q):
        return copy("to_prev", QS * k + q, out_buf.at[k, 1, rows(q)], near_in.at[k, 1, rows(q)], ring(k, 3))

    def extra_of(slot, q):
        if (slot, q) in ((3, 6), (3, 7), (1, 0), (1, 1)):
            return {(3, 6): 0, (3, 7): 1, (1, 0): 2, (1, 1): 3}[slot, q]
        return None

    def extra_back(n):
        return copy("y_extra", n, extra_out.at[rows(n)], extra_in.at[rows(n)], y_down)

    def send_far(k):
        for q in (0, 4, 1, 5, 2, 6, 3, 7):
            far_copy(k, q).start()

    def send_extra(slot):
        for q in range(QS):
            n = extra_of(slot, q)
            if n is not None:
                extra_out[rows(n), :] = grad[1, slot, rows(q), :].astype(BF16)
                extra_back(n).start()

    def send_near(k, slot, order, make):
        for q in order:
            n = extra_of(slot, q)
            if n is not None and k == 1:
                continue
            term = grad[k, slot, rows(q), :]
            if (q < 4) == (slot == 3):
                arrived("far", QS * k + q, far_in.at[k, rows(q)])
                term += far_in[k, rows(q), :].astype(F32)
            if n is not None:
                arrived("y_extra", n, extra_in.at[rows(n)])
                term += extra_in[rows(n), :].astype(F32)
            out_buf[k, slot, rows(q), :] = term.astype(BF16)
            make(k, q).start()

    def reduced(k, q):
        total = grad[k, 0, rows(q), :]
        if k == 0 or extra_of(3, q) is None:
            arrived("to_next", QS * k + q, near_in.at[k, 0, rows(q)])
            total += near_in[k, 0, rows(q), :].astype(F32)
        if k == 0 or extra_of(1, q) is None:
            arrived("to_prev", QS * k + q, near_in.at[k, 1, rows(q)])
            total += near_in[k, 1, rows(q), :].astype(F32)
        return total

    def back_copy(q):
        return copy("y_back", q, y_out.at[rows(q)], y_in.at[rows(q)], y_down)

    def send_back(order):
        for q in order:
            y_out[rows(q), :] = reduced(1, q).astype(BF16)
            back_copy(q).start()

    other_terms(2)
    send_far(1)
    for q in (2, 6, 3, 7):
        got_next(1, q)
    for q in (2, 6, 3, 7):
        got_prev(1, q)
    unit("late", "2")
    give(2)
    unit("late", "0")
    unit("late", "early")
    unit("late", "late")
    unit("early", "late")
    keep(2)
    send_far(0)
    other_terms(3)
    send_extra(3)
    send_near(1, 3, (4, 5), next_copy)
    other_terms(1)
    send_extra(1)
    send_near(1, 1, (2, 3), prev_copy)
    send_near(1, 3, (0, 1, 2, 3), next_copy)
    send_near(1, 1, (4, 5, 6, 7), prev_copy)
    unit("0", "late")
    give(3)
    give(1)
    other_terms(0)
    keep(3)
    send_near(0, 3, (4, 5), next_copy)
    keep(1)
    send_near(0, 1, (2, 3), prev_copy)
    send_back(BACK_ORDER[:2])
    for n in range(4):
        send_near(0, 3, (n,), next_copy)
        send_near(0, 1, (n + 4,), prev_copy)
    send_near(0, 3, (6, 7), next_copy)
    send_near(0, 1, (0, 1), prev_copy)
    send_back(BACK_ORDER[2:4])
    give(0)
    send_back(BACK_ORDER[4:6])
    keep(0)
    send_back(BACK_ORDER[6:])

    def rg_copy(q):
        return copy("rg", q, rg_theirs.at[rows(q)], rg_mine.at[pl.ds(ROWS + CHUNK * q, CHUNK)], partner)

    for q in BACK_ORDER:
        total = reduced(0, q)
        arrived("y_back", q, y_in.at[rows(q)])
        emb_grad = temper * (total + y_in[rows(q), :].astype(F32))
        scale = inv[rows(q), 0:1]
        unit_rows = raw[rows(q), :] * scale
        along = jnp.sum(unit_rows * emb_grad, axis=1, keepdims=True)
        value = ((emb_grad - unit_rows * along) * scale).astype(BF16)
        rg[rows(q), :] = value
        low, high = value[:, :HALF], value[:, HALF:]
        rg_mine[rows(q), :] = jnp.where(core == 0, low, high)
        rg_theirs[rows(q), :] = jnp.where(core == 0, high, low)
        rg_copy(q).start()

    for q in range(QS):
        arrived("rg", q, rg_mine.at[pl.ds(ROWS + CHUNK * q, CHUNK)])

    def part_of(n, d):
        at = pl.multiple_of(lax.rem((px if n else pz) + d, 4) * FEAT_Z, FEAT_Z)
        return dot((s_x if n else s_t)[pl.ds(at, FEAT_Z), :], rg_mine[:, pl.ds(256 * n, 256)], NN)

    def st_copy(n, d):
        return copy("st", 4 * n + d, st_out.at[n, d], st_in.at[n, d], ring_x(d) if n else ring_z(d))

    for d in (2, 1, 3):
        for n in range(2):
            st_out[n, d] = part_of(n, d).astype(BF16)
            st_copy(n, d).start()
    for n in range(2):
        st_sum[n] = part_of(n, 0)

    @pl.loop(0, FEAT // 256)
    def _(n):
        here = pl.ds(pl.multiple_of(n * 256, 256), 256)
        sg_ref[:, here] = dot(rg[...], w_ref[here, :], NT).astype(BF16)

    def group(n, dy, d):
        y = jnp.where(dy == 0, yh, 1 - yh)
        g = y * 4 + lax.rem(px + d, 4) if n == 0 else lax.rem(pz + d, 4) * 2 + y
        return st_sum[n, pl.ds(pl.multiple_of(g * OWN_ROWS, 8), OWN_ROWS), :]

    def stacked(value):
        return jnp.concatenate([value[:, :128], value[:, 128:]], axis=0)

    def end_copy(n, k):
        return copy("end", 8 * n + k, end_out.at[n, k], end_in.at[n, k], plane(n, k // 4, k % 4))

    for n in range(2):
        for d in (1, 3, 2):
            arrived("st", 4 * n + d, st_in.at[n, d])
        st_sum[n] += st_in[n, 1].astype(F32) + st_in[n, 2].astype(F32) + st_in[n, 3].astype(F32)
        for k in (6, 5, 7, 4, 2, 1, 3):
            end_out[n, k] = stacked(group(n, k // 4, k % 4)).astype(BF16)
            end_copy(n, k).start()

    def finished(n):
        total = stacked(group(n, 0, 0))
        for k in (1, 3, 2, 4, 5, 7, 6):
            arrived("end", 8 * n + k, end_in.at[n, k])
            total += end_in[n, k].astype(F32)
        return jnp.concatenate([total[:OWN_ROWS], total[OWN_ROWS:]], axis=1)

    p_fin = finished(0)
    q_fin = finished(1)
    both = jnp.concatenate([p_fin, q_fin], axis=1)
    first, second = both[:20], both[20:]
    theirs = jnp.where(core == 0, second, first)
    mine = jnp.where(core == 0, first, second)
    last_out[...] = jnp.concatenate([theirs, jnp.zeros((4, HALF), F32)], axis=0)
    copy("last", 0, last_out, last_in, partner).start()
    arrived("last", 0, last_in)
    got = last_in[:20, :]
    pg_ref[:, 0, :HALF] = jnp.where(core == 0, mine, got)
    pg_ref[:, 0, HALF:] = jnp.where(core == 0, got, mine)

    some = blocks.at[0]
    for q in range(QS):
        left("y", q, some.at[rows(q)])
        left("y_back", q, some.at[rows(q)])
        left("rg", q, rg_theirs.at[rows(q)])
    left("y_id", 0, ids.at[0])
    for k in range(2):
        for q in range(QS):
            left("ring", 3 * QS * k + q, some.at[rows(0)])
            left("ring", 3 * QS * k + QS + q, some.at[rows(0)])
            if k == 0 or q not in EXTRA:
                left("ring", 3 * QS * k + 2 * QS + q, some.at[rows(0)])
            left("far", QS * k + q, some.at[rows(0)])
            if k == 0 or extra_of(3, q) is None:
                left("to_next", QS * k + q, some.at[rows(0)])
            if k == 0 or extra_of(1, q) is None:
                left("to_prev", QS * k + q, some.at[rows(0)])
    for n in range(6):
        left("ring_id", n, ids.at[0])
    for n in range(4):
        for m in range(4):
            left("core", 4 * n + m, some.at[pl.ds(0, 2 * CHUNK)])
        left("core_id", n, ids.at[0])
        left("part", n, some)
        left("extra", n, some.at[rows(0)])
        left("y_extra", n, some.at[rows(0)])
    left("core_s", 0, s_other)
    for n in range(2):
        for d in (1, 2, 3):
            left("st", 4 * n + d, st_out.at[n, d])
        for k in range(1, 8):
            left("end", 8 * n + k, end_out.at[n, k])
    left("last", 0, last_out)


def local(states, projection, prompt_ids, log_temper, logit_offset):
    vmem = pl.BlockSpec(memory_space=pltpu.VMEM)
    hbm = pl.BlockSpec(memory_space=pl.ANY)
    scratch = [
        ((ROWS, FEAT), BF16),
        ((FEAT, EMB), BF16),
        ((4, ROWS, 128), F32),
        ((1, ROWS), jnp.int32),
        None,
        None,
        ((12, ROWS, EMB), BF16),
        ((12, 8, ROWS), jnp.int32),
        ((ROWS, EMB), F32),
        ((ROWS, 128), F32),
        ((4 * ROWS, 8 * ROWS), BF16),
        ((2, 4, ROWS, EMB), F32),
        ((2, 4, ROWS, EMB), BF16),
        ((2, ROWS, EMB), BF16),
        ((2, 2, ROWS, EMB), BF16),
        ((4 * CHUNK, EMB), BF16),
        ((4 * CHUNK, EMB), BF16),
        ((4, ROWS, EMB), BF16),
        ((4, ROWS, EMB), BF16),
        ((ROWS, EMB), BF16),
        ((ROWS, EMB), BF16),
        ((ROWS, EMB), BF16),
        ((2 * ROWS, HALF), BF16),
        ((ROWS, HALF), BF16),
        ((ROWS, FEAT), BF16),
        ((FEAT, 2 * ROWS), BF16),
        ((FEAT, 2 * ROWS), BF16),
        ((FEAT, ROWS), F32),
        ((2, 4, FEAT_Z, 256), BF16),
        ((2, 4, FEAT_Z, 256), BF16),
        ((2, FEAT_Z, 256), F32),
        ((2, 8, 2 * OWN_ROWS, 128), BF16),
        ((2, 8, 2 * OWN_ROWS, 128), BF16),
        ((24, HALF), F32),
        ((24, HALF), F32),
    ]
    state_grad, owned = pl.pallas_call(
        kernel,
        out_shape=(
            pltpu.VMEM((ROWS, FEAT), BF16),
            pltpu.VMEM((20, 1, EMB), F32),
        ),
        in_specs=[hbm] * 5,
        out_specs=(vmem, vmem),
        scratch_shapes=[pltpu.VMEM(*what) if what else pltpu.SMEM((1,), F32) for what in scratch]
        + [pltpu.SemaphoreType.DMA((4 + QUARTERS,))]
        + [pltpu.SemaphoreType.DMA((Sems.total(),)), pltpu.SemaphoreType.DMA((Sems.total(),))],
        compiler_params=pltpu.CompilerParams(
            collective_id=0, has_side_effects=True, vmem_limit_bytes=60 * 2**20
        ),
        name="contrast",
    )(states[0], projection[0], prompt_ids.reshape(1, ROWS), log_temper, logit_offset)
    return state_grad[None], owned.reshape(1, 20, EMB)


def solution(mesh):
    return jax.shard_map(
        local,
        mesh=mesh,
        in_specs=(P("tower", "batch", None), P("tower", None, None), P("batch"), P(), P()),
        out_specs=(P("tower", "batch", None), P("tower", "batch", None)),
        check_vma=False,
    )
```

```python
import jax
import jax.numpy as jnp
from jax import lax
from jax.experimental import pallas as pl
from jax.experimental.pallas import tpu as pltpu
from jax.sharding import PartitionSpec as P

EPSILON = 1e-06
MESH = pl.DeviceIdType.MESH
F32, BF16 = jnp.float32, jnp.bfloat16
NT = (((1,), (1,)), ((), ()))
TN = (((0,), (0,)), ((), ()))
NN = (((1,), (0,)), ((), ()))

ROWS = 256
EMB = 1024
FEAT = 1280
CHUNK = 32
QS = ROWS // CHUNK
HALF = EMB // 2
QUARTERS = 4
FEAT_Z = FEAT // 4
OWN_ROWS = 40
PADDED = 48
OTHER0 = 8

Y_ORDER = (0, 4, 1, 5, 2, 6, 3, 7)
NEXT_ORDER = (2, 3, 0, 1, 6, 7, 4, 5)
PREV_ORDER = (6, 7, 4, 5, 2, 3, 0, 1)
EXTRA = (2, 6, 3, 7)
BACK_ORDER = (4, 5, 6, 0, 7, 1, 2, 3)


class Sems:
    sizes = dict(
        y=QS, y_id=1, ring=2 * 3 * QS, ring_id=2 * 3, core=16, core_id=4, core_s=1, extra=4,
        part=4, far=2 * QS, to_next=2 * QS, to_prev=2 * QS, y_extra=4, y_back=QS,
        rg=QS, st=16, end=32, last=1,
    )

    @classmethod
    def at(cls, name, index=0):
        base = 0
        for key, size in cls.sizes.items():
            if key == name:
                return base + index
            base += size
        raise KeyError(name)

    @classmethod
    def total(cls):
        return sum(cls.sizes.values())


def dot(a, b, dims):
    return lax.dot_general(a, b, dims, preferred_element_type=F32)


def kernel(
    s_hbm, w_hbm, id_hbm, lt_hbm, of_hbm, sg_ref, pg_ref,
    s_ref, w_ref, cols, id_ref, lt_ref, of_ref, blocks, ids, raw, inv, pair, grad, out_buf, far_in, near_in, extra_out, extra_in, part_out, part_in, y_out, y_in,
    rg, rg_mine, rg_theirs, s_other, s_t, s_x, tall, st_out, st_in, st_sum, end_out, end_in, last_out, last_in,
    lsem, ssem, rsem,
):
    tower = lax.axis_index("tower")
    batch = lax.axis_index("batch")
    core = lax.rem(batch, 2)
    px = lax.rem(batch // 2, 4)
    yh = lax.rem(batch // 8, 2)
    pz = batch // 16
    other = 1 - tower

    def dev(t, z, y, x, c):
        return (t, ((z * 2 + y) * 4 + x) * 2 + c)

    def ring_x(d):
        return dev(tower, pz, yh, lax.rem(px + d, 4), core)

    def ring_z(d):
        return dev(tower, lax.rem(pz + d, 4), yh, px, core)

    def ring(k, d):
        r = tower if k == 0 else other
        return dev(tower, lax.rem(pz + r * d, 4), yh, lax.rem(px + (1 - r) * d, 4), core)

    partner = dev(tower, pz, yh, px, 1 - core)
    y_up = dev(other, pz, jnp.where(tower == 1, 1 - yh, yh), px, core)
    y_down = dev(other, pz, jnp.where(tower == 0, 1 - yh, yh), px, core)

    def plane(n, dy, d):
        x = lax.rem(px + d, 4) if n == 0 else px
        z = pz if n == 0 else lax.rem(pz + d, 4)
        return dev(tower, z, 1 - yh if dy else yh, x, core)

    def block(k, slot):
        return 2 * slot if k == 0 else OTHER0 + slot

    def copy(name, index, src, dst, where):
        n = Sems.at(name) + index
        return pltpu.make_async_remote_copy(
            src_ref=src, dst_ref=dst, send_sem=ssem.at[n], recv_sem=rsem.at[n],
            device_id=where, device_id_type=MESH,
        )

    def arrived(name, index, ref):
        copy(name, index, ref, ref, partner).wait_recv()

    def left(name, index, ref):
        copy(name, index, ref, ref, partner).wait_send()

    def rows(q):
        return pl.ds(CHUNK * q, CHUNK)

    def piece(k, slot, q):
        return blocks.at[block(k, slot), rows(q)]

    barrier = pltpu.get_barrier_semaphore()
    near = [partner, y_up, y_down] + [plane(n, 0, d) for n in range(2) for d in (1, 3)]
    for where in near:
        pl.semaphore_signal(barrier, inc=1, device_id=where, device_id_type=MESH)

    def halves(n):
        return pl.ds(n * HALF, HALF)

    def quarter(n):
        return pl.ds(n * (EMB // QUARTERS), EMB // QUARTERS)

    loads = [pltpu.make_async_copy(s_hbm, s_ref, lsem.at[0])]
    loads += [pltpu.make_async_copy(w_hbm.at[:, quarter(n)], w_ref.at[:, quarter(n)], lsem.at[1 + n]) for n in range(QUARTERS)]
    small = [(id_hbm, id_ref), (lt_hbm, lt_ref), (of_hbm, of_ref)]
    small = [pltpu.make_async_copy(src, dst, lsem.at[1 + QUARTERS + n]) for n, (src, dst) in enumerate(small)]
    for load in loads + small:
        load.start()
    small[0].wait()
    ids[0] = jnp.broadcast_to(id_ref[...], (8, ROWS))
    small[1].wait()
    small[2].wait()
    loads[0].wait()
    for n in range(QUARTERS):
        loads[1 + n].wait()
        raw[:, quarter(n)] = dot(s_ref[...], w_ref[:, quarter(n)], NN)

    pl.semaphore_wait(barrier, len(near))

    def to_next(k, q):
        return copy("ring", 3 * QS * k + q, piece(k, 0, q), piece(k, 1, q), ring(k, 1))

    def to_prev(k, q):
        return copy("ring", 3 * QS * k + QS + q, piece(k, 0, q), piece(k, 3, q), ring(k, 3))

    def onward(k, q):
        slot = 1 if q < QS // 2 else 3
        return copy("ring", 3 * QS * k + 2 * QS + q, piece(k, slot, q), piece(k, 2, q), ring(k, slot))

    def got_next(k, q):
        arrived("ring", 3 * QS * k + q, piece(k, 1, q))

    def got_prev(k, q):
        arrived("ring", 3 * QS * k + QS + q, piece(k, 3, q))

    def got_onward(k, q):
        arrived("ring", 3 * QS * k + 2 * QS + q, piece(k, 2, q))

    def extra(n):
        return copy("extra", n, piece(0, 2, EXTRA[n]), piece(1, 2, EXTRA[n]), y_up)

    def ids_out(k):
        copy("ring_id", 3 * k, ids.at[block(k, 0)], ids.at[block(k, 1)], ring(k, 1)).start()
        copy("ring_id", 3 * k + 1, ids.at[block(k, 0)], ids.at[block(k, 3)], ring(k, 3)).start()

    def ids_onward(k):
        arrived("ring_id", 3 * k, ids.at[block(k, 1)])
        copy("ring_id", 3 * k + 2, ids.at[block(k, 1)], ids.at[block(k, 2)], ring(k, 1)).start()
        arrived("ring_id", 3 * k + 1, ids.at[block(k, 3)])

    def core_copy(slot, n):
        there = pl.ds(2 * CHUNK * n, 2 * CHUNK)
        return copy("core", 4 * slot + n, blocks.at[2 * slot, there], blocks.at[2 * slot + 1, there], partner)

    def core_send(slot, *pieces):
        for n in pieces:
            core_copy(slot, n).start()

    def core_got(slot, *pieces):
        for n in pieces:
            arrived("core", 4 * slot + n, blocks.at[2 * slot + 1, pl.ds(2 * CHUNK * n, 2 * CHUNK)])

    def core_ids_got(slot):
        arrived("core_id", slot, ids.at[2 * slot + 1])

    def core_ids(slot):
        copy("core_id", slot, ids.at[2 * slot], ids.at[2 * slot + 1], partner).start()

    copy("y_id", 0, ids.at[0], ids.at[OTHER0], y_up).start()
    ids_out(0)
    def own_rows(q):
        part = raw[rows(q), :]
        length = jnp.sqrt(jnp.sum(part * part, axis=1, keepdims=True) + EPSILON)
        scale = 1.0 / length
        inv[rows(q), :] = jnp.broadcast_to(scale, (CHUNK, 128))
        blocks[0, rows(q)] = (part * scale).astype(BF16)

    def y_send(q):
        copy("y", q, piece(0, 0, q), piece(1, 0, q), y_up).start()

    for q in (0, 1):
        own_rows(q)
        y_send(q)
        own_rows(q + 2)
        to_next(0, q + 2).start()
        own_rows(q + 4)
        y_send(q + 4)
        own_rows(q + 6)
        to_prev(0, q + 6).start()
    for q in EXTRA:
        y_send(q)
    for q in (0, 1, 6):
        to_next(0, q).start()
    for q in (4, 5, 2):
        to_prev(0, q).start()
    core_send(0, 0, 1, 2, 3)
    core_ids(0)

    def turn(states, first):
        tall[...] = states[...].astype(F32).T
        here = pl.ds(first, ROWS)
        s_t[:, here] = tall[...].astype(BF16)
        for x in range(4):
            pieces = [tall[pl.ds((4 * k + x) * OWN_ROWS, OWN_ROWS), :] for k in range(8)]
            s_x[pl.ds(x * FEAT_Z, FEAT_Z), here] = jnp.concatenate(pieces, axis=0).astype(BF16)

    copy("core_s", 0, s_ref, s_other, partner).start()
    turn(s_ref, 0)

    temper = jnp.exp(jnp.full((1, 1), lt_ref[0], F32))
    slope = 0.5 * temper
    shift = jnp.full((1, 1), 0.5 * of_ref[0], F32)

    def id_columns(slot):
        cols[slot] = jnp.broadcast_to(ids[OTHER0 + slot, 0:1, :].astype(F32), (128, ROWS)).T

    other_rows = {
        "0": [(0, 0, 256)],
        "2": [(2, 0, 256)],
        "early": [(1, 0, 64), (1, 128, 64), (3, 0, 64), (3, 128, 64)],
        "late": [(1, 64, 64), (1, 192, 64), (3, 64, 64), (3, 192, 64)],
    }
    own_rows_of = {
        "0": [(0, 0, 0, 256), (0, 1, 0, 256)],
        "2": [(2, 0, 0, 256), (2, 1, 0, 256)],
        "early": [(1, 0, 0, 128), (1, 1, 0, 128), (3, 0, 128, 128), (3, 1, 128, 128)],
        "late": [(1, 0, 128, 128), (1, 1, 128, 128), (3, 0, 0, 128), (3, 1, 0, 128)],
    }

    def joined(parts, axis):
        return parts[0] if len(parts) == 1 else jnp.concatenate(parts, axis=axis)

    def unit(a, b):
        left_side, right_side = other_rows[a], own_rows_of[b]
        rest = joined([blocks[OTHER0 + n, pl.ds(at, size)] for n, at, size in left_side], 0)
        own = joined([blocks[2 * n + c, pl.ds(at, size)] for n, c, at, size in right_side], 0)
        logit = dot(rest, own, NT)
        value = jnp.tanh(logit * slope + shift) * 8.0
        row = joined([ids[2 * n + c, 0:1, pl.ds(at, size)] for n, c, at, size in right_side], 1).astype(F32)
        col = joined([cols[n, pl.ds(at, size)] for n, at, size in left_side], 0)
        same = jnp.concatenate([col] * 4, axis=1) == row
        value = (value + jnp.where(same, -8.0, 8.0)).astype(BF16)
        first = 0
        for n, at, size in left_side:
            begin = 0
            for m, c, start, width in right_side:
                pair[pl.ds(n * ROWS + at, size), pl.ds((2 * m + c) * ROWS + start, width)] = value[
                    first : first + size, begin : begin + width
                ]
                begin += width
            first += size

    def y_got(m):
        q = Y_ORDER[m]
        arrived("y", q, piece(1, 0, q))
        to_next(1, q).start()
        to_prev(1, q).start()

    def own_on(m):
        for q, got in ((NEXT_ORDER[m], got_next), (PREV_ORDER[m], got_prev)):
            got(0, q)
            onward(0, q).start()

    def other_on(q):
        (got_next if q < 4 else got_prev)(1, q)
        onward(1, q).start()

    def far_on(n):
        got_onward(0, EXTRA[n])
        extra(n).start()

    y_got(0)
    own_on(0)
    y_got(1)
    own_on(1)
    ids_onward(0)
    core_ids(1)
    core_ids(3)
    arrived("y_id", 0, ids.at[OTHER0])
    ids_out(1)
    arrived("core_s", 0, s_other)
    turn(s_other, ROWS)
    y_got(2)
    own_on(2)
    y_got(3)
    own_on(3)
    for q in (7, 4, 5):
        to_next(0, q).start()
    for q in (3, 0, 1):
        to_prev(0, q).start()
    core_send(1, 0, 1)
    core_send(3, 2, 3)
    other_on(0)
    y_got(4)
    other_on(4)
    y_got(5)
    far_on(0)
    far_on(1)
    ids_onward(1)
    other_on(1)
    y_got(6)
    far_on(2)
    far_on(3)
    core_send(2, 1, 3)
    other_on(5)
    y_got(7)
    arrived("ring_id", 2, ids.at[block(0, 2)])
    core_ids(2)
    for n in (0, 1, 3):
        id_columns(n)
        core_ids_got(n)
    core_got(0, 0, 1, 2, 3)
    unit("0", "0")
    core_got(1, 0, 1)
    core_got(3, 2, 3)
    unit("0", "early")
    for q in (0, 4, 1, 5):
        got_onward(0, q)
    core_send(2, 0, 2)
    for q in (4, 5):
        got_next(1, q)
    for q in (0, 1):
        got_prev(1, q)
    unit("early", "0")
    for q in (6, 7):
        got_next(0, q)
    core_send(1, 3)
    for q in (2, 3):
        got_prev(0, q)
    core_send(3, 1)
    unit("early", "early")
    core_ids_got(2)
    core_got(2, 0, 1, 2, 3)
    unit("0", "2")
    for q in (4, 5):
        got_next(0, q)
    core_send(1, 2)
    for q in (0, 1):
        got_prev(0, q)
    core_send(3, 0)
    unit("early", "2")
    arrived("ring_id", 5, ids.at[block(1, 2)])
    id_columns(2)
    for q in (0, 4, 1, 5):
        got_onward(1, q)
    for n in range(4):
        arrived("extra", n, piece(1, 2, EXTRA[n]))
    unit("2", "0")
    unit("2", "2")
    unit("2", "early")

    def own_terms(half, slot):
        rest = blocks[pl.ds(OTHER0, 4)].reshape(4 * ROWS, EMB)
        return dot(pair[:, pl.ds((2 * slot + half) * ROWS, ROWS)], rest, TN)

    def other_terms(slot):
        for n in range(2):
            cols = halves(n)
            own = blocks[pl.ds(0, 8), :, cols].reshape(8 * ROWS, HALF)
            grad[1, slot, :, cols] = dot(pair[pl.ds(slot * ROWS, ROWS), :], own, NN)

    def far_terms(names, last):
        what = [one for name in names for one in own_rows_of[name]]
        terms = joined([pair[pl.ds(2 * ROWS, ROWS), pl.ds((2 * m + c) * ROWS + at, size)] for m, c, at, size in what], 1)
        for n in range(2):
            own = joined([blocks[2 * m + c, pl.ds(at, size), halves(n)] for m, c, at, size in what], 0)
            value = dot(terms, own, NN)
            if last:
                out_buf[1, 2, :, halves(n)] = (grad[1, 2, :, halves(n)] + value).astype(BF16)
            else:
                grad[1, 2, :, halves(n)] = value

    def give(slot):
        part_out[slot] = own_terms(1, slot).astype(BF16)
        copy("part", slot, part_out.at[slot], part_in.at[slot], partner).start()

    def keep(slot):
        arrived("part", slot, part_in.at[slot])
        value = own_terms(0, slot) + part_in[slot].astype(F32)
        if slot == 2:
            out_buf[0, 2] = value.astype(BF16)
        else:
            grad[0, slot] = value

    def far_copy(k, q):
        return copy("far", QS * k + q, out_buf.at[k, 2, rows(q)], far_in.at[k, rows(q)], ring(k, 1 if q < 4 else 3))

    def next_copy(k, q):
        return copy("to_next", QS * k + q, out_buf.at[k, 3, rows(q)], near_in.at[k, 0, rows(q)], ring(k, 1))

    def prev_copy(k, q):
        return copy("to_prev", QS * k + q, out_buf.at[k, 1, rows(q)], near_in.at[k, 1, rows(q)], ring(k, 3))

    def extra_of(slot, q):
        if (slot, q) in ((3, 6), (3, 7), (1, 0), (1, 1)):
            return {(3, 6): 0, (3, 7): 1, (1, 0): 2, (1, 1): 3}[slot, q]
        return None

    def extra_back(n):
        return copy("y_extra", n, extra_out.at[rows(n)], extra_in.at[rows(n)], y_down)

    def send_far(k):
        for q in (0, 4, 1, 5, 2, 6, 3, 7):
            far_copy(k, q).start()

    def send_extra(slot):
        for q in range(QS):
            n = extra_of(slot, q)
            if n is not None:
                extra_out[rows(n), :] = grad[1, slot, rows(q), :].astype(BF16)
                extra_back(n).start()

    def send_near(k, slot, order, make):
        for q in order:
            n = extra_of(slot, q)
            if n is not None and k == 1:
                continue
            term = grad[k, slot, rows(q), :]
            if (q < 4) == (slot == 3):
                arrived("far", QS * k + q, far_in.at[k, rows(q)])
                term += far_in[k, rows(q), :].astype(F32)
            if n is not None:
                arrived("y_extra", n, extra_in.at[rows(n)])
                term += extra_in[rows(n), :].astype(F32)
            out_buf[k, slot, rows(q), :] = term.astype(BF16)
            make(k, q).start()

    def reduced(k, q):
        total = grad[k, 0, rows(q), :]
        if k == 0 or extra_of(3, q) is None:
            arrived("to_next", QS * k + q, near_in.at[k, 0, rows(q)])
            total += near_in[k, 0, rows(q), :].astype(F32)
        if k == 0 or extra_of(1, q) is None:
            arrived("to_prev", QS * k + q, near_in.at[k, 1, rows(q)])
            total += near_in[k, 1, rows(q), :].astype(F32)
        return total

    def back_copy(q):
        return copy("y_back", q, y_out.at[rows(q)], y_in.at[rows(q)], y_down)

    def send_back(order):
        for q in order:
            y_out[rows(q), :] = reduced(1, q).astype(BF16)
            back_copy(q).start()

    far_terms(("0", "2", "early"), False)
    core_got(1, 2, 3)
    core_got(3, 0, 1)
    unit("2", "late")
    far_terms(("late",), True)
    send_far(1)
    for q in (2, 6, 3, 7):
        got_next(1, q)
    for q in (2, 6, 3, 7):
        got_prev(1, q)
    unit("late", "2")
    give(2)
    unit("late", "0")
    unit("late", "early")
    unit("late", "late")
    unit("early", "late")
    keep(2)
    send_far(0)
    other_terms(3)
    send_extra(3)
    send_near(1, 3, (4, 5), next_copy)
    other_terms(1)
    send_extra(1)
    send_near(1, 1, (2, 3), prev_copy)
    send_near(1, 3, (0, 1, 2, 3), next_copy)
    send_near(1, 1, (4, 5, 6, 7), prev_copy)
    unit("0", "late")
    give(3)
    give(1)
    other_terms(0)
    keep(3)
    send_near(0, 3, (4, 5), next_copy)
    keep(1)
    send_near(0, 1, (2, 3), prev_copy)
    send_back(BACK_ORDER[:2])
    for n in range(4):
        send_near(0, 3, (n,), next_copy)
        send_near(0, 1, (n + 4,), prev_copy)
    send_near(0, 3, (6, 7), next_copy)
    send_near(0, 1, (0, 1), prev_copy)
    send_back(BACK_ORDER[2:4])
    give(0)
    send_back(BACK_ORDER[4:6])
    keep(0)
    send_back(BACK_ORDER[6:])

    def rg_copy(q):
        return copy("rg", q, rg_theirs.at[rows(q)], rg_mine.at[pl.ds(ROWS + CHUNK * q, CHUNK)], partner)

    for q in BACK_ORDER:
        total = reduced(0, q)
        arrived("y_back", q, y_in.at[rows(q)])
        emb_grad = temper * (total + y_in[rows(q), :].astype(F32))
        scale = inv[rows(q), 0:1]
        unit_rows = raw[rows(q), :] * scale
        along = jnp.sum(unit_rows * emb_grad, axis=1, keepdims=True)
        value = ((emb_grad - unit_rows * along) * scale).astype(BF16)
        rg[rows(q), :] = value
        low, high = value[:, :HALF], value[:, HALF:]
        rg_mine[rows(q), :] = jnp.where(core == 0, low, high)
        rg_theirs[rows(q), :] = jnp.where(core == 0, high, low)
        rg_copy(q).start()

    for q in range(QS):
        arrived("rg", q, rg_mine.at[pl.ds(ROWS + CHUNK * q, CHUNK)])

    def part_of(n, d):
        at = pl.multiple_of(lax.rem((px if n else pz) + d, 4) * FEAT_Z, FEAT_Z)
        return dot((s_x if n else s_t)[pl.ds(at, FEAT_Z), :], rg_mine[:, pl.ds(256 * n, 256)], NN)

    def st_copy(n, h, d):
        return copy("st", 8 * n + 4 * h + d, st_out.at[n, h, d], st_in.at[n, h, d], ring_x(d) if n else ring_z(d))

    for d in (2, 1, 3):
        for n in range(2):
            value = part_of(n, d).astype(BF16)
            for h in range(2):
                st_out[n, h, d] = value[:, 128 * h : 128 * h + 128]
            st_copy(n, 0, d).start()
    for d in (2, 1, 3):
        for n in range(2):
            st_copy(n, 1, d).start()
    for n in range(2):
        value = part_of(n, 0)
        for h in range(2):
            st_sum[n, h] = value[:, 128 * h : 128 * h + 128]

    @pl.loop(0, FEAT // 256)
    def _(n):
        here = pl.ds(pl.multiple_of(n * 256, 256), 256)
        sg_ref[:, here] = dot(rg[...], w_ref[here, :], NT).astype(BF16)

    def group(n, h, dy, d):
        y = jnp.where(dy == 0, yh, 1 - yh)
        g = y * 4 + lax.rem(px + d, 4) if n == 0 else lax.rem(pz + d, 4) * 2 + y
        return st_sum[n, h, pl.ds(pl.multiple_of(g * OWN_ROWS, 8), OWN_ROWS), :]

    def end_copy(n, h, k):
        m = 16 * n + 8 * h + k
        return copy("end", m, end_out.at[n, h, k], end_in.at[n, h, k], plane(n, k // 4, k % 4))

    pad = jnp.zeros((PADDED - OWN_ROWS, 128), F32)
    for h in range(2):
        for n in range(2):
            for d in (1, 3, 2):
                arrived("st", 8 * n + 4 * h + d, st_in.at[n, h, d])
            st_sum[n, h] += (
                st_in[n, h, 1].astype(F32) + st_in[n, h, 2].astype(F32) + st_in[n, h, 3].astype(F32)
            )
            for k in (6, 5, 7, 4, 2, 1, 3):
                value = jnp.concatenate([group(n, h, k // 4, k % 4), pad], axis=0)
                end_out[n, h, k] = value.astype(BF16)
                end_copy(n, h, k).start()

    def finished(n, h):
        total = group(n, h, 0, 0)
        for k in (1, 3, 2, 4, 5, 7, 6):
            arrived("end", 16 * n + 8 * h + k, end_in.at[n, h, k])
            total += end_in[n, h, k].astype(F32)[:OWN_ROWS]
        return total

    quarters = {(n, h): finished(n, h) for h in range(2) for n in range(2)}
    p_fin = jnp.concatenate([quarters[0, 0], quarters[0, 1]], axis=1)
    q_fin = jnp.concatenate([quarters[1, 0], quarters[1, 1]], axis=1)
    both = jnp.concatenate([p_fin, q_fin], axis=1)
    first, second = both[:20], both[20:]
    theirs = jnp.where(core == 0, second, first)
    mine = jnp.where(core == 0, first, second)
    last_out[...] = jnp.concatenate([theirs, jnp.zeros((4, HALF), F32)], axis=0)
    copy("last", 0, last_out, last_in, partner).start()
    arrived("last", 0, last_in)
    got = last_in[:20, :]
    pg_ref[:, 0, :HALF] = jnp.where(core == 0, mine, got)
    pg_ref[:, 0, HALF:] = jnp.where(core == 0, got, mine)

    some = blocks.at[0]
    for q in range(QS):
        left("y", q, some.at[rows(q)])
        left("y_back", q, some.at[rows(q)])
        left("rg", q, rg_theirs.at[rows(q)])
    left("y_id", 0, ids.at[0])
    for k in range(2):
        for q in range(QS):
            left("ring", 3 * QS * k + q, some.at[rows(0)])
            left("ring", 3 * QS * k + QS + q, some.at[rows(0)])
            if k == 0 or q not in EXTRA:
                left("ring", 3 * QS * k + 2 * QS + q, some.at[rows(0)])
            left("far", QS * k + q, some.at[rows(0)])
            if k == 0 or extra_of(3, q) is None:
                left("to_next", QS * k + q, some.at[rows(0)])
            if k == 0 or extra_of(1, q) is None:
                left("to_prev", QS * k + q, some.at[rows(0)])
    for n in range(6):
        left("ring_id", n, ids.at[0])
    for n in range(4):
        for m in range(4):
            left("core", 4 * n + m, some.at[pl.ds(0, 2 * CHUNK)])
        left("core_id", n, ids.at[0])
        left("part", n, some)
        left("extra", n, some.at[rows(0)])
        left("y_extra", n, some.at[rows(0)])
    left("core_s", 0, s_other)
    for n in range(2):
        for h in range(2):
            for d in (1, 2, 3):
                left("st", 8 * n + 4 * h + d, st_out.at[n, h, d])
            for k in range(1, 8):
                left("end", 16 * n + 8 * h + k, end_out.at[n, h, k])
    left("last", 0, last_out)


def local(states, projection, prompt_ids, log_temper, logit_offset):
    vmem = pl.BlockSpec(memory_space=pltpu.VMEM)
    hbm = pl.BlockSpec(memory_space=pl.ANY)
    scratch = [
        ((ROWS, FEAT), BF16),
        ((FEAT, EMB), BF16),
        ((4, ROWS, 128), F32),
        ((1, ROWS), jnp.int32),
        None,
        None,
        ((12, ROWS, EMB), BF16),
        ((12, 8, ROWS), jnp.int32),
        ((ROWS, EMB), F32),
        ((ROWS, 128), F32),
        ((4 * ROWS, 8 * ROWS), BF16),
        ((2, 4, ROWS, EMB), F32),
        ((2, 4, ROWS, EMB), BF16),
        ((2, ROWS, EMB), BF16),
        ((2, 2, ROWS, EMB), BF16),
        ((4 * CHUNK, EMB), BF16),
        ((4 * CHUNK, EMB), BF16),
        ((4, ROWS, EMB), BF16),
        ((4, ROWS, EMB), BF16),
        ((ROWS, EMB), BF16),
        ((ROWS, EMB), BF16),
        ((ROWS, EMB), BF16),
        ((2 * ROWS, HALF), BF16),
        ((ROWS, HALF), BF16),
        ((ROWS, FEAT), BF16),
        ((FEAT, 2 * ROWS), BF16),
        ((FEAT, 2 * ROWS), BF16),
        ((FEAT, ROWS), F32),
        ((2, 2, 4, FEAT_Z, 128), BF16),
        ((2, 2, 4, FEAT_Z, 128), BF16),
        ((2, 2, FEAT_Z, 128), F32),
        ((2, 2, 8, PADDED, 128), BF16),
        ((2, 2, 8, PADDED, 128), BF16),
        ((24, HALF), F32),
        ((24, HALF), F32),
    ]
    state_grad, owned = pl.pallas_call(
        kernel,
        out_shape=(
            pltpu.VMEM((ROWS, FEAT), BF16),
            pltpu.VMEM((20, 1, EMB), F32),
        ),
        in_specs=[hbm] * 5,
        out_specs=(vmem, vmem),
        scratch_shapes=[pltpu.VMEM(*what) if what else pltpu.SMEM((1,), F32) for what in scratch]
        + [pltpu.SemaphoreType.DMA((4 + QUARTERS,))]
        + [pltpu.SemaphoreType.DMA((Sems.total(),)), pltpu.SemaphoreType.DMA((Sems.total(),))],
        compiler_params=pltpu.CompilerParams(
            collective_id=0, has_side_effects=True, vmem_limit_bytes=60 * 2**20
        ),
        name="contrast",
    )(states[0], projection[0], prompt_ids.reshape(1, ROWS), log_temper, logit_offset)
    return state_grad[None], owned.reshape(1, 20, EMB)


def solution(mesh):
    return jax.shard_map(
        local,
        mesh=mesh,
        in_specs=(P("tower", "batch", None), P("tower", None, None), P("batch"), P(), P()),
        out_specs=(P("tower", "batch", None), P("tower", "batch", None)),
        check_vma=False,
    )
```

```python
import jax
import jax.numpy as jnp
from jax import lax
from jax.experimental import pallas as pl
from jax.experimental.pallas import tpu as pltpu
from jax.sharding import PartitionSpec as P

EPSILON = 1e-06
MESH = pl.DeviceIdType.MESH
F32, BF16 = jnp.float32, jnp.bfloat16
NT = (((1,), (1,)), ((), ()))
TN = (((0,), (0,)), ((), ()))
NN = (((1,), (0,)), ((), ()))

ROWS = 256
EMB = 1024
FEAT = 1280
CHUNK = 32
QS = ROWS // CHUNK
HALF = EMB // 2
QUARTERS = 4
FEAT_Z = FEAT // 4
OWN_ROWS = 40
PADDED = 48
OTHER0 = 8

Y_ORDER = (0, 4, 1, 5, 2, 6, 3, 7)
NEXT_ORDER = (2, 3, 0, 1, 6, 7, 4, 5)
PREV_ORDER = (6, 7, 4, 5, 2, 3, 0, 1)
EXTRA = (2, 6, 3, 7)


class Sems:
    sizes = dict(
        y=QS, y_id=1, ring=2 * 3 * QS, ring_id=2 * 3, core=16, core_id=4, core_s=1, extra=4,
        part=4, far=2 * QS, to_next=2 * QS, to_prev=2 * QS, y_extra=4, y_back=QS,
        rg=QS, st=16, end=32, last=1,
    )

    @classmethod
    def at(cls, name, index=0):
        base = 0
        for key, size in cls.sizes.items():
            if key == name:
                return base + index
            base += size
        raise KeyError(name)

    @classmethod
    def total(cls):
        return sum(cls.sizes.values())


def dot(a, b, dims):
    return lax.dot_general(a, b, dims, preferred_element_type=F32)


def kernel(
    s_hbm, w_hbm, id_hbm, lt_hbm, of_hbm, sg_ref, pg_ref,
    s_ref, w_ref, cols, id_ref, lt_ref, of_ref, blocks, ids, raw, inv, pair, grad, out_buf, far_in, near_in, extra_out, extra_in, part_out, part_in, y_out, y_in,
    rg, rg_mine, rg_theirs, s_other, s_t, s_x, tall, st_out, st_in, st_sum, end_out, end_in, last_out, last_in,
    lsem, ssem, rsem,
):
    tower = lax.axis_index("tower")
    batch = lax.axis_index("batch")
    core = lax.rem(batch, 2)
    px = lax.rem(batch // 2, 4)
    yh = lax.rem(batch // 8, 2)
    pz = batch // 16
    other = 1 - tower

    def dev(t, z, y, x, c):
        return (t, ((z * 2 + y) * 4 + x) * 2 + c)

    def ring_x(d):
        return dev(tower, pz, yh, lax.rem(px + d, 4), core)

    def ring_z(d):
        return dev(tower, lax.rem(pz + d, 4), yh, px, core)

    def ring(k, d):
        r = tower if k == 0 else other
        return dev(tower, lax.rem(pz + r * d, 4), yh, lax.rem(px + (1 - r) * d, 4), core)

    partner = dev(tower, pz, yh, px, 1 - core)
    y_up = dev(other, pz, jnp.where(tower == 1, 1 - yh, yh), px, core)
    y_down = dev(other, pz, jnp.where(tower == 0, 1 - yh, yh), px, core)

    def plane(n, dy, d):
        x = lax.rem(px + d, 4) if n == 0 else px
        z = pz if n == 0 else lax.rem(pz + d, 4)
        return dev(tower, z, 1 - yh if dy else yh, x, core)

    def block(k, slot):
        return 2 * slot if k == 0 else OTHER0 + slot

    def copy(name, index, src, dst, where):
        n = Sems.at(name) + index
        return pltpu.make_async_remote_copy(
            src_ref=src, dst_ref=dst, send_sem=ssem.at[n], recv_sem=rsem.at[n],
            device_id=where, device_id_type=MESH,
        )

    def arrived(name, index, ref):
        copy(name, index, ref, ref, partner).wait_recv()

    def left(name, index, ref):
        copy(name, index, ref, ref, partner).wait_send()

    def rows(q):
        return pl.ds(CHUNK * q, CHUNK)

    def piece(k, slot, q):
        return blocks.at[block(k, slot), rows(q)]

    barrier = pltpu.get_barrier_semaphore()
    near = [partner, y_up, y_down] + [plane(n, 0, d) for n in range(2) for d in (1, 3)]
    for where in near:
        pl.semaphore_signal(barrier, inc=1, device_id=where, device_id_type=MESH)

    def halves(n):
        return pl.ds(n * HALF, HALF)

    def quarter(n):
        return pl.ds(n * (EMB // QUARTERS), EMB // QUARTERS)

    loads = [pltpu.make_async_copy(s_hbm, s_ref, lsem.at[0])]
    loads += [pltpu.make_async_copy(w_hbm.at[:, quarter(n)], w_ref.at[:, quarter(n)], lsem.at[1 + n]) for n in range(QUARTERS)]
    small = [(id_hbm, id_ref), (lt_hbm, lt_ref), (of_hbm, of_ref)]
    small = [pltpu.make_async_copy(src, dst, lsem.at[1 + QUARTERS + n]) for n, (src, dst) in enumerate(small)]
    for load in loads + small:
        load.start()
    small[0].wait()
    ids[0] = jnp.broadcast_to(id_ref[...], (8, ROWS))
    small[1].wait()
    small[2].wait()
    loads[0].wait()
    for n in range(QUARTERS):
        loads[1 + n].wait()
        raw[:, quarter(n)] = dot(s_ref[...], w_ref[:, quarter(n)], NN)

    pl.semaphore_wait(barrier, len(near))

    def to_next(k, q):
        return copy("ring", 3 * QS * k + q, piece(k, 0, q), piece(k, 1, q), ring(k, 1))

    def to_prev(k, q):
        return copy("ring", 3 * QS * k + QS + q, piece(k, 0, q), piece(k, 3, q), ring(k, 3))

    def onward(k, q):
        slot = 1 if q < QS // 2 else 3
        return copy("ring", 3 * QS * k + 2 * QS + q, piece(k, slot, q), piece(k, 2, q), ring(k, slot))

    def got_next(k, q):
        arrived("ring", 3 * QS * k + q, piece(k, 1, q))

    def got_prev(k, q):
        arrived("ring", 3 * QS * k + QS + q, piece(k, 3, q))

    def got_onward(k, q):
        arrived("ring", 3 * QS * k + 2 * QS + q, piece(k, 2, q))

    def extra(n):
        return copy("extra", n, piece(0, 2, EXTRA[n]), piece(1, 2, EXTRA[n]), y_up)

    def ids_out(k):
        copy("ring_id", 3 * k, ids.at[block(k, 0)], ids.at[block(k, 1)], ring(k, 1)).start()
        copy("ring_id", 3 * k + 1, ids.at[block(k, 0)], ids.at[block(k, 3)], ring(k, 3)).start()

    def ids_onward(k):
        arrived("ring_id", 3 * k, ids.at[block(k, 1)])
        copy("ring_id", 3 * k + 2, ids.at[block(k, 1)], ids.at[block(k, 2)], ring(k, 1)).start()
        arrived("ring_id", 3 * k + 1, ids.at[block(k, 3)])

    def core_copy(slot, n):
        there = pl.ds(2 * CHUNK * n, 2 * CHUNK)
        return copy("core", 4 * slot + n, blocks.at[2 * slot, there], blocks.at[2 * slot + 1, there], partner)

    def core_send(slot, *pieces):
        for n in pieces:
            core_copy(slot, n).start()

    def core_got(slot, *pieces):
        for n in pieces:
            arrived("core", 4 * slot + n, blocks.at[2 * slot + 1, pl.ds(2 * CHUNK * n, 2 * CHUNK)])

    def core_ids_got(slot):
        arrived("core_id", slot, ids.at[2 * slot + 1])

    def core_ids(slot):
        copy("core_id", slot, ids.at[2 * slot], ids.at[2 * slot + 1], partner).start()

    copy("y_id", 0, ids.at[0], ids.at[OTHER0], y_up).start()
    ids_out(0)
    def own_rows(q):
        part = raw[rows(q), :]
        length = jnp.sqrt(jnp.sum(part * part, axis=1, keepdims=True) + EPSILON)
        scale = 1.0 / length
        inv[rows(q), :] = jnp.broadcast_to(scale, (CHUNK, 128))
        blocks[0, rows(q)] = (part * scale).astype(BF16)

    def y_send(q):
        copy("y", q, piece(0, 0, q), piece(1, 0, q), y_up).start()

    for q in (0, 1):
        own_rows(q)
        y_send(q)
        own_rows(q + 2)
        to_next(0, q + 2).start()
        own_rows(q + 4)
        y_send(q + 4)
        own_rows(q + 6)
        to_prev(0, q + 6).start()
    for q in EXTRA:
        y_send(q)
    for q in (0, 1, 6):
        to_next(0, q).start()
    for q in (4, 5, 2):
        to_prev(0, q).start()
    core_send(0, 0, 1, 2, 3)
    core_ids(0)

    def turn(states, first):
        tall[...] = states[...].astype(F32).T
        here = pl.ds(first, ROWS)
        s_t[:, here] = tall[...].astype(BF16)
        for x in range(4):
            pieces = [tall[pl.ds((4 * k + x) * OWN_ROWS, OWN_ROWS), :] for k in range(8)]
            s_x[pl.ds(x * FEAT_Z, FEAT_Z), here] = jnp.concatenate(pieces, axis=0).astype(BF16)

    copy("core_s", 0, s_ref, s_other, partner).start()
    turn(s_ref, 0)

    temper = jnp.exp(jnp.full((1, 1), lt_ref[0], F32))
    slope = 0.5 * temper
    shift = jnp.full((1, 1), 0.5 * of_ref[0], F32)

    def id_columns(slot):
        cols[slot] = jnp.broadcast_to(ids[OTHER0 + slot, 0:1, :].astype(F32), (128, ROWS)).T

    other_rows = {
        "0": [(0, 0, 256)],
        "2": [(2, 0, 256)],
        "early": [(1, 0, 64), (1, 128, 64), (3, 0, 64), (3, 128, 64)],
        "late": [(1, 64, 64), (1, 192, 64), (3, 64, 64), (3, 192, 64)],
    }
    own_rows_of = {
        "0": [(0, 0, 0, 256), (0, 1, 0, 256)],
        "2": [(2, 0, 0, 256), (2, 1, 0, 256)],
        "early": [(1, 0, 0, 128), (1, 1, 0, 128), (3, 0, 128, 128), (3, 1, 128, 128)],
        "late": [(1, 0, 128, 128), (1, 1, 128, 128), (3, 0, 0, 128), (3, 1, 0, 128)],
    }

    def joined(parts, axis):
        return parts[0] if len(parts) == 1 else jnp.concatenate(parts, axis=axis)

    def unit(a, b):
        left_side, right_side = other_rows[a], own_rows_of[b]
        rest = joined([blocks[OTHER0 + n, pl.ds(at, size)] for n, at, size in left_side], 0)
        own = joined([blocks[2 * n + c, pl.ds(at, size)] for n, c, at, size in right_side], 0)
        logit = dot(rest, own, NT)
        value = jnp.tanh(logit * slope + shift) * 8.0
        row = joined([ids[2 * n + c, 0:1, pl.ds(at, size)] for n, c, at, size in right_side], 1).astype(F32)
        col = joined([cols[n, pl.ds(at, size)] for n, at, size in left_side], 0)
        same = jnp.concatenate([col] * 4, axis=1) == row
        value = (value + jnp.where(same, -8.0, 8.0)).astype(BF16)
        first = 0
        for n, at, size in left_side:
            begin = 0
            for m, c, start, width in right_side:
                pair[pl.ds(n * ROWS + at, size), pl.ds((2 * m + c) * ROWS + start, width)] = value[
                    first : first + size, begin : begin + width
                ]
                begin += width
            first += size

    def y_got(m):
        q = Y_ORDER[m]
        arrived("y", q, piece(1, 0, q))
        to_next(1, q).start()
        to_prev(1, q).start()

    def own_on(m):
        for q, got in ((NEXT_ORDER[m], got_next), (PREV_ORDER[m], got_prev)):
            got(0, q)
            onward(0, q).start()

    def other_on(q):
        (got_next if q < 4 else got_prev)(1, q)
        onward(1, q).start()

    def far_on(n):
        got_onward(0, EXTRA[n])
        extra(n).start()

    def own_terms(half, slot):
        rest = blocks[pl.ds(OTHER0, 4)].reshape(4 * ROWS, EMB)
        return dot(pair[:, pl.ds((2 * slot + half) * ROWS, ROWS)], rest, TN)

    def other_terms(slot):
        for n in range(2):
            cols = halves(n)
            own = blocks[pl.ds(0, 8), :, cols].reshape(8 * ROWS, HALF)
            grad[1, slot, :, cols] = dot(pair[pl.ds(slot * ROWS, ROWS), :], own, NN)

    def far_terms(names, last):
        what = [one for name in names for one in own_rows_of[name]]
        terms = joined([pair[pl.ds(2 * ROWS, ROWS), pl.ds((2 * m + c) * ROWS + at, size)] for m, c, at, size in what], 1)
        for n in range(2):
            own = joined([blocks[2 * m + c, pl.ds(at, size), halves(n)] for m, c, at, size in what], 0)
            value = dot(terms, own, NN)
            if last:
                out_buf[1, 2, :, halves(n)] = (grad[1, 2, :, halves(n)] + value).astype(BF16)
            else:
                grad[1, 2, :, halves(n)] = value

    def give(slot):
        part_out[slot] = own_terms(1, slot).astype(BF16)
        copy("part", slot, part_out.at[slot], part_in.at[slot], partner).start()

    def keep(slot):
        arrived("part", slot, part_in.at[slot])
        value = own_terms(0, slot) + part_in[slot].astype(F32)
        if slot == 2:
            out_buf[0, 2] = value.astype(BF16)
        else:
            grad[0, slot] = value

    def far_copy(k, q):
        return copy("far", QS * k + q, out_buf.at[k, 2, rows(q)], far_in.at[k, rows(q)], ring(k, 1 if q < 4 else 3))

    def next_copy(k, q):
        return copy("to_next", QS * k + q, out_buf.at[k, 3, rows(q)], near_in.at[k, 0, rows(q)], ring(k, 1))

    def prev_copy(k, q):
        return copy("to_prev", QS * k + q, out_buf.at[k, 1, rows(q)], near_in.at[k, 1, rows(q)], ring(k, 3))

    def extra_of(slot, q):
        if (slot, q) in ((3, 6), (3, 7), (1, 0), (1, 1)):
            return {(3, 6): 0, (3, 7): 1, (1, 0): 2, (1, 1): 3}[slot, q]
        return None

    def extra_back(n):
        return copy("y_extra", n, extra_out.at[rows(n)], extra_in.at[rows(n)], y_down)

    def send_far(k):
        for q in (0, 4, 1, 5, 2, 6, 3, 7):
            far_copy(k, q).start()

    def send_extra(slot):
        for q in range(QS):
            n = extra_of(slot, q)
            if n is not None:
                extra_out[rows(n), :] = grad[1, slot, rows(q), :].astype(BF16)
                extra_back(n).start()

    def send_near(k, slot, order, make):
        for q in order:
            n = extra_of(slot, q)
            if n is not None and k == 1:
                continue
            term = grad[k, slot, rows(q), :]
            if (q < 4) == (slot == 3):
                arrived("far", QS * k + q, far_in.at[k, rows(q)])
                term += far_in[k, rows(q), :].astype(F32)
            if n is not None:
                arrived("y_extra", n, extra_in.at[rows(n)])
                term += extra_in[rows(n), :].astype(F32)
            out_buf[k, slot, rows(q), :] = term.astype(BF16)
            make(k, q).start()

    def reduced(k, q):
        total = grad[k, 0, rows(q), :]
        if k == 0 or extra_of(3, q) is None:
            arrived("to_next", QS * k + q, near_in.at[k, 0, rows(q)])
            total += near_in[k, 0, rows(q), :].astype(F32)
        if k == 0 or extra_of(1, q) is None:
            arrived("to_prev", QS * k + q, near_in.at[k, 1, rows(q)])
            total += near_in[k, 1, rows(q), :].astype(F32)
        return total

    def back_copy(q):
        return copy("y_back", q, y_out.at[rows(q)], y_in.at[rows(q)], y_down)

    def send_back(order):
        for q in order:
            y_out[rows(q), :] = reduced(1, q).astype(BF16)
            back_copy(q).start()

    def rg_copy(q):
        return copy("rg", q, rg_theirs.at[rows(q)], rg_mine.at[pl.ds(ROWS + CHUNK * q, CHUNK)], partner)

    def finish(q):
        total = reduced(0, q)
        arrived("y_back", q, y_in.at[rows(q)])
        emb_grad = temper * (total + y_in[rows(q), :].astype(F32))
        scale = inv[rows(q), 0:1]
        unit_rows = raw[rows(q), :] * scale
        along = jnp.sum(unit_rows * emb_grad, axis=1, keepdims=True)
        value = ((emb_grad - unit_rows * along) * scale).astype(BF16)
        rg[rows(q), :] = value
        low, high = value[:, :HALF], value[:, HALF:]
        rg_mine[rows(q), :] = jnp.where(core == 0, low, high)
        rg_theirs[rows(q), :] = jnp.where(core == 0, high, low)
        rg_copy(q).start()

    arrived("y_id", 0, ids.at[OTHER0])
    ids_out(1)
    y_got(0)
    y_got(1)
    y_got(2)
    ids_onward(1)
    own_on(0)
    ids_onward(0)
    own_on(3)
    y_got(3)
    y_got(4)
    own_on(1)
    y_got(5)
    own_on(2)
    core_send(1, 0, 1)
    core_send(3, 2, 3)
    y_got(6)
    to_next(0, 5).start()
    to_prev(0, 1).start()
    to_next(0, 4).start()
    far_on(0)
    far_on(3)
    got_onward(0, 5)
    far_on(1)
    y_got(7)
    core_ids(1)
    core_ids(3)
    core_got(0, 0, 1, 2, 3)
    to_next(0, 7).start()
    got_onward(0, 1)
    core_got(3, 2, 3)
    got_next(1, 4)
    got_next(1, 5)
    got_prev(1, 0)
    got_prev(1, 1)
    other_on(5)
    to_prev(0, 0).start()
    other_on(4)
    other_on(1)
    arrived("core_s", 0, s_other)
    turn(s_other, ROWS)
    id_columns(1)
    id_columns(3)
    core_ids_got(1)
    core_ids_got(3)
    core_got(1, 0, 1)
    got_onward(0, 0)
    id_columns(0)
    core_ids_got(0)
    far_on(2)
    other_on(0)
    got_onward(0, 4)
    unit("0", "early")
    arrived("ring_id", 2, ids.at[block(0, 2)])
    core_ids(2)
    core_send(2, 1, 3)
    core_send(2, 0, 2)
    to_prev(0, 3).start()
    unit("early", "early")
    unit("0", "0")
    unit("early", "0")
    core_ids_got(2)
    core_got(2, 0, 1, 2, 3)
    got_next(1, 2)
    got_prev(1, 2)
    got_next(1, 6)
    got_prev(1, 6)
    got_next(1, 3)
    got_prev(1, 3)
    got_next(1, 7)
    got_prev(1, 7)
    got_prev(0, 0)
    got_prev(0, 1)
    core_send(3, 0)
    unit("late", "2")
    unit("late", "early")
    unit("late", "0")
    unit("0", "2")
    got_prev(0, 2)
    got_prev(0, 3)
    core_send(3, 1)
    got_next(0, 4)
    got_next(0, 5)
    core_send(1, 2)
    unit("early", "2")
    arrived("ring_id", 5, ids.at[block(1, 2)])
    id_columns(2)
    got_next(0, 6)
    got_next(0, 7)
    core_send(1, 3)
    arrived("extra", 0, piece(1, 2, EXTRA[0]))
    arrived("extra", 1, piece(1, 2, EXTRA[1]))
    arrived("extra", 2, piece(1, 2, EXTRA[2]))
    arrived("extra", 3, piece(1, 2, EXTRA[3]))
    got_onward(1, 0)
    got_onward(1, 4)
    got_onward(1, 1)
    got_onward(1, 5)
    unit("2", "2")
    unit("2", "early")
    unit("2", "0")
    far_terms(("0", "2", "early"), False)
    core_got(1, 2, 3)
    core_got(3, 0, 1)
    unit("2", "late")
    far_terms(("late",), True)
    send_far(1)
    give(2)
    unit("early", "late")
    unit("late", "late")
    other_terms(3)
    send_extra(3)
    keep(2)
    send_far(0)
    unit("0", "late")
    give(1)
    give(3)
    send_near(1, 3, (1,), next_copy)
    other_terms(1)
    send_extra(1)
    send_near(1, 3, (0,), next_copy)
    send_near(1, 1, (6,), prev_copy)
    other_terms(0)
    send_near(1, 1, (7,), prev_copy)
    keep(1)
    keep(3)
    send_near(0, 1, (2,), prev_copy)
    send_near(0, 3, (4,), next_copy)
    send_back((1,))
    send_near(1, 3, (2,), next_copy)
    send_near(1, 1, (2,), prev_copy)
    send_near(1, 3, (5,), next_copy)
    send_near(0, 1, (4,), prev_copy)
    send_near(1, 1, (5,), prev_copy)
    send_near(0, 3, (0,), next_copy)
    send_near(0, 1, (5,), prev_copy)
    send_back((6,))
    send_near(1, 3, (4,), next_copy)
    send_near(0, 1, (0,), prev_copy)
    send_near(0, 3, (2,), next_copy)
    give(0)
    send_near(0, 3, (5,), next_copy)
    send_near(0, 3, (1,), next_copy)
    send_near(0, 1, (1,), prev_copy)
    send_near(1, 1, (4,), prev_copy)
    send_near(1, 3, (3,), next_copy)
    send_near(0, 3, (7,), next_copy)
    send_back((0,))
    send_back((7,))
    keep(0)
    send_near(0, 3, (6,), next_copy)
    send_back((2,))
    send_near(0, 3, (3,), next_copy)
    send_near(1, 1, (3,), prev_copy)
    send_near(0, 1, (6,), prev_copy)
    send_near(0, 1, (7,), prev_copy)
    send_near(0, 1, (3,), prev_copy)
    send_back((5,))
    send_back((4,))
    send_back((3,))
    finish(1)
    finish(2)
    finish(6)
    finish(0)
    finish(4)
    finish(7)
    finish(5)
    finish(3)

    for q in range(QS):
        arrived("rg", q, rg_mine.at[pl.ds(ROWS + CHUNK * q, CHUNK)])

    def part_of(n, d):
        at = pl.multiple_of(lax.rem((px if n else pz) + d, 4) * FEAT_Z, FEAT_Z)
        return dot((s_x if n else s_t)[pl.ds(at, FEAT_Z), :], rg_mine[:, pl.ds(256 * n, 256)], NN)

    def st_copy(n, h, d):
        return copy("st", 8 * n + 4 * h + d, st_out.at[n, h, d], st_in.at[n, h, d], ring_x(d) if n else ring_z(d))

    for d in (2, 1, 3):
        for n in range(2):
            value = part_of(n, d).astype(BF16)
            for h in range(2):
                st_out[n, h, d] = value[:, 128 * h : 128 * h + 128]
            st_copy(n, 0, d).start()
    for d in (2, 1, 3):
        for n in range(2):
            st_copy(n, 1, d).start()
    for n in range(2):
        value = part_of(n, 0)
        for h in range(2):
            st_sum[n, h] = value[:, 128 * h : 128 * h + 128]

    @pl.loop(0, FEAT // 256)
    def _(n):
        here = pl.ds(pl.multiple_of(n * 256, 256), 256)
        sg_ref[:, here] = dot(rg[...], w_ref[here, :], NT).astype(BF16)

    def group(n, h, dy, d):
        y = jnp.where(dy == 0, yh, 1 - yh)
        g = y * 4 + lax.rem(px + d, 4) if n == 0 else lax.rem(pz + d, 4) * 2 + y
        return st_sum[n, h, pl.ds(pl.multiple_of(g * OWN_ROWS, 8), OWN_ROWS), :]

    def end_copy(n, h, k):
        m = 16 * n + 8 * h + k
        return copy("end", m, end_out.at[n, h, k], end_in.at[n, h, k], plane(n, k // 4, k % 4))

    pad = jnp.zeros((PADDED - OWN_ROWS, 128), F32)
    for h in range(2):
        for n in range(2):
            for d in (1, 3, 2):
                arrived("st", 8 * n + 4 * h + d, st_in.at[n, h, d])
            st_sum[n, h] += (
                st_in[n, h, 1].astype(F32) + st_in[n, h, 2].astype(F32) + st_in[n, h, 3].astype(F32)
            )
            for k in (6, 5, 7, 4, 2, 1, 3):
                value = jnp.concatenate([group(n, h, k // 4, k % 4), pad], axis=0)
                end_out[n, h, k] = value.astype(BF16)
                end_copy(n, h, k).start()

    def finished(n, h):
        total = group(n, h, 0, 0)
        for k in (1, 3, 2, 4, 5, 7, 6):
            arrived("end", 16 * n + 8 * h + k, end_in.at[n, h, k])
            total += end_in[n, h, k].astype(F32)[:OWN_ROWS]
        return total

    quarters = {(n, h): finished(n, h) for h in range(2) for n in range(2)}
    p_fin = jnp.concatenate([quarters[0, 0], quarters[0, 1]], axis=1)
    q_fin = jnp.concatenate([quarters[1, 0], quarters[1, 1]], axis=1)
    both = jnp.concatenate([p_fin, q_fin], axis=1)
    first, second = both[:20], both[20:]
    theirs = jnp.where(core == 0, second, first)
    mine = jnp.where(core == 0, first, second)
    last_out[...] = jnp.concatenate([theirs, jnp.zeros((4, HALF), F32)], axis=0)
    copy("last", 0, last_out, last_in, partner).start()
    arrived("last", 0, last_in)
    got = last_in[:20, :]
    pg_ref[:, 0, :HALF] = jnp.where(core == 0, mine, got)
    pg_ref[:, 0, HALF:] = jnp.where(core == 0, got, mine)

    some = blocks.at[0]
    for q in range(QS):
        left("y", q, some.at[rows(q)])
        left("y_back", q, some.at[rows(q)])
        left("rg", q, rg_theirs.at[rows(q)])
    left("y_id", 0, ids.at[0])
    for k in range(2):
        for q in range(QS):
            left("ring", 3 * QS * k + q, some.at[rows(0)])
            left("ring", 3 * QS * k + QS + q, some.at[rows(0)])
            if k == 0 or q not in EXTRA:
                left("ring", 3 * QS * k + 2 * QS + q, some.at[rows(0)])
            left("far", QS * k + q, some.at[rows(0)])
            if k == 0 or extra_of(3, q) is None:
                left("to_next", QS * k + q, some.at[rows(0)])
            if k == 0 or extra_of(1, q) is None:
                left("to_prev", QS * k + q, some.at[rows(0)])
    for n in range(6):
        left("ring_id", n, ids.at[0])
    for n in range(4):
        for m in range(4):
            left("core", 4 * n + m, some.at[pl.ds(0, 2 * CHUNK)])
        left("core_id", n, ids.at[0])
        left("part", n, some)
        left("extra", n, some.at[rows(0)])
        left("y_extra", n, some.at[rows(0)])
    left("core_s", 0, s_other)
    for n in range(2):
        for h in range(2):
            for d in (1, 2, 3):
                left("st", 8 * n + 4 * h + d, st_out.at[n, h, d])
            for k in range(1, 8):
                left("end", 16 * n + 8 * h + k, end_out.at[n, h, k])
    left("last", 0, last_out)


def local(states, projection, prompt_ids, log_temper, logit_offset):
    vmem = pl.BlockSpec(memory_space=pltpu.VMEM)
    hbm = pl.BlockSpec(memory_space=pl.ANY)
    scratch = [
        ((ROWS, FEAT), BF16),
        ((FEAT, EMB), BF16),
        ((4, ROWS, 128), F32),
        ((1, ROWS), jnp.int32),
        None,
        None,
        ((12, ROWS, EMB), BF16),
        ((12, 8, ROWS), jnp.int32),
        ((ROWS, EMB), F32),
        ((ROWS, 128), F32),
        ((4 * ROWS, 8 * ROWS), BF16),
        ((2, 4, ROWS, EMB), F32),
        ((2, 4, ROWS, EMB), BF16),
        ((2, ROWS, EMB), BF16),
        ((2, 2, ROWS, EMB), BF16),
        ((4 * CHUNK, EMB), BF16),
        ((4 * CHUNK, EMB), BF16),
        ((4, ROWS, EMB), BF16),
        ((4, ROWS, EMB), BF16),
        ((ROWS, EMB), BF16),
        ((ROWS, EMB), BF16),
        ((ROWS, EMB), BF16),
        ((2 * ROWS, HALF), BF16),
        ((ROWS, HALF), BF16),
        ((ROWS, FEAT), BF16),
        ((FEAT, 2 * ROWS), BF16),
        ((FEAT, 2 * ROWS), BF16),
        ((FEAT, ROWS), F32),
        ((2, 2, 4, FEAT_Z, 128), BF16),
        ((2, 2, 4, FEAT_Z, 128), BF16),
        ((2, 2, FEAT_Z, 128), F32),
        ((2, 2, 8, PADDED, 128), BF16),
        ((2, 2, 8, PADDED, 128), BF16),
        ((24, HALF), F32),
        ((24, HALF), F32),
    ]
    state_grad, owned = pl.pallas_call(
        kernel,
        out_shape=(
            pltpu.VMEM((ROWS, FEAT), BF16),
            pltpu.VMEM((20, 1, EMB), F32),
        ),
        in_specs=[hbm] * 5,
        out_specs=(vmem, vmem),
        scratch_shapes=[pltpu.VMEM(*what) if what else pltpu.SMEM((1,), F32) for what in scratch]
        + [pltpu.SemaphoreType.DMA((4 + QUARTERS,))]
        + [pltpu.SemaphoreType.DMA((Sems.total(),)), pltpu.SemaphoreType.DMA((Sems.total(),))],
        compiler_params=pltpu.CompilerParams(
            collective_id=0, has_side_effects=True, vmem_limit_bytes=60 * 2**20
        ),
        name="contrast",
    )(states[0], projection[0], prompt_ids.reshape(1, ROWS), log_temper, logit_offset)
    return state_grad[None], owned.reshape(1, 20, EMB)


def solution(mesh):
    return jax.shard_map(
        local,
        mesh=mesh,
        in_specs=(P("tower", "batch", None), P("tower", None, None), P("batch"), P(), P()),
        out_specs=(P("tower", "batch", None), P("tower", "batch", None)),
        check_vma=False,
    )
```

```python
import jax
import jax.numpy as jnp
from jax import lax
from jax.experimental import pallas as pl
from jax.experimental.pallas import tpu as pltpu
from jax.sharding import PartitionSpec as P

EPSILON = 1e-06
MESH = pl.DeviceIdType.MESH
F32, BF16 = jnp.float32, jnp.bfloat16
NT = (((1,), (1,)), ((), ()))
TN = (((0,), (0,)), ((), ()))
NN = (((1,), (0,)), ((), ()))

ROWS = 256
EMB = 1024
FEAT = 1280
CHUNK = 32
QS = ROWS // CHUNK
HALF = EMB // 2
QUARTERS = 4
FEAT_Z = FEAT // 4
OWN_ROWS = 40
PADDED = 48
OTHER0 = 8

Y_ORDER = (0, 4, 1, 5, 2, 6, 3, 7)
NEXT_ORDER = (2, 3, 0, 1, 6, 7, 4, 5)
PREV_ORDER = (6, 7, 4, 5, 2, 3, 0, 1)
EXTRA = (2, 6, 3, 7)


class Sems:
    sizes = dict(
        y=QS, y_id=1, ring=2 * 3 * QS, ring_id=2 * 3, core=16, core_id=4, core_s=1, extra=4,
        part=4, far=2 * QS, to_next=2 * QS, to_prev=2 * QS, y_extra=4, y_back=QS,
        rg=QS, st=16, end=32, last=1,
    )

    @classmethod
    def at(cls, name, index=0):
        base = 0
        for key, size in cls.sizes.items():
            if key == name:
                return base + index
            base += size
        raise KeyError(name)

    @classmethod
    def total(cls):
        return sum(cls.sizes.values())


def dot(a, b, dims):
    return lax.dot_general(a, b, dims, preferred_element_type=F32)


def kernel(
    s_hbm, w_hbm, id_hbm, lt_hbm, of_hbm, sg_ref, pg_ref,
    s_ref, w_ref, cols, id_ref, lt_ref, of_ref, blocks, ids, raw, inv, pair, grad, out_buf, far_in, near_in, extra_out, extra_in, part_out, part_in, y_out, y_in,
    rg, rg_mine, rg_theirs, s_other, s_t, s_x, tall, st_out, st_in, st_sum, end_out, end_in, last_out, last_in,
    lsem, ssem, rsem,
):
    tower = lax.axis_index("tower")
    batch = lax.axis_index("batch")
    core = lax.rem(batch, 2)
    px = lax.rem(batch // 2, 4)
    yh = lax.rem(batch // 8, 2)
    pz = batch // 16
    other = 1 - tower

    def dev(t, z, y, x, c):
        return (t, ((z * 2 + y) * 4 + x) * 2 + c)

    def ring_x(d):
        return dev(tower, pz, yh, lax.rem(px + d, 4), core)

    def ring_z(d):
        return dev(tower, lax.rem(pz + d, 4), yh, px, core)

    def ring(k, d):
        r = tower if k == 0 else other
        return dev(tower, lax.rem(pz + r * d, 4), yh, lax.rem(px + (1 - r) * d, 4), core)

    partner = dev(tower, pz, yh, px, 1 - core)
    y_up = dev(other, pz, jnp.where(tower == 1, 1 - yh, yh), px, core)
    y_down = dev(other, pz, jnp.where(tower == 0, 1 - yh, yh), px, core)

    def plane(n, dy, d):
        x = lax.rem(px + d, 4) if n == 0 else px
        z = pz if n == 0 else lax.rem(pz + d, 4)
        return dev(tower, z, 1 - yh if dy else yh, x, core)

    def block(k, slot):
        return 2 * slot if k == 0 else OTHER0 + slot

    def copy(name, index, src, dst, where):
        n = Sems.at(name) + index
        return pltpu.make_async_remote_copy(
            src_ref=src, dst_ref=dst, send_sem=ssem.at[n], recv_sem=rsem.at[n],
            device_id=where, device_id_type=MESH,
        )

    def arrived(name, index, ref):
        copy(name, index, ref, ref, partner).wait_recv()

    def left(name, index, ref):
        copy(name, index, ref, ref, partner).wait_send()

    def rows(q):
        return pl.ds(CHUNK * q, CHUNK)

    def piece(k, slot, q):
        return blocks.at[block(k, slot), rows(q)]

    barrier = pltpu.get_barrier_semaphore()
    near = [partner, y_up, y_down] + [plane(n, 0, d) for n in range(2) for d in (1, 3)]
    for where in near:
        pl.semaphore_signal(barrier, inc=1, device_id=where, device_id_type=MESH)

    def halves(n):
        return pl.ds(n * HALF, HALF)

    def quarter(n):
        return pl.ds(n * (EMB // QUARTERS), EMB // QUARTERS)

    loads = [pltpu.make_async_copy(s_hbm, s_ref, lsem.at[0])]
    loads += [pltpu.make_async_copy(w_hbm.at[:, quarter(n)], w_ref.at[:, quarter(n)], lsem.at[1 + n]) for n in range(QUARTERS)]
    small = [(id_hbm, id_ref), (lt_hbm, lt_ref), (of_hbm, of_ref)]
    small = [pltpu.make_async_copy(src, dst, lsem.at[1 + QUARTERS + n]) for n, (src, dst) in enumerate(small)]
    for load in loads + small:
        load.start()
    small[0].wait()
    ids[0] = jnp.broadcast_to(id_ref[...], (8, ROWS))
    small[1].wait()
    small[2].wait()
    loads[0].wait()
    for n in range(QUARTERS):
        loads[1 + n].wait()
        raw[:, quarter(n)] = dot(s_ref[...], w_ref[:, quarter(n)], NN)

    pl.semaphore_wait(barrier, len(near))

    def to_next(k, q):
        return copy("ring", 3 * QS * k + q, piece(k, 0, q), piece(k, 1, q), ring(k, 1))

    def to_prev(k, q):
        return copy("ring", 3 * QS * k + QS + q, piece(k, 0, q), piece(k, 3, q), ring(k, 3))

    def onward(k, q):
        slot = 1 if q < QS // 2 else 3
        return copy("ring", 3 * QS * k + 2 * QS + q, piece(k, slot, q), piece(k, 2, q), ring(k, slot))

    def got_next(k, q):
        arrived("ring", 3 * QS * k + q, piece(k, 1, q))

    def got_prev(k, q):
        arrived("ring", 3 * QS * k + QS + q, piece(k, 3, q))

    def got_onward(k, q):
        arrived("ring", 3 * QS * k + 2 * QS + q, piece(k, 2, q))

    def extra(n):
        return copy("extra", n, piece(0, 2, EXTRA[n]), piece(1, 2, EXTRA[n]), y_up)

    def ids_out(k):
        copy("ring_id", 3 * k, ids.at[block(k, 0)], ids.at[block(k, 1)], ring(k, 1)).start()
        copy("ring_id", 3 * k + 1, ids.at[block(k, 0)], ids.at[block(k, 3)], ring(k, 3)).start()

    def ids_onward(k):
        arrived("ring_id", 3 * k, ids.at[block(k, 1)])
        copy("ring_id", 3 * k + 2, ids.at[block(k, 1)], ids.at[block(k, 2)], ring(k, 1)).start()
        arrived("ring_id", 3 * k + 1, ids.at[block(k, 3)])

    def core_copy(slot, n):
        there = pl.ds(2 * CHUNK * n, 2 * CHUNK)
        return copy("core", 4 * slot + n, blocks.at[2 * slot, there], blocks.at[2 * slot + 1, there], partner)

    def core_send(slot, *pieces):
        for n in pieces:
            core_copy(slot, n).start()

    def core_got(slot, *pieces):
        for n in pieces:
            arrived("core", 4 * slot + n, blocks.at[2 * slot + 1, pl.ds(2 * CHUNK * n, 2 * CHUNK)])

    def core_ids_got(slot):
        arrived("core_id", slot, ids.at[2 * slot + 1])

    def core_ids(slot):
        copy("core_id", slot, ids.at[2 * slot], ids.at[2 * slot + 1], partner).start()

    copy("y_id", 0, ids.at[0], ids.at[OTHER0], y_up).start()
    ids_out(0)
    def own_rows(q):
        part = raw[rows(q), :]
        length = jnp.sqrt(jnp.sum(part * part, axis=1, keepdims=True) + EPSILON)
        scale = 1.0 / length
        inv[rows(q), :] = jnp.broadcast_to(scale, (CHUNK, 128))
        blocks[0, rows(q)] = (part * scale).astype(BF16)

    def y_send(q):
        copy("y", q, piece(0, 0, q), piece(1, 0, q), y_up).start()

    for q in (0, 1):
        own_rows(q)
        y_send(q)
        own_rows(q + 2)
        to_next(0, q + 2).start()
        own_rows(q + 4)
        y_send(q + 4)
        own_rows(q + 6)
        to_prev(0, q + 6).start()
    for q in EXTRA:
        y_send(q)
    for q in (0, 1, 6):
        to_next(0, q).start()
    for q in (4, 5, 2):
        to_prev(0, q).start()
    core_send(0, 0, 1, 2, 3)
    core_ids(0)

    def turn(states, first):
        tall[...] = states[...].astype(F32).T
        here = pl.ds(first, ROWS)
        s_t[:, here] = tall[...].astype(BF16)
        for x in range(4):
            pieces = [tall[pl.ds((4 * k + x) * OWN_ROWS, OWN_ROWS), :] for k in range(8)]
            s_x[pl.ds(x * FEAT_Z, FEAT_Z), here] = jnp.concatenate(pieces, axis=0).astype(BF16)

    copy("core_s", 0, s_ref, s_other, partner).start()
    turn(s_ref, 0)

    temper = jnp.exp(jnp.full((1, 1), lt_ref[0], F32))
    slope = 0.5 * temper
    shift = jnp.full((1, 1), 0.5 * of_ref[0], F32)

    def id_columns(slot):
        cols[slot] = jnp.broadcast_to(ids[OTHER0 + slot, 0:1, :].astype(F32), (128, ROWS)).T

    other_rows = {
        "0": [(0, 0, 256)],
        "2": [(2, 0, 256)],
        "early": [(1, 0, 64), (1, 128, 64), (3, 0, 64), (3, 128, 64)],
        "late": [(1, 64, 64), (1, 192, 64), (3, 64, 64), (3, 192, 64)],
    }
    own_rows_of = {
        "0": [(0, 0, 0, 256), (0, 1, 0, 256)],
        "2": [(2, 0, 0, 256), (2, 1, 0, 256)],
        "early": [(1, 0, 0, 128), (1, 1, 0, 128), (3, 0, 128, 128), (3, 1, 128, 128)],
        "late": [(1, 0, 128, 128), (1, 1, 128, 128), (3, 0, 0, 128), (3, 1, 0, 128)],
    }

    def joined(parts, axis):
        return parts[0] if len(parts) == 1 else jnp.concatenate(parts, axis=axis)

    def unit(a, b):
        left_side, right_side = other_rows[a], own_rows_of[b]
        rest = joined([blocks[OTHER0 + n, pl.ds(at, size)] for n, at, size in left_side], 0)
        own = joined([blocks[2 * n + c, pl.ds(at, size)] for n, c, at, size in right_side], 0)
        logit = dot(rest, own, NT)
        value = jnp.tanh(logit * slope + shift) * 8.0
        row = joined([ids[2 * n + c, 0:1, pl.ds(at, size)] for n, c, at, size in right_side], 1).astype(F32)
        col = joined([cols[n, pl.ds(at, size)] for n, at, size in left_side], 0)
        same = jnp.concatenate([col] * 4, axis=1) == row
        value = (value + jnp.where(same, -8.0, 8.0)).astype(BF16)
        first = 0
        for n, at, size in left_side:
            begin = 0
            for m, c, start, width in right_side:
                pair[pl.ds(n * ROWS + at, size), pl.ds((2 * m + c) * ROWS + start, width)] = value[
                    first : first + size, begin : begin + width
                ]
                begin += width
            first += size

    def y_got(m):
        q = Y_ORDER[m]
        arrived("y", q, piece(1, 0, q))
        to_next(1, q).start()
        to_prev(1, q).start()

    def own_on(m):
        for q, got in ((NEXT_ORDER[m], got_next), (PREV_ORDER[m], got_prev)):
            got(0, q)
            onward(0, q).start()

    def other_on(q):
        (got_next if q < 4 else got_prev)(1, q)
        onward(1, q).start()

    def far_on(n):
        got_onward(0, EXTRA[n])
        extra(n).start()

    def own_terms(half, slot):
        rest = blocks[pl.ds(OTHER0, 4)].reshape(4 * ROWS, EMB)
        return dot(pair[:, pl.ds((2 * slot + half) * ROWS, ROWS)], rest, TN)

    def other_terms(slot):
        for n in range(2):
            cols = halves(n)
            own = blocks[pl.ds(0, 8), :, cols].reshape(8 * ROWS, HALF)
            grad[1, slot, :, cols] = dot(pair[pl.ds(slot * ROWS, ROWS), :], own, NN)

    def far_terms(names, last):
        what = [one for name in names for one in own_rows_of[name]]
        terms = joined([pair[pl.ds(2 * ROWS, ROWS), pl.ds((2 * m + c) * ROWS + at, size)] for m, c, at, size in what], 1)
        for n in range(2):
            own = joined([blocks[2 * m + c, pl.ds(at, size), halves(n)] for m, c, at, size in what], 0)
            value = dot(terms, own, NN)
            if last:
                out_buf[1, 2, :, halves(n)] = (grad[1, 2, :, halves(n)] + value).astype(BF16)
            else:
                grad[1, 2, :, halves(n)] = value

    def give(slot):
        part_out[slot] = own_terms(1, slot).astype(BF16)
        copy("part", slot, part_out.at[slot], part_in.at[slot], partner).start()

    def keep(slot):
        arrived("part", slot, part_in.at[slot])
        value = own_terms(0, slot) + part_in[slot].astype(F32)
        if slot == 2:
            out_buf[0, 2] = value.astype(BF16)
        else:
            grad[0, slot] = value

    def far_copy(k, q):
        return copy("far", QS * k + q, out_buf.at[k, 2, rows(q)], far_in.at[k, rows(q)], ring(k, 1 if q < 4 else 3))

    def next_copy(k, q):
        return copy("to_next", QS * k + q, out_buf.at[k, 3, rows(q)], near_in.at[k, 0, rows(q)], ring(k, 1))

    def prev_copy(k, q):
        return copy("to_prev", QS * k + q, out_buf.at[k, 1, rows(q)], near_in.at[k, 1, rows(q)], ring(k, 3))

    def extra_of(slot, q):
        if (slot, q) in ((3, 6), (3, 7), (1, 0), (1, 1)):
            return {(3, 6): 0, (3, 7): 1, (1, 0): 2, (1, 1): 3}[slot, q]
        return None

    def extra_back(n):
        return copy("y_extra", n, extra_out.at[rows(n)], extra_in.at[rows(n)], y_down)

    def send_far(k):
        for q in (0, 4, 1, 5, 2, 6, 3, 7):
            far_copy(k, q).start()

    def send_extra(slot):
        for q in range(QS):
            n = extra_of(slot, q)
            if n is not None:
                extra_out[rows(n), :] = grad[1, slot, rows(q), :].astype(BF16)
                extra_back(n).start()

    def send_near(k, slot, order, make):
        for q in order:
            n = extra_of(slot, q)
            if n is not None and k == 1:
                continue
            term = grad[k, slot, rows(q), :]
            if (q < 4) == (slot == 3):
                arrived("far", QS * k + q, far_in.at[k, rows(q)])
                term += far_in[k, rows(q), :].astype(F32)
            if n is not None:
                arrived("y_extra", n, extra_in.at[rows(n)])
                term += extra_in[rows(n), :].astype(F32)
            out_buf[k, slot, rows(q), :] = term.astype(BF16)
            make(k, q).start()

    def reduced(k, q):
        total = grad[k, 0, rows(q), :]
        if k == 0 or extra_of(3, q) is None:
            arrived("to_next", QS * k + q, near_in.at[k, 0, rows(q)])
            total += near_in[k, 0, rows(q), :].astype(F32)
        if k == 0 or extra_of(1, q) is None:
            arrived("to_prev", QS * k + q, near_in.at[k, 1, rows(q)])
            total += near_in[k, 1, rows(q), :].astype(F32)
        return total

    def back_copy(q):
        return copy("y_back", q, y_out.at[rows(q)], y_in.at[rows(q)], y_down)

    def send_back(order):
        for q in order:
            y_out[rows(q), :] = reduced(1, q).astype(BF16)
            back_copy(q).start()

    def rg_copy(q):
        return copy("rg", q, rg_theirs.at[rows(q)], rg_mine.at[pl.ds(ROWS + CHUNK * q, CHUNK)], partner)

    def finish(q):
        total = reduced(0, q)
        arrived("y_back", q, y_in.at[rows(q)])
        emb_grad = temper * (total + y_in[rows(q), :].astype(F32))
        scale = inv[rows(q), 0:1]
        unit_rows = raw[rows(q), :] * scale
        along = jnp.sum(unit_rows * emb_grad, axis=1, keepdims=True)
        value = ((emb_grad - unit_rows * along) * scale).astype(BF16)
        rg[rows(q), :] = value
        low, high = value[:, :HALF], value[:, HALF:]
        rg_mine[rows(q), :] = jnp.where(core == 0, low, high)
        rg_theirs[rows(q), :] = jnp.where(core == 0, high, low)
        rg_copy(q).start()

    arrived("y_id", 0, ids.at[OTHER0])
    ids_out(1)
    y_got(0)
    y_got(1)
    ids_onward(1)
    core_got(0, 0, 1, 2, 3)
    own_on(1)
    ids_onward(0)
    own_on(0)
    own_on(2)
    y_got(2)
    own_on(3)
    core_ids(1)
    core_ids(3)
    y_got(3)
    core_send(3, 2, 3)
    y_got(4)
    y_got(5)
    to_next(0, 7).start()
    far_on(1)
    to_prev(0, 3).start()
    got_next(1, 4)
    got_next(1, 5)
    got_prev(1, 0)
    got_prev(1, 1)
    y_got(6)
    y_got(7)
    other_on(5)
    other_on(0)
    arrived("ring_id", 2, ids.at[block(0, 2)])
    core_ids(2)
    id_columns(0)
    core_ids_got(0)
    far_on(3)
    to_next(0, 4).start()
    far_on(2)
    id_columns(1)
    id_columns(3)
    core_ids_got(1)
    core_ids_got(3)
    far_on(0)
    core_got(3, 2, 3)
    to_next(0, 5).start()
    other_on(1)
    arrived("core_s", 0, s_other)
    turn(s_other, ROWS)
    got_onward(0, 0)
    other_on(4)
    core_send(1, 0, 1)
    to_prev(0, 1).start()
    unit("0", "0")
    core_send(2, 1, 3)
    got_onward(0, 1)
    got_onward(0, 4)
    got_onward(0, 5)
    to_prev(0, 0).start()
    core_send(2, 0, 2)
    core_got(1, 0, 1)
    unit("early", "early")
    got_next(0, 6)
    got_next(0, 7)
    core_send(1, 3)
    unit("0", "early")
    unit("early", "0")
    got_prev(0, 2)
    got_prev(0, 3)
    core_send(3, 1)
    arrived("ring_id", 5, ids.at[block(1, 2)])
    id_columns(2)
    core_ids_got(2)
    core_got(2, 0, 1, 2, 3)
    got_next(1, 2)
    got_prev(1, 2)
    got_next(1, 6)
    got_prev(1, 6)
    got_next(1, 3)
    got_prev(1, 3)
    got_next(1, 7)
    got_prev(1, 7)
    unit("early", "2")
    unit("late", "early")
    unit("late", "2")
    unit("0", "2")
    unit("late", "0")
    arrived("extra", 0, piece(1, 2, EXTRA[0]))
    arrived("extra", 1, piece(1, 2, EXTRA[1]))
    arrived("extra", 2, piece(1, 2, EXTRA[2]))
    arrived("extra", 3, piece(1, 2, EXTRA[3]))
    got_prev(0, 0)
    got_prev(0, 1)
    core_send(3, 0)
    got_next(0, 4)
    got_next(0, 5)
    core_send(1, 2)
    got_onward(1, 0)
    got_onward(1, 4)
    got_onward(1, 1)
    got_onward(1, 5)
    unit("2", "early")
    unit("2", "0")
    unit("2", "2")
    far_terms(("0", "2", "early"), False)
    give(2)
    core_got(1, 2, 3)
    core_got(3, 0, 1)
    unit("2", "late")
    far_terms(("late",), True)
    send_far(1)
    unit("0", "late")
    unit("early", "late")
    unit("late", "late")
    other_terms(3)
    send_extra(3)
    keep(2)
    send_far(0)
    give(3)
    send_near(1, 3, (0,), next_copy)
    give(1)
    other_terms(1)
    send_extra(1)
    send_near(1, 3, (1,), next_copy)
    send_near(1, 1, (6,), prev_copy)
    keep(3)
    other_terms(0)
    send_near(0, 3, (4,), next_copy)
    keep(1)
    send_near(0, 1, (4,), prev_copy)
    send_back((0,))
    send_near(1, 3, (4,), next_copy)
    send_near(1, 1, (7,), prev_copy)
    send_near(1, 1, (5,), prev_copy)
    send_near(0, 3, (5,), next_copy)
    send_near(1, 1, (4,), prev_copy)
    send_near(0, 1, (2,), prev_copy)
    send_near(1, 1, (2,), prev_copy)
    send_back((1,))
    send_near(0, 1, (6,), prev_copy)
    send_near(1, 3, (5,), next_copy)
    send_near(0, 3, (2,), next_copy)
    send_near(1, 3, (3,), next_copy)
    give(0)
    send_near(0, 3, (6,), next_copy)
    send_near(0, 3, (7,), next_copy)
    send_near(1, 3, (2,), next_copy)
    send_near(0, 1, (7,), prev_copy)
    send_near(0, 1, (0,), prev_copy)
    send_near(1, 1, (3,), prev_copy)
    send_back((6,))
    send_back((7,))
    send_near(0, 3, (1,), next_copy)
    send_near(0, 1, (1,), prev_copy)
    send_back((5,))
    send_near(0, 1, (5,), prev_copy)
    send_near(0, 3, (0,), next_copy)
    send_near(0, 1, (3,), prev_copy)
    send_back((4,))
    send_near(0, 3, (3,), next_copy)
    send_back((2,))
    keep(0)
    send_back((3,))
    finish(6)
    finish(0)
    finish(5)
    finish(2)
    finish(1)
    finish(4)
    finish(7)
    finish(3)

    for q in range(QS):
        arrived("rg", q, rg_mine.at[pl.ds(ROWS + CHUNK * q, CHUNK)])

    def part_of(n, d):
        at = pl.multiple_of(lax.rem((px if n else pz) + d, 4) * FEAT_Z, FEAT_Z)
        return dot((s_x if n else s_t)[pl.ds(at, FEAT_Z), :], rg_mine[:, pl.ds(256 * n, 256)], NN)

    def st_copy(n, h, d):
        return copy("st", 8 * n + 4 * h + d, st_out.at[n, h, d], st_in.at[n, h, d], ring_x(d) if n else ring_z(d))

    for d in (2, 1, 3):
        for n in range(2):
            value = part_of(n, d).astype(BF16)
            for h in range(2):
                st_out[n, h, d] = value[:, 128 * h : 128 * h + 128]
            st_copy(n, 0, d).start()
    for d in (2, 1, 3):
        for n in range(2):
            st_copy(n, 1, d).start()
    for n in range(2):
        value = part_of(n, 0)
        for h in range(2):
            st_sum[n, h] = value[:, 128 * h : 128 * h + 128]

    @pl.loop(0, FEAT // 256)
    def _(n):
        here = pl.ds(pl.multiple_of(n * 256, 256), 256)
        sg_ref[:, here] = dot(rg[...], w_ref[here, :], NT).astype(BF16)

    def group(n, h, dy, d):
        y = jnp.where(dy == 0, yh, 1 - yh)
        g = y * 4 + lax.rem(px + d, 4) if n == 0 else lax.rem(pz + d, 4) * 2 + y
        return st_sum[n, h, pl.ds(pl.multiple_of(g * OWN_ROWS, 8), OWN_ROWS), :]

    def end_copy(n, h, k):
        m = 16 * n + 8 * h + k
        return copy("end", m, end_out.at[n, h, k], end_in.at[n, h, k], plane(n, k // 4, k % 4))

    pad = jnp.zeros((PADDED - OWN_ROWS, 128), F32)
    for h in range(2):
        for n in range(2):
            for d in (1, 3, 2):
                arrived("st", 8 * n + 4 * h + d, st_in.at[n, h, d])
            st_sum[n, h] += (
                st_in[n, h, 1].astype(F32) + st_in[n, h, 2].astype(F32) + st_in[n, h, 3].astype(F32)
            )
            for k in (6, 5, 7, 4, 2, 1, 3):
                value = jnp.concatenate([group(n, h, k // 4, k % 4), pad], axis=0)
                end_out[n, h, k] = value.astype(BF16)
                end_copy(n, h, k).start()

    def finished(n, h):
        total = group(n, h, 0, 0)
        for k in (1, 3, 2, 4, 5, 7, 6):
            arrived("end", 16 * n + 8 * h + k, end_in.at[n, h, k])
            total += end_in[n, h, k].astype(F32)[:OWN_ROWS]
        return total

    quarters = {(n, h): finished(n, h) for h in range(2) for n in range(2)}
    p_fin = jnp.concatenate([quarters[0, 0], quarters[0, 1]], axis=1)
    q_fin = jnp.concatenate([quarters[1, 0], quarters[1, 1]], axis=1)
    both = jnp.concatenate([p_fin, q_fin], axis=1)
    first, second = both[:20], both[20:]
    theirs = jnp.where(core == 0, second, first)
    mine = jnp.where(core == 0, first, second)
    last_out[...] = jnp.concatenate([theirs, jnp.zeros((4, HALF), F32)], axis=0)
    copy("last", 0, last_out, last_in, partner).start()
    arrived("last", 0, last_in)
    got = last_in[:20, :]
    pg_ref[:, 0, :HALF] = jnp.where(core == 0, mine, got)
    pg_ref[:, 0, HALF:] = jnp.where(core == 0, got, mine)

    some = blocks.at[0]
    for q in range(QS):
        left("y", q, some.at[rows(q)])
        left("y_back", q, some.at[rows(q)])
        left("rg", q, rg_theirs.at[rows(q)])
    left("y_id", 0, ids.at[0])
    for k in range(2):
        for q in range(QS):
            left("ring", 3 * QS * k + q, some.at[rows(0)])
            left("ring", 3 * QS * k + QS + q, some.at[rows(0)])
            if k == 0 or q not in EXTRA:
                left("ring", 3 * QS * k + 2 * QS + q, some.at[rows(0)])
            left("far", QS * k + q, some.at[rows(0)])
            if k == 0 or extra_of(3, q) is None:
                left("to_next", QS * k + q, some.at[rows(0)])
            if k == 0 or extra_of(1, q) is None:
                left("to_prev", QS * k + q, some.at[rows(0)])
    for n in range(6):
        left("ring_id", n, ids.at[0])
    for n in range(4):
        for m in range(4):
            left("core", 4 * n + m, some.at[pl.ds(0, 2 * CHUNK)])
        left("core_id", n, ids.at[0])
        left("part", n, some)
        left("extra", n, some.at[rows(0)])
        left("y_extra", n, some.at[rows(0)])
    left("core_s", 0, s_other)
    for n in range(2):
        for h in range(2):
            for d in (1, 2, 3):
                left("st", 8 * n + 4 * h + d, st_out.at[n, h, d])
            for k in range(1, 8):
                left("end", 16 * n + 8 * h + k, end_out.at[n, h, k])
    left("last", 0, last_out)


def local(states, projection, prompt_ids, log_temper, logit_offset):
    vmem = pl.BlockSpec(memory_space=pltpu.VMEM)
    hbm = pl.BlockSpec(memory_space=pl.ANY)
    scratch = [
        ((ROWS, FEAT), BF16),
        ((FEAT, EMB), BF16),
        ((4, ROWS, 128), F32),
        ((1, ROWS), jnp.int32),
        None,
        None,
        ((12, ROWS, EMB), BF16),
        ((12, 8, ROWS), jnp.int32),
        ((ROWS, EMB), F32),
        ((ROWS, 128), F32),
        ((4 * ROWS, 8 * ROWS), BF16),
        ((2, 4, ROWS, EMB), F32),
        ((2, 4, ROWS, EMB), BF16),
        ((2, ROWS, EMB), BF16),
        ((2, 2, ROWS, EMB), BF16),
        ((4 * CHUNK, EMB), BF16),
        ((4 * CHUNK, EMB), BF16),
        ((4, ROWS, EMB), BF16),
        ((4, ROWS, EMB), BF16),
        ((ROWS, EMB), BF16),
        ((ROWS, EMB), BF16),
        ((ROWS, EMB), BF16),
        ((2 * ROWS, HALF), BF16),
        ((ROWS, HALF), BF16),
        ((ROWS, FEAT), BF16),
        ((FEAT, 2 * ROWS), BF16),
        ((FEAT, 2 * ROWS), BF16),
        ((FEAT, ROWS), F32),
        ((2, 2, 4, FEAT_Z, 128), BF16),
        ((2, 2, 4, FEAT_Z, 128), BF16),
        ((2, 2, FEAT_Z, 128), F32),
        ((2, 2, 8, PADDED, 128), BF16),
        ((2, 2, 8, PADDED, 128), BF16),
        ((24, HALF), F32),
        ((24, HALF), F32),
    ]
    state_grad, owned = pl.pallas_call(
        kernel,
        out_shape=(
            pltpu.VMEM((ROWS, FEAT), BF16),
            pltpu.VMEM((20, 1, EMB), F32),
        ),
        in_specs=[hbm] * 5,
        out_specs=(vmem, vmem),
        scratch_shapes=[pltpu.VMEM(*what) if what else pltpu.SMEM((1,), F32) for what in scratch]
        + [pltpu.SemaphoreType.DMA((4 + QUARTERS,))]
        + [pltpu.SemaphoreType.DMA((Sems.total(),)), pltpu.SemaphoreType.DMA((Sems.total(),))],
        compiler_params=pltpu.CompilerParams(
            collective_id=0, has_side_effects=True, vmem_limit_bytes=60 * 2**20
        ),
        name="contrast",
    )(states[0], projection[0], prompt_ids.reshape(1, ROWS), log_temper, logit_offset)
    return state_grad[None], owned.reshape(1, 20, EMB)


def solution(mesh):
    return jax.shard_map(
        local,
        mesh=mesh,
        in_specs=(P("tower", "batch", None), P("tower", None, None), P("batch"), P(), P()),
        out_specs=(P("tower", "batch", None), P("tower", "batch", None)),
        check_vma=False,
    )
```

```python
import jax
import jax.numpy as jnp
from jax import lax
from jax.experimental import pallas as pl
from jax.experimental.pallas import tpu as pltpu
from jax.sharding import PartitionSpec as P

EPSILON = 1e-06
MESH = pl.DeviceIdType.MESH
F32, BF16 = jnp.float32, jnp.bfloat16
NT = (((1,), (1,)), ((), ()))
TN = (((0,), (0,)), ((), ()))
NN = (((1,), (0,)), ((), ()))

ROWS = 256
EMB = 1024
FEAT = 1280
CHUNK = 32
QS = ROWS // CHUNK
HALF = EMB // 2
QUARTERS = 4
FEAT_Z = FEAT // 4
OWN_ROWS = 40
PADDED = 48
OTHER0 = 8

Y_ORDER = (0, 4, 1, 5, 2, 6, 3, 7)
NEXT_ORDER = (2, 3, 0, 1, 6, 7, 4, 5)
PREV_ORDER = (6, 7, 4, 5, 2, 3, 0, 1)
EXTRA = (2, 6, 3, 7)


class Sems:
    sizes = dict(
        y=QS, y_id=1, ring=2 * 3 * QS, ring_id=2 * 3, core=16, core_id=4, core_s=1, extra=4,
        part=4, far=2 * QS, to_next=2 * QS, to_prev=2 * QS, y_extra=4, y_back=QS,
        rg=QS, st=16, end=32, last=1,
    )

    @classmethod
    def at(cls, name, index=0):
        base = 0
        for key, size in cls.sizes.items():
            if key == name:
                return base + index
            base += size
        raise KeyError(name)

    @classmethod
    def total(cls):
        return sum(cls.sizes.values())


def dot(a, b, dims):
    return lax.dot_general(a, b, dims, preferred_element_type=F32)


def kernel(
    s_hbm, w_hbm, id_hbm, lt_hbm, of_hbm, sg_ref, pg_ref,
    s_ref, w_ref, cols, id_ref, lt_ref, of_ref, blocks, ids, raw, inv, pair, grad, out_buf, far_in, near_in, extra_out, extra_in, part_out, part_in, y_out, y_in,
    rg, rg_mine, rg_theirs, s_other, s_t, s_x, tall, st_out, st_in, st_sum, end_out, end_in, last_out, last_in,
    lsem, ssem, rsem,
):
    tower = lax.axis_index("tower")
    batch = lax.axis_index("batch")
    core = lax.rem(batch, 2)
    px = lax.rem(batch // 2, 4)
    yh = lax.rem(batch // 8, 2)
    pz = batch // 16
    other = 1 - tower

    def dev(t, z, y, x, c):
        return (t, ((z * 2 + y) * 4 + x) * 2 + c)

    def ring_x(d):
        return dev(tower, pz, yh, lax.rem(px + d, 4), core)

    def ring_z(d):
        return dev(tower, lax.rem(pz + d, 4), yh, px, core)

    def ring(k, d):
        r = tower if k == 0 else other
        return dev(tower, lax.rem(pz + r * d, 4), yh, lax.rem(px + (1 - r) * d, 4), core)

    partner = dev(tower, pz, yh, px, 1 - core)
    y_up = dev(other, pz, jnp.where(tower == 1, 1 - yh, yh), px, core)
    y_down = dev(other, pz, jnp.where(tower == 0, 1 - yh, yh), px, core)

    def plane(n, dy, d):
        x = lax.rem(px + d, 4) if n == 0 else px
        z = pz if n == 0 else lax.rem(pz + d, 4)
        return dev(tower, z, 1 - yh if dy else yh, x, core)

    def block(k, slot):
        return 2 * slot if k == 0 else OTHER0 + slot

    def copy(name, index, src, dst, where):
        n = Sems.at(name) + index
        return pltpu.make_async_remote_copy(
            src_ref=src, dst_ref=dst, send_sem=ssem.at[n], recv_sem=rsem.at[n],
            device_id=where, device_id_type=MESH,
        )

    def arrived(name, index, ref):
        copy(name, index, ref, ref, partner).wait_recv()

    def left(name, index, ref):
        copy(name, index, ref, ref, partner).wait_send()

    def rows(q):
        return pl.ds(CHUNK * q, CHUNK)

    def piece(k, slot, q):
        return blocks.at[block(k, slot), rows(q)]

    barrier = pltpu.get_barrier_semaphore()
    near = [partner, y_up, y_down] + [plane(n, 0, d) for n in range(2) for d in (1, 3)]
    for where in near:
        pl.semaphore_signal(barrier, inc=1, device_id=where, device_id_type=MESH)

    def halves(n):
        return pl.ds(n * HALF, HALF)

    def quarter(n):
        return pl.ds(n * (EMB // QUARTERS), EMB // QUARTERS)

    loads = [pltpu.make_async_copy(s_hbm, s_ref, lsem.at[0])]
    loads += [pltpu.make_async_copy(w_hbm.at[:, quarter(n)], w_ref.at[:, quarter(n)], lsem.at[1 + n]) for n in range(QUARTERS)]
    small = [(id_hbm, id_ref), (lt_hbm, lt_ref), (of_hbm, of_ref)]
    small = [pltpu.make_async_copy(src, dst, lsem.at[1 + QUARTERS + n]) for n, (src, dst) in enumerate(small)]
    for load in loads + small:
        load.start()
    small[0].wait()
    ids[0] = jnp.broadcast_to(id_ref[...], (8, ROWS))
    small[1].wait()
    small[2].wait()
    loads[0].wait()
    for n in range(QUARTERS):
        loads[1 + n].wait()
        raw[:, quarter(n)] = dot(s_ref[...], w_ref[:, quarter(n)], NN)

    pl.semaphore_wait(barrier, len(near))

    def to_next(k, q):
        return copy("ring", 3 * QS * k + q, piece(k, 0, q), piece(k, 1, q), ring(k, 1))

    def to_prev(k, q):
        return copy("ring", 3 * QS * k + QS + q, piece(k, 0, q), piece(k, 3, q), ring(k, 3))

    def onward(k, q):
        slot = 1 if q < QS // 2 else 3
        return copy("ring", 3 * QS * k + 2 * QS + q, piece(k, slot, q), piece(k, 2, q), ring(k, slot))

    def got_next(k, q):
        arrived("ring", 3 * QS * k + q, piece(k, 1, q))

    def got_prev(k, q):
        arrived("ring", 3 * QS * k + QS + q, piece(k, 3, q))

    def got_onward(k, q):
        arrived("ring", 3 * QS * k + 2 * QS + q, piece(k, 2, q))

    def extra(n):
        return copy("extra", n, piece(0, 2, EXTRA[n]), piece(1, 2, EXTRA[n]), y_up)

    def ids_out(k):
        copy("ring_id", 3 * k, ids.at[block(k, 0)], ids.at[block(k, 1)], ring(k, 1)).start()
        copy("ring_id", 3 * k + 1, ids.at[block(k, 0)], ids.at[block(k, 3)], ring(k, 3)).start()

    def ids_onward(k):
        arrived("ring_id", 3 * k, ids.at[block(k, 1)])
        copy("ring_id", 3 * k + 2, ids.at[block(k, 1)], ids.at[block(k, 2)], ring(k, 1)).start()
        arrived("ring_id", 3 * k + 1, ids.at[block(k, 3)])

    def core_copy(slot, n):
        there = pl.ds(2 * CHUNK * n, 2 * CHUNK)
        return copy("core", 4 * slot + n, blocks.at[2 * slot, there], blocks.at[2 * slot + 1, there], partner)

    def core_send(slot, *pieces):
        for n in pieces:
            core_copy(slot, n).start()

    def core_got(slot, *pieces):
        for n in pieces:
            arrived("core", 4 * slot + n, blocks.at[2 * slot + 1, pl.ds(2 * CHUNK * n, 2 * CHUNK)])

    def core_ids_got(slot):
        arrived("core_id", slot, ids.at[2 * slot + 1])

    def core_ids(slot):
        copy("core_id", slot, ids.at[2 * slot], ids.at[2 * slot + 1], partner).start()

    copy("y_id", 0, ids.at[0], ids.at[OTHER0], y_up).start()
    ids_out(0)
    def own_rows(q):
        part = raw[rows(q), :]
        length = jnp.sqrt(jnp.sum(part * part, axis=1, keepdims=True) + EPSILON)
        scale = 1.0 / length
        inv[rows(q), :] = jnp.broadcast_to(scale, (CHUNK, 128))
        blocks[0, rows(q)] = (part * scale).astype(BF16)

    def y_send(q):
        copy("y", q, piece(0, 0, q), piece(1, 0, q), y_up).start()

    for q in (0, 1):
        own_rows(q)
        y_send(q)
        own_rows(q + 2)
        to_next(0, q + 2).start()
        own_rows(q + 4)
        y_send(q + 4)
        own_rows(q + 6)
        to_prev(0, q + 6).start()
    for q in EXTRA:
        y_send(q)
    for q in (0, 1, 6):
        to_next(0, q).start()
    for q in (4, 5, 2):
        to_prev(0, q).start()
    core_send(0, 0, 1, 2, 3)
    core_ids(0)

    def turn(states, first):
        tall[...] = states[...].astype(F32).T
        here = pl.ds(first, ROWS)
        s_t[:, here] = tall[...].astype(BF16)
        for x in range(4):
            pieces = [tall[pl.ds((4 * k + x) * OWN_ROWS, OWN_ROWS), :] for k in range(8)]
            s_x[pl.ds(x * FEAT_Z, FEAT_Z), here] = jnp.concatenate(pieces, axis=0).astype(BF16)

    copy("core_s", 0, s_ref, s_other, partner).start()
    turn(s_ref, 0)

    temper = jnp.exp(jnp.full((1, 1), lt_ref[0], F32))
    slope = 0.5 * temper
    shift = jnp.full((1, 1), 0.5 * of_ref[0], F32)

    def id_columns(slot):
        cols[slot] = jnp.broadcast_to(ids[OTHER0 + slot, 0:1, :].astype(F32), (128, ROWS)).T

    other_rows = {
        "0": [(0, 0, 256)],
        "2": [(2, 0, 256)],
        "early": [(1, 0, 64), (1, 128, 64), (3, 0, 64), (3, 128, 64)],
        "late": [(1, 64, 64), (1, 192, 64), (3, 64, 64), (3, 192, 64)],
    }
    own_rows_of = {
        "0": [(0, 0, 0, 256), (0, 1, 0, 256)],
        "2": [(2, 0, 0, 256), (2, 1, 0, 256)],
        "early": [(1, 0, 0, 128), (1, 1, 0, 128), (3, 0, 128, 128), (3, 1, 128, 128)],
        "late": [(1, 0, 128, 128), (1, 1, 128, 128), (3, 0, 0, 128), (3, 1, 0, 128)],
    }

    def joined(parts, axis):
        return parts[0] if len(parts) == 1 else jnp.concatenate(parts, axis=axis)

    def unit(a, b):
        left_side, right_side = other_rows[a], own_rows_of[b]
        rest = joined([blocks[OTHER0 + n, pl.ds(at, size)] for n, at, size in left_side], 0)
        own = joined([blocks[2 * n + c, pl.ds(at, size)] for n, c, at, size in right_side], 0)
        logit = dot(rest, own, NT)
        value = jnp.tanh(logit * slope + shift) * 8.0
        row = joined([ids[2 * n + c, 0:1, pl.ds(at, size)] for n, c, at, size in right_side], 1).astype(F32)
        col = joined([cols[n, pl.ds(at, size)] for n, at, size in left_side], 0)
        same = jnp.concatenate([col] * 4, axis=1) == row
        value = (value + jnp.where(same, -8.0, 8.0)).astype(BF16)
        first = 0
        for n, at, size in left_side:
            begin = 0
            for m, c, start, width in right_side:
                pair[pl.ds(n * ROWS + at, size), pl.ds((2 * m + c) * ROWS + start, width)] = value[
                    first : first + size, begin : begin + width
                ]
                begin += width
            first += size

    def y_got(m):
        q = Y_ORDER[m]
        arrived("y", q, piece(1, 0, q))
        to_next(1, q).start()
        to_prev(1, q).start()

    def own_on(m):
        for q, got in ((NEXT_ORDER[m], got_next), (PREV_ORDER[m], got_prev)):
            got(0, q)
            onward(0, q).start()

    def other_on(q):
        (got_next if q < 4 else got_prev)(1, q)
        onward(1, q).start()

    def far_on(n):
        got_onward(0, EXTRA[n])
        extra(n).start()

    def own_terms(half, slot):
        rest = blocks[pl.ds(OTHER0, 4)].reshape(4 * ROWS, EMB)
        return dot(pair[:, pl.ds((2 * slot + half) * ROWS, ROWS)], rest, TN)

    def other_terms(slot):
        for n in range(2):
            cols = halves(n)
            own = blocks[pl.ds(0, 8), :, cols].reshape(8 * ROWS, HALF)
            grad[1, slot, :, cols] = dot(pair[pl.ds(slot * ROWS, ROWS), :], own, NN)

    def far_terms(names, last):
        what = [one for name in names for one in own_rows_of[name]]
        terms = joined([pair[pl.ds(2 * ROWS, ROWS), pl.ds((2 * m + c) * ROWS + at, size)] for m, c, at, size in what], 1)
        for n in range(2):
            own = joined([blocks[2 * m + c, pl.ds(at, size), halves(n)] for m, c, at, size in what], 0)
            value = dot(terms, own, NN)
            if last:
                out_buf[1, 2, :, halves(n)] = (grad[1, 2, :, halves(n)] + value).astype(BF16)
            else:
                grad[1, 2, :, halves(n)] = value

    def give(slot):
        part_out[slot] = own_terms(1, slot).astype(BF16)
        copy("part", slot, part_out.at[slot], part_in.at[slot], partner).start()

    def keep(slot):
        arrived("part", slot, part_in.at[slot])
        value = own_terms(0, slot) + part_in[slot].astype(F32)
        if slot == 2:
            out_buf[0, 2] = value.astype(BF16)
        else:
            grad[0, slot] = value

    def far_copy(k, q):
        return copy("far", QS * k + q, out_buf.at[k, 2, rows(q)], far_in.at[k, rows(q)], ring(k, 1 if q < 4 else 3))

    def next_copy(k, q):
        return copy("to_next", QS * k + q, out_buf.at[k, 3, rows(q)], near_in.at[k, 0, rows(q)], ring(k, 1))

    def prev_copy(k, q):
        return copy("to_prev", QS * k + q, out_buf.at[k, 1, rows(q)], near_in.at[k, 1, rows(q)], ring(k, 3))

    def extra_of(slot, q):
        if (slot, q) in ((3, 6), (3, 7), (1, 0), (1, 1)):
            return {(3, 6): 0, (3, 7): 1, (1, 0): 2, (1, 1): 3}[slot, q]
        return None

    def extra_back(n):
        return copy("y_extra", n, extra_out.at[rows(n)], extra_in.at[rows(n)], y_down)

    def send_far(k):
        for q in (0, 4, 1, 5, 2, 6, 3, 7):
            far_copy(k, q).start()

    def send_extra(slot):
        for q in range(QS):
            n = extra_of(slot, q)
            if n is not None:
                extra_out[rows(n), :] = grad[1, slot, rows(q), :].astype(BF16)
                extra_back(n).start()

    def send_near(k, slot, order, make):
        for q in order:
            n = extra_of(slot, q)
            if n is not None and k == 1:
                continue
            term = grad[k, slot, rows(q), :]
            if (q < 4) == (slot == 3):
                arrived("far", QS * k + q, far_in.at[k, rows(q)])
                term += far_in[k, rows(q), :].astype(F32)
            if n is not None:
                arrived("y_extra", n, extra_in.at[rows(n)])
                term += extra_in[rows(n), :].astype(F32)
            out_buf[k, slot, rows(q), :] = term.astype(BF16)
            make(k, q).start()

    def reduced(k, q):
        total = grad[k, 0, rows(q), :]
        if k == 0 or extra_of(3, q) is None:
            arrived("to_next", QS * k + q, near_in.at[k, 0, rows(q)])
            total += near_in[k, 0, rows(q), :].astype(F32)
        if k == 0 or extra_of(1, q) is None:
            arrived("to_prev", QS * k + q, near_in.at[k, 1, rows(q)])
            total += near_in[k, 1, rows(q), :].astype(F32)
        return total

    def back_copy(q):
        return copy("y_back", q, y_out.at[rows(q)], y_in.at[rows(q)], y_down)

    def send_back(order):
        for q in order:
            y_out[rows(q), :] = reduced(1, q).astype(BF16)
            back_copy(q).start()

    def rg_copy(q):
        return copy("rg", q, rg_theirs.at[rows(q)], rg_mine.at[pl.ds(ROWS + CHUNK * q, CHUNK)], partner)

    def finish(q):
        total = reduced(0, q)
        arrived("y_back", q, y_in.at[rows(q)])
        emb_grad = temper * (total + y_in[rows(q), :].astype(F32))
        scale = inv[rows(q), 0:1]
        unit_rows = raw[rows(q), :] * scale
        along = jnp.sum(unit_rows * emb_grad, axis=1, keepdims=True)
        value = ((emb_grad - unit_rows * along) * scale).astype(BF16)
        rg[rows(q), :] = value
        low, high = value[:, :HALF], value[:, HALF:]
        rg_mine[rows(q), :] = jnp.where(core == 0, low, high)
        rg_theirs[rows(q), :] = jnp.where(core == 0, high, low)
        rg_copy(q).start()

    arrived("y_id", 0, ids.at[OTHER0])
    ids_out(1)
    y_got(0)
    y_got(1)
    ids_onward(1)
    core_got(0, 0, 1, 2, 3)
    got_next(0, 3)
    onward(0, 3).start()
    got_prev(0, 7)
    onward(0, 7).start()
    ids_onward(0)
    got_next(0, 2)
    onward(0, 2).start()
    got_prev(0, 6)
    onward(0, 6).start()
    got_next(0, 0)
    onward(0, 0).start()
    got_prev(0, 4)
    onward(0, 4).start()
    y_got(2)
    got_next(0, 1)
    onward(0, 1).start()
    got_prev(0, 5)
    onward(0, 5).start()
    core_ids(1)
    core_ids(3)
    to_next(0, 7).start()
    y_got(3)
    core_send(3, 2, 3)
    y_got(4)
    y_got(5)
    far_on(1)
    to_prev(0, 3).start()
    got_next(1, 4)
    got_next(1, 5)
    got_prev(1, 0)
    got_prev(1, 1)
    arrived("ring_id", 2, ids.at[block(0, 2)])
    core_ids(2)
    id_columns(0)
    core_ids_got(0)
    y_got(6)
    y_got(7)
    other_on(5)
    other_on(0)
    far_on(3)
    to_next(0, 4).start()
    far_on(2)
    id_columns(1)
    id_columns(3)
    core_ids_got(1)
    core_ids_got(3)
    far_on(0)
    core_got(3, 2, 3)
    to_next(0, 5).start()
    other_on(1)
    arrived("core_s", 0, s_other)
    turn(s_other, ROWS)
    got_onward(0, 0)
    other_on(4)
    core_send(1, 0, 1)
    to_prev(0, 1).start()
    unit("0", "0")
    core_send(2, 1, 3)
    got_onward(0, 1)
    got_onward(0, 4)
    got_onward(0, 5)
    to_prev(0, 0).start()
    core_send(2, 0, 2)
    core_got(1, 0, 1)
    unit("early", "early")
    got_next(0, 6)
    got_next(0, 7)
    core_send(1, 3)
    unit("0", "early")
    unit("early", "0")
    got_prev(0, 2)
    got_prev(0, 3)
    core_send(3, 1)
    arrived("ring_id", 5, ids.at[block(1, 2)])
    id_columns(2)
    core_ids_got(2)
    core_got(2, 0, 1, 2, 3)
    got_next(1, 2)
    got_prev(1, 2)
    got_next(1, 6)
    got_prev(1, 6)
    got_next(1, 3)
    got_prev(1, 3)
    got_next(1, 7)
    got_prev(1, 7)
    unit("early", "2")
    unit("late", "early")
    unit("late", "2")
    unit("0", "2")
    unit("late", "0")
    arrived("extra", 0, piece(1, 2, EXTRA[0]))
    arrived("extra", 1, piece(1, 2, EXTRA[1]))
    arrived("extra", 2, piece(1, 2, EXTRA[2]))
    arrived("extra", 3, piece(1, 2, EXTRA[3]))
    got_prev(0, 0)
    got_prev(0, 1)
    core_send(3, 0)
    got_next(0, 4)
    got_next(0, 5)
    core_send(1, 2)
    got_onward(1, 0)
    got_onward(1, 4)
    got_onward(1, 1)
    got_onward(1, 5)
    unit("2", "early")
    unit("2", "0")
    unit("2", "2")
    far_terms(("0", "2", "early"), False)
    give(2)
    core_got(1, 2, 3)
    core_got(3, 0, 1)
    unit("2", "late")
    far_terms(("late",), True)
    send_far(1)
    unit("0", "late")
    unit("early", "late")
    unit("late", "late")
    other_terms(3)
    send_extra(3)
    keep(2)
    send_far(0)
    give(3)
    send_near(1, 3, (0,), next_copy)
    give(1)
    other_terms(1)
    send_extra(1)
    send_near(1, 3, (1,), next_copy)
    send_near(1, 1, (6,), prev_copy)
    keep(3)
    other_terms(0)
    send_near(0, 3, (4,), next_copy)
    keep(1)
    send_near(0, 1, (4,), prev_copy)
    send_back((0,))
    send_near(1, 3, (4,), next_copy)
    send_near(1, 1, (7,), prev_copy)
    send_near(1, 1, (5,), prev_copy)
    send_near(0, 3, (5,), next_copy)
    send_near(1, 1, (4,), prev_copy)
    send_near(0, 1, (2,), prev_copy)
    send_near(1, 1, (2,), prev_copy)
    send_back((1,))
    send_near(0, 1, (6,), prev_copy)
    send_near(1, 3, (5,), next_copy)
    send_near(0, 3, (2,), next_copy)
    send_near(1, 3, (3,), next_copy)
    give(0)
    send_near(0, 3, (6,), next_copy)
    send_near(0, 3, (7,), next_copy)
    send_near(1, 3, (2,), next_copy)
    send_near(0, 1, (7,), prev_copy)
    send_near(0, 1, (0,), prev_copy)
    send_near(1, 1, (3,), prev_copy)
    send_back((6,))
    send_back((7,))
    send_near(0, 3, (1,), next_copy)
    send_near(0, 1, (1,), prev_copy)
    send_near(0, 3, (0,), next_copy)
    send_back((5,))
    send_near(0, 1, (5,), prev_copy)
    keep(0)
    send_near(0, 1, (3,), prev_copy)
    send_back((4,))
    send_near(0, 3, (3,), next_copy)
    send_back((2,))
    send_back((3,))
    finish(6)
    finish(0)
    finish(5)
    finish(2)
    finish(1)
    finish(4)
    finish(7)
    finish(3)

    for q in range(QS):
        arrived("rg", q, rg_mine.at[pl.ds(ROWS + CHUNK * q, CHUNK)])

    def part_of(n, d):
        at = pl.multiple_of(lax.rem((px if n else pz) + d, 4) * FEAT_Z, FEAT_Z)
        return dot((s_x if n else s_t)[pl.ds(at, FEAT_Z), :], rg_mine[:, pl.ds(256 * n, 256)], NN)

    def st_copy(n, h, d):
        return copy("st", 8 * n + 4 * h + d, st_out.at[n, h, d], st_in.at[n, h, d], ring_x(d) if n else ring_z(d))

    for some in ((2,), (1, 3)):
        values = {(n, d): part_of(n, d).astype(BF16) for d in some for n in range(2)}
        for (n, d), value in values.items():
            for h in range(2):
                st_out[n, h, d] = value[:, 128 * h : 128 * h + 128]
        for n, d in values:
            st_copy(n, 0, d).start()
    for d in (2, 1, 3):
        for n in range(2):
            st_copy(n, 1, d).start()
    for n in range(2):
        value = part_of(n, 0)
        for h in range(2):
            st_sum[n, h] = value[:, 128 * h : 128 * h + 128]
    for n in range(FEAT // 256):
        here = pl.ds(n * 256, 256)
        sg_ref[:, here] = dot(rg[...], w_ref[here, :], NT).astype(BF16)

    def group(n, h, dy, d):
        y = jnp.where(dy == 0, yh, 1 - yh)
        g = y * 4 + lax.rem(px + d, 4) if n == 0 else lax.rem(pz + d, 4) * 2 + y
        return st_sum[n, h, pl.ds(pl.multiple_of(g * OWN_ROWS, 8), OWN_ROWS), :]

    def end_copy(n, h, k):
        m = 16 * n + 8 * h + k
        return copy("end", m, end_out.at[n, h, k], end_in.at[n, h, k], plane(n, k // 4, k % 4))

    pad = jnp.zeros((PADDED - OWN_ROWS, 128), F32)
    for h in range(2):
        for n in range(2):
            for d in (1, 3, 2):
                arrived("st", 8 * n + 4 * h + d, st_in.at[n, h, d])
            st_sum[n, h] += (
                st_in[n, h, 1].astype(F32) + st_in[n, h, 2].astype(F32) + st_in[n, h, 3].astype(F32)
            )
            for k in (6, 5, 7, 4, 2, 1, 3):
                value = jnp.concatenate([group(n, h, k // 4, k % 4), pad], axis=0)
                end_out[n, h, k] = value.astype(BF16)
                end_copy(n, h, k).start()

    def finished(n, h):
        total = group(n, h, 0, 0)
        for k in (1, 3, 2, 4, 5, 7, 6):
            arrived("end", 16 * n + 8 * h + k, end_in.at[n, h, k])
            total += end_in[n, h, k].astype(F32)[:OWN_ROWS]
        return total

    quarters = {(n, h): finished(n, h) for h in range(2) for n in range(2)}
    p_fin = jnp.concatenate([quarters[0, 0], quarters[0, 1]], axis=1)
    q_fin = jnp.concatenate([quarters[1, 0], quarters[1, 1]], axis=1)
    both = jnp.concatenate([p_fin, q_fin], axis=1)
    first, second = both[:20], both[20:]
    theirs = jnp.where(core == 0, second, first)
    mine = jnp.where(core == 0, first, second)
    last_out[...] = jnp.concatenate([theirs, jnp.zeros((4, HALF), F32)], axis=0)
    copy("last", 0, last_out, last_in, partner).start()
    arrived("last", 0, last_in)
    got = last_in[:20, :]
    pg_ref[:, 0, :HALF] = jnp.where(core == 0, mine, got)
    pg_ref[:, 0, HALF:] = jnp.where(core == 0, got, mine)

    some = blocks.at[0]
    for q in range(QS):
        left("y", q, some.at[rows(q)])
        left("y_back", q, some.at[rows(q)])
        left("rg", q, rg_theirs.at[rows(q)])
    left("y_id", 0, ids.at[0])
    for k in range(2):
        for q in range(QS):
            left("ring", 3 * QS * k + q, some.at[rows(0)])
            left("ring", 3 * QS * k + QS + q, some.at[rows(0)])
            if k == 0 or q not in EXTRA:
                left("ring", 3 * QS * k + 2 * QS + q, some.at[rows(0)])
            left("far", QS * k + q, some.at[rows(0)])
            if k == 0 or extra_of(3, q) is None:
                left("to_next", QS * k + q, some.at[rows(0)])
            if k == 0 or extra_of(1, q) is None:
                left("to_prev", QS * k + q, some.at[rows(0)])
    for n in range(6):
        left("ring_id", n, ids.at[0])
    for n in range(4):
        for m in range(4):
            left("core", 4 * n + m, some.at[pl.ds(0, 2 * CHUNK)])
        left("core_id", n, ids.at[0])
        left("part", n, some)
        left("extra", n, some.at[rows(0)])
        left("y_extra", n, some.at[rows(0)])
    left("core_s", 0, s_other)
    for n in range(2):
        for h in range(2):
            for d in (1, 2, 3):
                left("st", 8 * n + 4 * h + d, st_out.at[n, h, d])
            for k in range(1, 8):
                left("end", 16 * n + 8 * h + k, end_out.at[n, h, k])
    left("last", 0, last_out)


def local(states, projection, prompt_ids, log_temper, logit_offset):
    vmem = pl.BlockSpec(memory_space=pltpu.VMEM)
    hbm = pl.BlockSpec(memory_space=pl.ANY)
    scratch = [
        ((ROWS, FEAT), BF16),
        ((FEAT, EMB), BF16),
        ((4, ROWS, 128), F32),
        ((1, ROWS), jnp.int32),
        None,
        None,
        ((12, ROWS, EMB), BF16),
        ((12, 8, ROWS), jnp.int32),
        ((ROWS, EMB), F32),
        ((ROWS, 128), F32),
        ((4 * ROWS, 8 * ROWS), BF16),
        ((2, 4, ROWS, EMB), F32),
        ((2, 4, ROWS, EMB), BF16),
        ((2, ROWS, EMB), BF16),
        ((2, 2, ROWS, EMB), BF16),
        ((4 * CHUNK, EMB), BF16),
        ((4 * CHUNK, EMB), BF16),
        ((4, ROWS, EMB), BF16),
        ((4, ROWS, EMB), BF16),
        ((ROWS, EMB), BF16),
        ((ROWS, EMB), BF16),
        ((ROWS, EMB), BF16),
        ((2 * ROWS, HALF), BF16),
        ((ROWS, HALF), BF16),
        ((ROWS, FEAT), BF16),
        ((FEAT, 2 * ROWS), BF16),
        ((FEAT, 2 * ROWS), BF16),
        ((FEAT, ROWS), F32),
        ((2, 2, 4, FEAT_Z, 128), BF16),
        ((2, 2, 4, FEAT_Z, 128), BF16),
        ((2, 2, FEAT_Z, 128), F32),
        ((2, 2, 8, PADDED, 128), BF16),
        ((2, 2, 8, PADDED, 128), BF16),
        ((24, HALF), F32),
        ((24, HALF), F32),
    ]
    state_grad, owned = pl.pallas_call(
        kernel,
        out_shape=(
            pltpu.VMEM((ROWS, FEAT), BF16),
            pltpu.VMEM((20, 1, EMB), F32),
        ),
        in_specs=[hbm] * 5,
        out_specs=(vmem, vmem),
        scratch_shapes=[pltpu.VMEM(*what) if what else pltpu.SMEM((1,), F32) for what in scratch]
        + [pltpu.SemaphoreType.DMA((4 + QUARTERS,))]
        + [pltpu.SemaphoreType.DMA((Sems.total(),)), pltpu.SemaphoreType.DMA((Sems.total(),))],
        compiler_params=pltpu.CompilerParams(
            collective_id=0, has_side_effects=True, vmem_limit_bytes=60 * 2**20
        ),
        name="contrast",
    )(states[0], projection[0], prompt_ids.reshape(1, ROWS), log_temper, logit_offset)
    return state_grad[None], owned.reshape(1, 20, EMB)


def solution(mesh):
    return jax.shard_map(
        local,
        mesh=mesh,
        in_specs=(P("tower", "batch", None), P("tower", None, None), P("batch"), P(), P()),
        out_specs=(P("tower", "batch", None), P("tower", "batch", None)),
        check_vma=False,
    )
```
